32 devices in a mesh: row: 16 (over z, x, core), col: 2 (over y).
Axes of the slice: x: 2, y: 2, z: 4, core: 2. Of those that a mesh axis runs over, the one named last changes fastest.
Arguments:
- p_tiles: bfloat16 [128, 2, 128, 128], P(('row', 'col')), may hold values from -0.5 to 0.5
- p_cols: int32 [128, 2], P(('row', 'col')), may hold values from 0 to 15, as said below
- q_tiles: bfloat16 [128, 6, 128, 128], P(('row', 'col')), may hold values from -1.796875 to 1.796875
- q_cols: int32 [128, 6], P(('row', 'col')), may hold values from 0 to 15, all different within a row
Outputs:
- coarse: float32 [2048, 2048], P('row', 'col')
The draws below stay inside these ranges and needn't reach their ends.
Inputs may be any that keep to these rules, and one draw needn't show every extreme that they name: `p_cols`: the 2 coarse tiles in one row differ; among the fine blocks held by the devices of one index of col, every coarse tile is named at least once and at most 16 times, and some tile exactly 16 times. `q_cols`: the 6 coarse tiles in one row differ; every coarse tile appears somewhere.
All inputs are finite; a program needn't handle non-finite values.
Results may differ from the reference program's by a relative error of at most 0.0003.
Values may be sent and summed in bfloat16 or wider, within the bound.
No kernel may reach another device: no remote copies, remote signals or barrier semaphores. Data moves between devices by JAX's collectives and lax.ppermute only.
A program may use at most 128 MiB of HBM per device.

```python
import math
import jax
import jax.numpy as jnp
from jax import lax

BT = 128
FT_DEV = 4
KP = 2
KQ = 6
CT = 16
NFT = 128


def draw_p_cols(key, part):
    groups = NFT // (FT_DEV * CT)
    quarter = CT // 4
    mean_load = FT_DEV * KP
    profile = jnp.concatenate([jnp.full((quarter,), 2 * mean_load, jnp.int32), jnp.full((quarter,), mean_load, jnp.int32), jnp.full((CT - 2 * quarter,), mean_load // 2, jnp.int32)])
    bounds = jnp.cumsum(profile)
    total = CT * mean_load
    half_len = total // 2

    def one_group(group_key):
        labels = jax.random.permutation(jax.random.fold_in(group_key, 1), CT).astype(jnp.int32)
        position = jnp.arange(total, dtype=jnp.int32)
        which = jnp.sum((position[:, None] >= bounds[None, :]).astype(jnp.int32), axis=1)
        listing = jnp.take(labels, which)
        paired = jnp.stack([listing[:half_len], listing[half_len:]], axis=1)
        order = jax.random.permutation(jax.random.fold_in(group_key, 2), half_len)
        return jnp.take(paired, order, axis=0)
    keys = jax.vmap(lambda index: jax.random.fold_in(key, index))(jnp.arange(groups, dtype=jnp.int32))
    stacked = jax.vmap(one_group)(keys)
    shaped = stacked.reshape(groups, CT, FT_DEV, KP)
    return jnp.transpose(shaped, (1, 0, 2, 3)).reshape(NFT, KP).astype(jnp.int32)


def level_of(key, shape, shards, least, high):
    loudness, own = 1.0, jax.random.fold_in(key, 6)
    for dim, parts in shards:
        steps = jnp.exp(jax.random.uniform(jax.random.fold_in(own, dim), (parts,), jnp.float32, least / len(shards), high / len(shards)))
        loudness = loudness * jnp.repeat(steps, shape[dim] // parts).reshape([-1 if axis == dim else 1 for axis in range(len(shape))])
    return loudness


def choose_distinct(stream_key, rows, amount, top, lift):
    order = jax.random.permutation(jax.random.fold_in(stream_key, 1), amount)
    boost = order
    for power in range(3):
        boost = boost * boost // amount
    boost = boost * lift // amount
    chance = jax.random.randint(jax.random.fold_in(stream_key, 2), (rows, amount), 0, 4096) + boost
    sure = jax.random.permutation(jax.random.fold_in(stream_key, 3), rows)[jnp.arange(amount) % rows]
    chance = jnp.where(jnp.arange(rows)[:, None] == sure[None, :], 1 << 14, chance)
    priority = chance * amount + jnp.arange(amount)
    return lax.top_k(priority.astype(jnp.int32), top)[1].astype(jnp.int32)


def normal_values(key, shape, scale, most, cuts=(), kind=jnp.bfloat16):
    loudness = level_of(key, shape, cuts, -0.22, 0.18) if cuts else 1.0
    entries = jax.random.normal(key, shape, jnp.float32) * scale * loudness
    return jnp.minimum(jnp.maximum(entries, -most), most).astype(kind)


def setup_inputs(seed: int = 0) -> dict:
    seeds = jax.random.split(jax.random.key(seed), 5)
    return {
        "p_tiles": normal_values(seeds[0], (NFT, KP, BT, BT), BT ** -0.5, 0.5, ((0, 32),)),
        "p_cols": draw_p_cols(jax.random.fold_in(seeds[4], 71), 0),
        "q_tiles": normal_values(seeds[2], (NFT, KQ, BT, BT), 0.3, 1.796875, ((0, 32),)),
        "q_cols": choose_distinct(seeds[3], NFT, CT, KQ, 3072),
    }


def reference(p_tiles, p_cols, q_tiles, q_cols):
    blocks, per_block, extent, _ = p_tiles.shape
    others = q_tiles.shape[1]
    bundle = math.gcd(blocks, 32)
    count = blocks // bundle
    p_groups = p_tiles.reshape(count, bundle, per_block, extent, extent)
    q_groups = q_tiles.reshape(count, bundle, others, extent, extent)
    p_idgroups = p_cols.reshape(count, bundle, per_block)
    q_idgroups = q_cols.reshape(count, bundle, others)

    def one_bundle(running, inputs):
        p_set, q_set, p_ids, q_ids = inputs
        terms = jnp.einsum("fkab,flad->fklbd", p_set.astype(jnp.float32), q_set.astype(jnp.float32),
                           precision=lax.Precision.HIGHEST)
        row_ids = jnp.broadcast_to(p_ids[:, :, None], (bundle, per_block, others)).astype(jnp.int32)
        col_ids = jnp.broadcast_to(q_ids[:, None, :], (bundle, per_block, others)).astype(jnp.int32)
        running = running.at[row_ids, :, col_ids, :].add(terms)
        return running, None

    start_sum = jnp.zeros((CT, extent, CT, extent), jnp.float32)
    summed, _ = lax.scan(one_bundle, start_sum, (p_groups, q_groups, p_idgroups, q_idgroups))
    return summed.reshape(CT * extent, CT * extent)
```

```python
import functools

import jax
import jax.numpy as jnp
from jax import lax
from jax.experimental import pallas as pl
from jax.experimental.pallas import tpu as pltpu
from jax.sharding import Mesh
from jax.sharding import PartitionSpec as P

SEATS = 8


def slice_kernel(q_ref, out_ref):
    blocks, per_block, extent, _ = q_ref.shape
    strip = extent // SEATS
    for f in range(blocks):
        for k in range(per_block):
            flipped = q_ref[f, k].T
            for j in range(SEATS):
                out_ref[j, f, k] = flipped[j * strip:(j + 1) * strip]


def product_kernel(tile_count, p_ids, q_ids, q_ref, p_ref, acc_ref):
    blocks, rows, _ = q_ref.shape
    per_p = p_ref.shape[1]
    strip = acc_ref.shape[1]
    per_q = rows // strip
    acc_ref[...] = jnp.zeros_like(acc_ref)

    def one_block(f, carry):
        left = q_ref[f]
        for k in range(per_p):
            product = jnp.dot(left, p_ref[f, k], preferred_element_type=jnp.float32)
            base = p_ids[f * per_p + k] * tile_count
            for l in range(per_q):
                spot = base + q_ids[f * per_q + l]
                acc_ref[spot] += product[l * strip:(l + 1) * strip]
        return carry

    lax.fori_loop(0, blocks, one_block, 0)


def finish_kernel(x_ref, out_ref):
    seats, tiles, strip, extent = x_ref.shape
    for t in range(tiles):
        stacked = x_ref[:, t].reshape(seats * strip, extent)
        out_ref[:, t * extent:(t + 1) * extent] = stacked.T


def body(p_tiles, p_cols, q_tiles, q_cols):
    blocks, per_p, extent, _ = p_tiles.shape
    per_q = q_tiles.shape[1]
    planes = lax.axis_size("plane")
    side, cols = lax.axis_size("side"), lax.axis_size("col")
    tile_count = planes * side
    strip = extent // SEATS
    seat = ("side", "col")

    sliced = pl.pallas_call(
        slice_kernel,
        out_shape=jax.ShapeDtypeStruct((SEATS, blocks, per_q, strip, extent), q_tiles.dtype),
        name="cut_columns",
    )(q_tiles)
    q_here = lax.all_to_all(sliced, seat, split_axis=0, concat_axis=0, tiled=True)
    p_here = lax.all_gather(p_tiles, seat, axis=0, tiled=True)
    ids = jnp.concatenate([p_cols, q_cols], axis=1)
    ids = lax.all_gather(ids, seat, axis=0, tiled=True)

    total = SEATS * blocks
    acc = pl.pallas_call(
        functools.partial(product_kernel, tile_count),
        out_shape=jax.ShapeDtypeStruct((tile_count * tile_count, strip, extent), jnp.float32),
        grid_spec=pltpu.PrefetchScalarGridSpec(
            num_scalar_prefetch=2,
            grid=(),
            in_specs=[pl.BlockSpec(memory_space=pltpu.VMEM)] * 2,
            out_specs=pl.BlockSpec(memory_space=pltpu.VMEM),
        ),
        compiler_params=pltpu.CompilerParams(vmem_limit_bytes=40 << 20),
        name="products",
    )(
        ids[:, :per_p].reshape(-1),
        ids[:, per_p:].reshape(-1),
        q_here.reshape(total, per_q * strip, extent),
        p_here.reshape(total, per_p, extent, extent),
    )

    parts = acc.reshape(planes, side * tile_count, strip, extent)
    here = lax.axis_index("plane")

    def pick(place):
        place = jnp.clip(place, 0, planes - 1)
        return lax.dynamic_index_in_dim(parts, place, 0, keepdims=False)

    up = down = None
    for step in range(planes - 1):
        send_up = pick(planes - 1 - step + here)
        send_down = pick(here - (planes - 1 - step))
        if step:
            send_up, send_down = send_up + up, send_down + down
        up = lax.ppermute(send_up, "plane", [(z, z + 1) for z in range(step + 1)])
        down = lax.ppermute(
            send_down, "plane", [(planes - 1 - z, planes - 2 - z) for z in range(step + 1)]
        )
    summed = pick(here)
    if planes > 1:
        summed = summed + up + down

    mine = summed.reshape(SEATS, tile_count // cols, strip, extent)
    landed = lax.all_to_all(mine, seat, split_axis=0, concat_axis=0, tiled=True)
    return pl.pallas_call(
        finish_kernel,
        out_shape=jax.ShapeDtypeStruct((extent, tile_count // cols * extent), jnp.float32),
        name="turn",
    )(landed)


def solution(mesh):
    rows, cols = mesh.devices.shape
    side = SEATS // cols
    inner = Mesh(mesh.devices.reshape(rows // side, side, cols), ("plane", "side", "col"))
    every = ("plane", "side", "col")
    placed = (
        P(every, None, None, None),
        P(every, None),
        P(every, None, None, None),
        P(every, None),
    )
    return jax.shard_map(
        body, mesh=inner, in_specs=placed, out_specs=P(("plane", "side"), "col"), check_vma=False
    )
```

```python
import functools

import jax
import jax.numpy as jnp
from jax import lax
from jax.experimental import pallas as pl
from jax.experimental.pallas import tpu as pltpu
from jax.sharding import Mesh
from jax.sharding import PartitionSpec as P

SEATS = 16


def slice_kernel(q_ref, out_ref):
    blocks, per_block, extent, _ = q_ref.shape
    strip = extent // SEATS
    for f in range(blocks):
        flipped = [q_ref[f, k].astype(jnp.float32).T for k in range(per_block)]
        for j in range(SEATS):
            pieces = [tile[j * strip:(j + 1) * strip] for tile in flipped]
            out_ref[j, f] = jnp.concatenate(pieces, axis=0).astype(out_ref.dtype)


def product_kernel(tile_count, p_ids, q_ids, q_ref, p_ref, acc_ref):
    blocks, rows, _ = q_ref.shape
    per_p = p_ref.shape[1]
    strip = acc_ref.shape[1]
    per_q = rows // strip
    acc_ref[...] = jnp.zeros_like(acc_ref)

    def one_block(f, carry):
        left = q_ref[f]
        for k in range(per_p):
            product = jnp.dot(left, p_ref[f, k], preferred_element_type=jnp.float32)
            base = p_ids[f * per_p + k] * tile_count
            for l in range(per_q):
                spot = base + q_ids[f * per_q + l]
                acc_ref[spot] += product[l * strip:(l + 1) * strip]
        return carry

    lax.fori_loop(0, blocks, one_block, 0, unroll=2)


def finish_kernel(x_ref, out_ref):
    seats, tiles, strip, extent = x_ref.shape
    for t in range(tiles):
        stacked = x_ref[:, t].reshape(seats * strip, extent)
        out_ref[:, t * extent:(t + 1) * extent] = stacked.T


def body(p_tiles, p_cols, q_tiles, q_cols):
    blocks, per_p, extent, _ = p_tiles.shape
    per_q = q_tiles.shape[1]
    planes = lax.axis_size("plane")
    side, cols = lax.axis_size("side"), lax.axis_size("col")
    tile_count = planes * side
    strip = extent // SEATS
    seat = ("side", "col")

    sliced = pl.pallas_call(
        slice_kernel,
        out_shape=jax.ShapeDtypeStruct((SEATS, blocks, per_q * strip, extent), q_tiles.dtype),
        name="cut_columns",
    )(q_tiles)
    q_here = lax.all_to_all(sliced, seat, split_axis=0, concat_axis=0, tiled=True)
    p_here = lax.all_gather(p_tiles, seat, axis=0, tiled=True)
    ids = jnp.concatenate([p_cols, q_cols], axis=1)
    ids = lax.all_gather(ids, seat, axis=0, tiled=True)

    total = SEATS * blocks
    acc = pl.pallas_call(
        functools.partial(product_kernel, tile_count),
        out_shape=jax.ShapeDtypeStruct((tile_count * tile_count, strip, extent), jnp.float32),
        grid_spec=pltpu.PrefetchScalarGridSpec(
            num_scalar_prefetch=2,
            grid=(),
            in_specs=[pl.BlockSpec(memory_space=pltpu.VMEM)] * 2,
            out_specs=pl.BlockSpec(memory_space=pltpu.VMEM),
        ),
        compiler_params=pltpu.CompilerParams(vmem_limit_bytes=40 << 20),
        name="products",
    )(
        ids[:, :per_p].reshape(-1),
        ids[:, per_p:].reshape(-1),
        q_here.reshape(total, per_q * strip, extent),
        p_here.reshape(total, per_p, extent, extent),
    )

    parts = acc.reshape(planes, side * tile_count, strip, extent)
    here = lax.axis_index("plane")

    if planes == 2:
        away = lax.dynamic_index_in_dim(parts, 1 - here, 0, keepdims=False)
        kept = lax.dynamic_index_in_dim(parts, here, 0, keepdims=False)
        summed = kept + lax.ppermute(away, "plane", [(0, 1), (1, 0)])
    else:
        summed = lax.psum_scatter(parts, "plane", scatter_dimension=0, tiled=False)

    mine = summed.reshape(SEATS, tile_count // cols, strip, extent)
    landed = lax.all_to_all(mine, seat, split_axis=0, concat_axis=0, tiled=True)
    return pl.pallas_call(
        finish_kernel,
        out_shape=jax.ShapeDtypeStruct((extent, tile_count // cols * extent), jnp.float32),
        name="turn",
    )(landed)


def solution(mesh):
    rows, cols = mesh.devices.shape
    side = SEATS // cols
    inner = Mesh(mesh.devices.reshape(rows // side, side, cols), ("plane", "side", "col"))
    every = ("plane", "side", "col")
    placed = (
        P(every, None, None, None),
        P(every, None),
        P(every, None, None, None),
        P(every, None),
    )
    return jax.shard_map(
        body, mesh=inner, in_specs=placed, out_specs=P(("plane", "side"), "col"), check_vma=False
    )
```

```python
import functools

import jax
import jax.numpy as jnp
from jax import lax
from jax.experimental import pallas as pl
from jax.experimental.pallas import tpu as pltpu
from jax.sharding import Mesh
from jax.sharding import PartitionSpec as P

SEATS = 16
SUB = 8


def offsets():
    pairs, cores, cols = (lax.axis_size(name) for name in ("pair", "core", "col"))
    far_first = [(a, b) for a in reversed(range(pairs)) for b in reversed(range(cols))]
    return [(a, b, c) for a, b in far_first for c in range(cores)]


def origin(a, b, c):
    pairs, cores, cols = (lax.axis_size(name) for name in ("pair", "core", "col"))
    pair = lax.rem(lax.axis_index("pair") + (pairs - a), pairs)
    core = lax.rem(lax.axis_index("core") + (cores - c), cores)
    return (pair * cores + core) * cols + lax.rem(lax.axis_index("col") + (cols - b), cols)


def slice_kernel(p_ids, q_ids, q_ref, out_ref):
    blocks, per_q, extent, _ = q_ref.shape
    per_p = p_ids.shape[1]
    strip = extent // SEATS
    rows = per_q * strip
    lane = lax.broadcasted_iota(jnp.int32, (2 * SUB, extent), 1)
    ids = jnp.zeros((2 * SUB, extent), jnp.int32)
    for f in range(blocks):
        for k in range(per_p + per_q):
            value = p_ids[f, k] if k < per_p else q_ids[f, k - per_p]
            ids = jnp.where(lane == f * (per_p + per_q) + k, value, ids)
    ids = ids.astype(out_ref.dtype)
    for f in range(blocks):
        flipped = [q_ref[f, k].astype(jnp.float32).T for k in range(per_q)]
        for j in range(SEATS):
            pieces = [tile[j * strip:(j + 1) * strip] for tile in flipped]
            out_ref[j, f * rows:(f + 1) * rows] = jnp.concatenate(pieces, axis=0).astype(out_ref.dtype)
    for j in range(SEATS):
        out_ref[j, blocks * rows:] = ids


def product_kernel(tile_count, q_ref, *rest):
    p_refs, (acc_ref, wide_ids, ids, id_sem) = rest[:SEATS], rest[SEATS:]
    blocks, per_p, extent, _ = p_refs[0].shape
    strip = acc_ref.shape[1]
    rows = (q_ref.shape[1] - 2 * SUB) // blocks
    per_q = rows // strip
    for s in range(SEATS):
        wide_ids[s:s + 1] = q_ref[s, blocks * rows:, :].astype(jnp.int32)[:1]
    id_copy = pltpu.make_async_copy(wide_ids, ids, id_sem)
    id_copy.start()
    acc_ref[...] = jnp.zeros_like(acc_ref)
    id_copy.wait()
    for (a, b, c), p_ref in zip(offsets(), p_refs):
        seat = origin(a, b, c)
        for f in range(blocks):
            left = q_ref[seat, f * rows:(f + 1) * rows]
            first = f * (per_p + per_q)
            for k in range(per_p):
                product = jnp.dot(left, p_ref[f, k], preferred_element_type=jnp.float32)
                base = ids[seat, first + k] * tile_count
                for l in range(per_q):
                    spot = base + ids[seat, first + per_p + l]
                    acc_ref[spot] += product[l * strip:(l + 1) * strip]


def finish_kernel(x_ref, out_ref):
    seats, tiles, strip, extent = x_ref.shape
    for t in range(tiles):
        stacked = x_ref[:, t].reshape(seats * strip, extent)
        out_ref[:, t * extent:(t + 1) * extent] = stacked.T


def body(p_tiles, p_cols, q_tiles, q_cols):
    blocks, per_p, extent, _ = p_tiles.shape
    per_q = q_tiles.shape[1]
    planes = lax.axis_size("plane")
    pairs, cores, cols = lax.axis_size("pair"), lax.axis_size("core"), lax.axis_size("col")
    tile_count = planes * pairs * cores
    strip = extent // SEATS
    height = blocks * per_q * strip + 2 * SUB
    seat = ("pair", "core", "col")

    sliced = pl.pallas_call(
        slice_kernel,
        out_shape=jax.ShapeDtypeStruct((SEATS, height, extent), q_tiles.dtype),
        in_specs=[pl.BlockSpec(memory_space=pltpu.SMEM)] * 2 + [pl.BlockSpec(memory_space=pltpu.VMEM)],
        name="cut_columns",
    )(p_cols, q_cols, q_tiles)
    p_tiles, sliced = lax.optimization_barrier((p_tiles, sliced))
    q_here = lax.all_to_all(sliced, seat, split_axis=0, concat_axis=0, tiled=True)

    near = {}
    for a, b, c in offsets():
        if c == 0:
            moved = p_tiles
            if a or b:
                hops = []
                for i in range(pairs):
                    for j in range(cols):
                        hops.append((i * cols + j, (i + a) % pairs * cols + (j + b) % cols))
                moved = lax.ppermute(p_tiles, ("pair", "col"), hops)
        else:
            hops = [(i, (i + c) % cores) for i in range(cores)]
            moved = lax.ppermute(near[a, b, 0], "core", hops)
        near[a, b, c] = moved

    acc = pl.pallas_call(
        functools.partial(product_kernel, tile_count),
        out_shape=jax.ShapeDtypeStruct((tile_count * tile_count, strip, extent), jnp.float32),
        scratch_shapes=[
            pltpu.VMEM((SEATS, extent), jnp.int32),
            pltpu.SMEM((SEATS, extent), jnp.int32),
            pltpu.SemaphoreType.DMA,
        ],
        compiler_params=pltpu.CompilerParams(vmem_limit_bytes=24 << 20),
        name="products",
    )(q_here, *near.values())

    parts = acc.reshape(planes, pairs * cores * tile_count, strip, extent)
    here = lax.axis_index("plane")

    if planes == 2:
        away = lax.dynamic_index_in_dim(parts, 1 - here, 0, keepdims=False)
        kept = lax.dynamic_index_in_dim(parts, here, 0, keepdims=False)
        summed = kept + lax.ppermute(away, "plane", [(0, 1), (1, 0)])
    else:
        summed = lax.psum_scatter(parts, "plane", scatter_dimension=0, tiled=False)

    mine = summed.reshape(SEATS, tile_count // cols, strip, extent)
    landed = lax.all_to_all(mine, seat, split_axis=0, concat_axis=0, tiled=True)
    return pl.pallas_call(
        finish_kernel,
        out_shape=jax.ShapeDtypeStruct((extent, tile_count // cols * extent), jnp.float32),
        name="turn",
    )(landed)


def solution(mesh):
    rows, cols = mesh.devices.shape
    pairs = SEATS // (2 * cols)
    shape = (rows // (2 * pairs), pairs, 2, cols)
    every = ("plane", "pair", "core", "col")
    inner = Mesh(mesh.devices.reshape(shape), every)
    placed = (
        P(every, None, None, None),
        P(every, None),
        P(every, None, None, None),
        P(every, None),
    )
    return jax.shard_map(
        body, mesh=inner, in_specs=placed, out_specs=P(every[:3], "col"), check_vma=False
    )
```

```python
import functools

import jax
import jax.numpy as jnp
from jax import lax
from jax.experimental import pallas as pl
from jax.experimental.pallas import tpu as pltpu
from jax.sharding import Mesh
from jax.sharding import PartitionSpec as P

SEATS = 16
SUB = 8


def axes(core, cols):
    bits = [bit for bit in (1, 2, 4, 8) if bit != cols]
    return bits[core:] + bits[:core]


def origin(step, swapped, seat, cols):
    first = lax.rem(seat // cols, 2)
    if swapped:
        seat, first = seat ^ cols, 1 - first
    masks = []
    for core in range(2):
        d = axes(core, cols)
        masks.append((0, d[0], d[1], d[2], d[0] ^ d[1], d[1] ^ d[2], d[2] ^ d[0], 7 * 2 + 1 - cols)[step])
    return seat ^ jnp.where(first == 0, masks[0], masks[1])


def slice_kernel(p_ids, q_ids, q_ref, out_ref):
    blocks, per_q, extent, _ = q_ref.shape
    per_p = p_ids.shape[0]
    strip = extent // SEATS
    rows = per_q * strip
    lane = lax.broadcasted_iota(jnp.int32, (2 * SUB, extent), 1)
    ids = jnp.zeros((2 * SUB, extent), jnp.int32)
    for f in range(blocks):
        for k in range(per_p + per_q):
            value = p_ids[k, f] if k < per_p else q_ids[f, k - per_p]
            ids = jnp.where(lane == f * (per_p + per_q) + k, value, ids)
    ids = ids.astype(out_ref.dtype)
    for f in range(blocks):
        flipped = [q_ref[f, k].astype(jnp.float32).T for k in range(per_q)]
        for j in range(SEATS):
            pieces = [tile[j * strip:(j + 1) * strip] for tile in flipped]
            out_ref[j, f * rows:(f + 1) * rows] = jnp.concatenate(pieces, axis=0).astype(out_ref.dtype)
    for j in range(SEATS):
        out_ref[j, blocks * rows:] = ids


def product_kernel(tile_count, cols, q_ref, *rest):
    p_refs, (acc_ref, held, p_sems, wide_ids, ids, id_sem) = rest[:SEATS], rest[SEATS:]
    blocks, per_p, extent, _ = p_refs[0].shape
    strip = acc_ref.shape[1]
    rows = (q_ref.shape[1] - 2 * SUB) // blocks
    per_q = rows // strip
    copies = [pltpu.make_async_copy(p_refs[i], held.at[i], p_sems.at[i]) for i in range(SEATS)]
    for copy in copies:
        copy.start()
    for s in range(SEATS):
        wide_ids[s:s + 1] = q_ref[s, blocks * rows:, :].astype(jnp.int32)[:1]
    id_copy = pltpu.make_async_copy(wide_ids, ids, id_sem)
    id_copy.start()
    acc_ref[...] = jnp.zeros_like(acc_ref)
    id_copy.wait()
    here = lax.axis_index(("pair", "core", "col"))
    for i in range(SEATS):
        copies[i].wait()
        seat = origin(i // 2, i % 2, here, cols)
        for f in range(blocks):
            left = q_ref[seat, f * rows:(f + 1) * rows]
            first = f * (per_p + per_q)
            for k in range(per_p):
                product = jnp.dot(left, held[i, f, k], preferred_element_type=jnp.float32)
                base = ids[seat, first + k] * tile_count
                for l in range(per_q):
                    spot = base + ids[seat, first + per_p + l]
                    acc_ref[spot] += product[l * strip:(l + 1) * strip]


def finish_kernel(x_ref, out_ref):
    planes, seats, tiles, strip, extent = x_ref.shape
    for t in range(tiles):
        whole = x_ref[0, :, t]
        for z in range(1, planes):
            whole = whole + x_ref[z, :, t]
        out_ref[:, t * extent:(t + 1) * extent] = whole.reshape(seats * strip, extent).T


def body(p_tiles, p_cols, q_tiles, q_cols):
    blocks, per_p, extent, _ = p_tiles.shape
    per_q = q_tiles.shape[1]
    planes = lax.axis_size("plane")
    pairs, cores, cols = lax.axis_size("pair"), lax.axis_size("core"), lax.axis_size("col")
    tile_count = planes * pairs * cores
    strip = extent // SEATS
    height = blocks * per_q * strip + 2 * SUB
    seat = ("pair", "core", "col")

    sliced = pl.pallas_call(
        slice_kernel,
        out_shape=jax.ShapeDtypeStruct((SEATS, height, extent), q_tiles.dtype),
        in_specs=[pl.BlockSpec(memory_space=pltpu.SMEM)] * 2 + [pl.BlockSpec(memory_space=pltpu.VMEM)],
        name="cut_columns",
    )(p_cols.T, q_cols, q_tiles)
    q_here = lax.all_to_all(sliced, seat, split_axis=0, concat_axis=0, tiled=True)

    def along(values, step):
        hops = [(s, s ^ axes(s // cols % 2, cols)[step]) for s in range(SEATS)]
        return lax.ppermute(values, seat, hops)

    def across(values):
        return lax.ppermute(values, seat, [(s, s ^ cols) for s in range(SEATS)])

    one, two, three = (along(p_tiles, step) for step in range(3))
    one, two, three, _ = lax.optimization_barrier((one, two, three, sliced))
    sets = [p_tiles, one, two, three, along(one, 1), along(two, 2), along(three, 0)]
    sets.append(along(sets[4], 2))
    sets = [each for kept in sets for each in (kept, across(kept))]

    acc = pl.pallas_call(
        functools.partial(product_kernel, tile_count, cols),
        out_shape=jax.ShapeDtypeStruct((tile_count * tile_count, strip, extent), jnp.float32),
        in_specs=[pl.BlockSpec(memory_space=pltpu.VMEM)]
        + [pl.BlockSpec(memory_space=pl.ANY)] * SEATS,
        scratch_shapes=[
            pltpu.VMEM((SEATS, blocks, per_p, extent, extent), p_tiles.dtype),
            pltpu.SemaphoreType.DMA((SEATS,)),
            pltpu.VMEM((SEATS, extent), jnp.int32),
            pltpu.SMEM((SEATS, extent), jnp.int32),
            pltpu.SemaphoreType.DMA,
        ],
        compiler_params=pltpu.CompilerParams(vmem_limit_bytes=60 << 20),
        name="products",
    )(q_here, *sets)

    every = ("plane",) + seat
    parts = acc.reshape(planes * SEATS, tile_count // cols, strip, extent)
    landed = lax.all_to_all(parts, every, split_axis=0, concat_axis=0, tiled=True)
    return pl.pallas_call(
        finish_kernel,
        out_shape=jax.ShapeDtypeStruct((extent, tile_count // cols * extent), jnp.float32),
        name="turn",
    )(landed.reshape(planes, SEATS, tile_count // cols, strip, extent))


def solution(mesh):
    rows, cols = mesh.devices.shape
    pairs = SEATS // (2 * cols)
    shape = (rows // (2 * pairs), pairs, 2, cols)
    every = ("plane", "pair", "core", "col")
    inner = Mesh(mesh.devices.reshape(shape), every)
    placed = (
        P(every, None, None, None),
        P(every, None),
        P(every, None, None, None),
        P(every, None),
    )
    return jax.shard_map(
        body, mesh=inner, in_specs=placed, out_specs=P(every[:3], "col"), check_vma=False
    )
```

```python
import functools

import jax
import jax.numpy as jnp
from jax import lax
from jax.experimental import pallas as pl
from jax.experimental.pallas import tpu as pltpu
from jax.sharding import Mesh
from jax.sharding import PartitionSpec as P

SEATS = 16
SUB = 8


def axes(core, cols):
    bits = [bit for bit in (1, 2, 4, 8) if bit != cols]
    return bits[core:] + bits[:core]


def origin(step, swapped, seat, cols):
    first = lax.rem(seat // cols, 2)
    if swapped:
        seat, first = seat ^ cols, 1 - first
    masks = []
    for core in range(2):
        d = axes(core, cols)
        masks.append((0, d[0], d[1], d[2], d[0] ^ d[1], d[1] ^ d[2], d[2] ^ d[0], 7 * 2 + 1 - cols)[step])
    return seat ^ jnp.where(first == 0, masks[0], masks[1])


def slice_kernel(p_ids, q_ids, q_ref, out_ref):
    blocks, per_q, extent, _ = q_ref.shape
    per_p = p_ids.shape[0]
    strip = extent // SEATS
    rows = per_q * strip
    lane = lax.broadcasted_iota(jnp.int32, (2 * SUB, extent), 1)
    ids = jnp.zeros((2 * SUB, extent), jnp.int32)
    for f in range(blocks):
        for k in range(per_p + per_q):
            value = p_ids[k, f] if k < per_p else q_ids[f, k - per_p]
            ids = jnp.where(lane == f * (per_p + per_q) + k, value, ids)
    ids = ids.astype(out_ref.dtype)
    for f in range(blocks):
        flipped = [q_ref[f, k].astype(jnp.float32).T for k in range(per_q)]
        for j in range(SEATS):
            pieces = [tile[j * strip:(j + 1) * strip] for tile in flipped]
            out_ref[j, f * rows:(f + 1) * rows] = jnp.concatenate(pieces, axis=0).astype(out_ref.dtype)
    for j in range(SEATS):
        out_ref[j, blocks * rows:] = ids


def product_kernel(tile_count, cols, steps, q_ref, *rest):
    count = 2 * len(steps)
    p_refs, (acc_ref, wide_ids, ids, id_sem) = rest[:count], rest[-4:]
    blocks, per_p, extent, _ = p_refs[0].shape
    strip = acc_ref.shape[1]
    rows = (q_ref.shape[1] - 2 * SUB) // blocks
    per_q = rows // strip
    for s in range(SEATS):
        wide_ids[s:s + 1] = q_ref[s, blocks * rows:, :].astype(jnp.int32)[:1]
    id_copy = pltpu.make_async_copy(wide_ids, ids, id_sem)
    id_copy.start()
    if len(rest) == count + 4:
        acc_ref[...] = jnp.zeros_like(acc_ref)
    else:
        acc_ref[...] = rest[count][...]
    here = lax.axis_index(("pair", "core", "col"))
    id_copy.wait()
    for i in range(count):
        seat = origin(steps[i // 2], i % 2, here, cols)
        for f in range(blocks):
            left = q_ref[seat, f * rows:(f + 1) * rows]
            first = f * (per_p + per_q)
            for k in range(per_p):
                product = jnp.dot(left, p_refs[i][f, k], preferred_element_type=jnp.float32)
                base = ids[seat, first + k] * tile_count
                for l in range(per_q):
                    spot = base + ids[seat, first + per_p + l]
                    acc_ref[spot] += product[l * strip:(l + 1) * strip]


def add_products(q_here, sets, steps, acc, tile_count, cols, strip):
    per_p, extent = sets[0].shape[1:3]
    operands = [q_here, *sets] + ([] if acc is None else [acc])
    rows = q_here.shape[1] - 2 * SUB
    return pl.pallas_call(
        functools.partial(product_kernel, tile_count, cols, steps),
        out_shape=jax.ShapeDtypeStruct((tile_count * tile_count, strip, extent), jnp.float32),
        in_specs=[pl.BlockSpec(memory_space=pltpu.VMEM)] * len(operands),
        out_specs=pl.BlockSpec(memory_space=pltpu.VMEM),
        scratch_shapes=[
            pltpu.VMEM((SEATS, extent), jnp.int32),
            pltpu.SMEM((SEATS, extent), jnp.int32),
            pltpu.SemaphoreType.DMA,
        ],
        input_output_aliases={} if acc is None else {len(operands) - 1: 0},
        cost_estimate=pl.CostEstimate(
            flops=2 * len(sets) * per_p * rows * extent * extent,
            bytes_accessed=len(sets) * (1 << 20),
            transcendentals=0,
        ),
        compiler_params=pltpu.CompilerParams(vmem_limit_bytes=24 << 20),
        name="products",
    )(*operands)


def finish_kernel(x_ref, out_ref):
    planes, seats, tiles, strip, extent = x_ref.shape
    for t in range(tiles):
        whole = x_ref[0, :, t]
        for z in range(1, planes):
            whole = whole + x_ref[z, :, t]
        out_ref[:, t * extent:(t + 1) * extent] = whole.reshape(seats * strip, extent).T


def body(p_tiles, p_cols, q_tiles, q_cols):
    blocks, per_p, extent, _ = p_tiles.shape
    per_q = q_tiles.shape[1]
    planes, cols = lax.axis_size("plane"), lax.axis_size("col")
    tile_count = planes * SEATS // cols
    strip = extent // SEATS
    height = blocks * per_q * strip + 2 * SUB
    seat = ("pair", "core", "col")

    sliced = pl.pallas_call(
        slice_kernel,
        out_shape=jax.ShapeDtypeStruct((SEATS, height, extent), q_tiles.dtype),
        in_specs=[pl.BlockSpec(memory_space=pltpu.SMEM)] * 2 + [pl.BlockSpec(memory_space=pltpu.VMEM)],
        cost_estimate=pl.CostEstimate(flops=0, bytes_accessed=8 << 20, transcendentals=0),
        name="cut_columns",
    )(p_cols.T, q_cols, q_tiles)
    def along(values, step):
        hops = [(s, s ^ axes(s // cols % 2, cols)[step]) for s in range(SEATS)]
        return lax.ppermute(values, seat, hops)

    def across(values):
        return lax.ppermute(values, seat, [(s, s ^ cols) for s in range(SEATS)])

    one, two, three = (along(p_tiles, step) for step in range(3))
    one, two, three, sliced = lax.optimization_barrier((one, two, three, sliced))
    q_here = lax.all_to_all(sliced, seat, split_axis=0, concat_axis=0, tiled=True)
    four, five, six = along(one, 1), along(two, 2), along(three, 0)
    seven = along(four, 2)
    acc = None
    sets = (p_tiles, one, two, three, four, five, six, seven)
    for steps in ((0, 1, 2, 3), (4, 5, 6), (7,)):
        batch = [each for step in steps for each in (sets[step], across(sets[step]))]
        acc = add_products(q_here, batch, steps, acc, tile_count, cols, strip)
    every = ("plane",) + seat
    parts = acc.reshape(planes * SEATS, tile_count // cols, strip, extent)
    landed = lax.all_to_all(parts, every, split_axis=0, concat_axis=0, tiled=True)
    return pl.pallas_call(
        finish_kernel,
        out_shape=jax.ShapeDtypeStruct((extent, tile_count // cols * extent), jnp.float32),
        name="turn",
    )(landed.reshape(planes, SEATS, tile_count // cols, strip, extent))


def solution(mesh):
    rows, cols = mesh.devices.shape
    pairs = SEATS // (2 * cols)
    shape = (rows // (2 * pairs), pairs, 2, cols)
    every = ("plane", "pair", "core", "col")
    inner = Mesh(mesh.devices.reshape(shape), every)
    placed = (
        P(every, None, None, None),
        P(every, None),
        P(every, None, None, None),
        P(every, None),
    )
    return jax.shard_map(
        body, mesh=inner, in_specs=placed, out_specs=P(every[:3], "col"), check_vma=False
    )
```

```python
import functools

import jax
import jax.numpy as jnp
from jax import lax
from jax.experimental import pallas as pl
from jax.experimental.pallas import tpu as pltpu
from jax.sharding import Mesh
from jax.sharding import PartitionSpec as P

SEATS = 16
SUB = 8


def axes(core, cols):
    bits = [bit for bit in (1, 2, 4, 8) if bit != cols]
    return bits[core:] + bits[:core]


def origin(step, swapped, seat, cols):
    first = lax.rem(seat // cols, 2)
    if swapped:
        seat, first = seat ^ cols, 1 - first
    masks = []
    for core in range(2):
        d = axes(core, cols)
        masks.append((0, d[0], d[1], d[2], d[0] ^ d[1], d[1] ^ d[2], d[2] ^ d[0], 7 * 2 + 1 - cols)[step])
    return seat ^ jnp.where(first == 0, masks[0], masks[1])


def slice_kernel(p_ids, q_ids, q_ref, out_ref):
    blocks, per_q, extent, _ = q_ref.shape
    per_p = p_ids.shape[0]
    strip = extent // SEATS
    rows = per_q * strip
    lane = lax.broadcasted_iota(jnp.int32, (2 * SUB, extent), 1)
    ids = jnp.zeros((2 * SUB, extent), jnp.int32)
    for f in range(blocks):
        for k in range(per_p + per_q):
            value = p_ids[k, f] if k < per_p else q_ids[f, k - per_p]
            ids = jnp.where(lane == f * (per_p + per_q) + k, value, ids)
    ids = ids.astype(out_ref.dtype)
    for f in range(blocks):
        flipped = [q_ref[f, k].astype(jnp.float32).T for k in range(per_q)]
        for j in range(SEATS):
            pieces = [tile[j * strip:(j + 1) * strip] for tile in flipped]
            out_ref[j, f * rows:(f + 1) * rows] = jnp.concatenate(pieces, axis=0).astype(out_ref.dtype)
    for j in range(SEATS):
        out_ref[j, blocks * rows:] = ids


def product_kernel(tile_count, cols, routes, q_ref, *rest):
    count = len(routes)
    p_refs, (acc_ref, wide_ids, ids, id_sem) = rest[:count], rest[-4:]
    blocks, per_p, extent, _ = p_refs[0].shape
    strip = acc_ref.shape[1]
    rows = (q_ref.shape[1] - 2 * SUB) // blocks
    per_q = rows // strip
    for s in range(SEATS):
        wide_ids[s:s + 1] = q_ref[s, blocks * rows:, :].astype(jnp.int32)[:1]
    id_copy = pltpu.make_async_copy(wide_ids, ids, id_sem)
    id_copy.start()
    if len(rest) == count + 4:
        acc_ref[...] = jnp.zeros_like(acc_ref)
    else:
        acc_ref[...] = rest[count][...]
    here = lax.axis_index(("pair", "core", "col"))
    id_copy.wait()
    for i in range(count):
        seat = origin(*routes[i], here, cols)
        for f in range(blocks):
            left = q_ref[seat, f * rows:(f + 1) * rows]
            first = f * (per_p + per_q)
            for k in range(per_p):
                product = jnp.dot(left, p_refs[i][f, k], preferred_element_type=jnp.float32)
                base = ids[seat, first + k] * tile_count
                for l in range(per_q):
                    spot = base + ids[seat, first + per_p + l]
                    acc_ref[spot] += product[l * strip:(l + 1) * strip]


def add_products(q_here, sets, routes, acc, tile_count, cols, strip):
    per_p, extent = sets[0].shape[1:3]
    operands = [q_here, *sets] + ([] if acc is None else [acc])
    rows = q_here.shape[1] - 2 * SUB
    return pl.pallas_call(
        functools.partial(product_kernel, tile_count, cols, routes),
        out_shape=jax.ShapeDtypeStruct((tile_count * tile_count, strip, extent), jnp.float32),
        in_specs=[pl.BlockSpec(memory_space=pltpu.VMEM)] * len(operands),
        out_specs=pl.BlockSpec(memory_space=pltpu.VMEM),
        scratch_shapes=[
            pltpu.VMEM((SEATS, extent), jnp.int32),
            pltpu.SMEM((SEATS, extent), jnp.int32),
            pltpu.SemaphoreType.DMA,
        ],
        input_output_aliases={} if acc is None else {len(operands) - 1: 0},
        cost_estimate=pl.CostEstimate(
            flops=2 * len(sets) * per_p * rows * extent * extent,
            bytes_accessed=len(sets) * (1 << 20),
            transcendentals=0,
        ),
        compiler_params=pltpu.CompilerParams(vmem_limit_bytes=16 << 20),
        name="products",
    )(*operands)


def finish_kernel(x_ref, out_ref):
    planes, seats, tiles, strip, extent = x_ref.shape
    for t in range(tiles):
        whole = x_ref[0, :, t]
        for z in range(1, planes):
            whole = whole + x_ref[z, :, t]
        out_ref[:, t * extent:(t + 1) * extent] = whole.reshape(seats * strip, extent).T


def body(p_tiles, p_cols, q_tiles, q_cols):
    blocks, per_p, extent, _ = p_tiles.shape
    per_q = q_tiles.shape[1]
    planes, cols = lax.axis_size("plane"), lax.axis_size("col")
    tile_count = planes * SEATS // cols
    strip = extent // SEATS
    height = blocks * per_q * strip + 2 * SUB
    seat = ("pair", "core", "col")

    sliced = pl.pallas_call(
        slice_kernel,
        out_shape=jax.ShapeDtypeStruct((SEATS, height, extent), q_tiles.dtype),
        in_specs=[pl.BlockSpec(memory_space=pltpu.SMEM)] * 2 + [pl.BlockSpec(memory_space=pltpu.VMEM)],
        cost_estimate=pl.CostEstimate(flops=0, bytes_accessed=8 << 20, transcendentals=0),
        compiler_params=pltpu.CompilerParams(vmem_limit_bytes=8 << 20),
        name="cut_columns",
    )(p_cols.T, q_cols, q_tiles)
    def along(values, step):
        hops = [(s, s ^ axes(s // cols % 2, cols)[step]) for s in range(SEATS)]
        return lax.ppermute(values, seat, hops)

    def across(values):
        return lax.ppermute(values, seat, [(s, s ^ cols) for s in range(SEATS)])

    def opposite(values):
        return lax.ppermute(values, seat, [(s, s ^ (SEATS - 1 - cols)) for s in range(SEATS)])

    def add(acc, sets, routes):
        return add_products(q_here, sets, routes, acc, tile_count, cols, strip)

    beside = across(p_tiles)
    first = [along(p_tiles, step) for step in range(3)] + [opposite(p_tiles)]
    sliced, beside = lax.optimization_barrier((sliced, beside))
    q_here = lax.all_to_all(sliced, seat, split_axis=0, concat_axis=0, tiled=True)
    second = [along(first[step], (step + 1) % 3) for step in range(3)]
    sets = [p_tiles, beside] + first + [across(each) for each in first]
    steps = (1, 2, 3, 7)
    acc = add(
        None, sets, [(0, 0), (0, 1)] + [(step, 0) for step in steps] + [(step, 1) for step in steps]
    )
    *second, acc = lax.optimization_barrier((*second, acc))
    crossed = [across(each) for each in second]
    acc = add(acc, second, [(4, 0), (5, 0), (6, 0)])
    acc = add(acc, crossed, [(4, 1), (5, 1), (6, 1)])
    every = ("plane",) + seat
    parts = acc.reshape(planes * SEATS, tile_count // cols, strip, extent)
    landed = lax.all_to_all(parts, every, split_axis=0, concat_axis=0, tiled=True)
    return pl.pallas_call(
        finish_kernel,
        out_shape=jax.ShapeDtypeStruct((extent, tile_count // cols * extent), jnp.float32),
        compiler_params=pltpu.CompilerParams(vmem_limit_bytes=16 << 20),
        name="turn",
    )(landed.reshape(planes, SEATS, tile_count // cols, strip, extent))


def solution(mesh):
    rows, cols = mesh.devices.shape
    pairs = SEATS // (2 * cols)
    shape = (rows // (2 * pairs), pairs, 2, cols)
    every = ("plane", "pair", "core", "col")
    inner = Mesh(mesh.devices.reshape(shape), every)
    placed = (
        P(every, None, None, None),
        P(every, None),
        P(every, None, None, None),
        P(every, None),
    )
    return jax.shard_map(
        body, mesh=inner, in_specs=placed, out_specs=P(every[:3], "col"), check_vma=False
    )
```

```python
import functools

import jax
import jax.numpy as jnp
from jax import lax
from jax.experimental import pallas as pl
from jax.experimental.pallas import tpu as pltpu
from jax.sharding import Mesh
from jax.sharding import PartitionSpec as P

SEATS = 16
SUB = 8


def axes(core, cols):
    bits = [bit for bit in (1, 2, 4, 8) if bit != cols]
    return bits[core:] + bits[:core]


def origin(step, swapped, seat, cols):
    first = lax.rem(seat // cols, 2)
    if swapped:
        seat, first = seat ^ cols, 1 - first
    masks = []
    for core in range(2):
        d = axes(core, cols)
        masks.append((0, d[0], d[1], d[2], d[0] ^ d[1], d[1] ^ d[2], d[2] ^ d[0], 7 * 2 + 1 - cols)[step])
    return seat ^ jnp.where(first == 0, masks[0], masks[1])


def slice_kernel(p_ids, q_ids, q_ref, out_ref):
    blocks, per_q, extent, _ = q_ref.shape
    per_p = p_ids.shape[0]
    strip = extent // SEATS
    rows = per_q * strip
    lane = lax.broadcasted_iota(jnp.int32, (2 * SUB, extent), 1)
    ids = jnp.zeros((2 * SUB, extent), jnp.int32)
    for f in range(blocks):
        for k in range(per_p + per_q):
            value = p_ids[k, f] if k < per_p else q_ids[f, k - per_p]
            ids = jnp.where(lane == f * (per_p + per_q) + k, value, ids)
    ids = ids.astype(out_ref.dtype)
    for f in range(blocks):
        flipped = [q_ref[f, k].astype(jnp.float32).T for k in range(per_q)]
        for j in range(SEATS):
            pieces = [tile[j * strip:(j + 1) * strip] for tile in flipped]
            out_ref[j, f * rows:(f + 1) * rows] = jnp.concatenate(pieces, axis=0).astype(out_ref.dtype)
    for j in range(SEATS):
        out_ref[j, blocks * rows:] = ids


def product_kernel(tile_count, cols, routes, q_ref, *rest):
    count = len(routes)
    p_refs, (acc_ref, held, p_sems, wide_ids, ids, id_sem) = rest[:count], rest[-6:]
    blocks, per_p, extent, _ = p_refs[0].shape
    strip = acc_ref.shape[1]
    rows = (q_ref.shape[1] - 2 * SUB) // blocks
    per_q = rows // strip
    copies = [pltpu.make_async_copy(p_refs[i], held.at[i], p_sems.at[i]) for i in range(count)]
    for copy in copies:
        copy.start()
    for s in range(SEATS):
        wide_ids[s:s + 1] = q_ref[s, blocks * rows:, :].astype(jnp.int32)[:1]
    id_copy = pltpu.make_async_copy(wide_ids, ids, id_sem)
    id_copy.start()
    if len(rest) == count + 6:
        acc_ref[...] = jnp.zeros_like(acc_ref)
    else:
        acc_ref[...] = rest[count][...]
    here = lax.axis_index(("pair", "core", "col"))
    id_copy.wait()
    for i in range(count):
        copies[i].wait()
        seat = origin(*routes[i], here, cols)
        for f in range(blocks):
            left = q_ref[seat, f * rows:(f + 1) * rows]
            first = f * (per_p + per_q)
            for k in range(per_p):
                product = jnp.dot(left, held[i, f, k], preferred_element_type=jnp.float32)
                base = ids[seat, first + k] * tile_count
                for l in range(per_q):
                    spot = base + ids[seat, first + per_p + l]
                    acc_ref[spot] += product[l * strip:(l + 1) * strip]


def add_products(q_here, sets, routes, acc, tile_count, cols, strip):
    per_p, extent = sets[0].shape[1:3]
    more = [] if acc is None else [acc]
    operands = [q_here, *sets, *more]
    in_vmem = pl.BlockSpec(memory_space=pltpu.VMEM)
    rows = q_here.shape[1] - 2 * SUB
    return pl.pallas_call(
        functools.partial(product_kernel, tile_count, cols, routes),
        out_shape=jax.ShapeDtypeStruct((tile_count * tile_count, strip, extent), jnp.float32),
        in_specs=[in_vmem] + [pl.BlockSpec(memory_space=pl.ANY)] * len(sets) + [in_vmem] * len(more),
        out_specs=pl.BlockSpec(memory_space=pltpu.VMEM),
        scratch_shapes=[
            pltpu.VMEM((len(sets),) + sets[0].shape, sets[0].dtype),
            pltpu.SemaphoreType.DMA((len(sets),)),
            pltpu.VMEM((SEATS, extent), jnp.int32),
            pltpu.SMEM((SEATS, extent), jnp.int32),
            pltpu.SemaphoreType.DMA,
        ],
        input_output_aliases={} if acc is None else {len(operands) - 1: 0},
        cost_estimate=pl.CostEstimate(
            flops=2 * len(sets) * per_p * rows * extent * extent,
            bytes_accessed=len(sets) * (1 << 20),
            transcendentals=0,
        ),
        compiler_params=pltpu.CompilerParams(vmem_limit_bytes=16 << 20),
        name="products",
    )(*operands)


def finish_kernel(x_ref, out_ref):
    planes, seats, tiles, strip, extent = x_ref.shape
    for t in range(tiles):
        whole = x_ref[0, :, t]
        for z in range(1, planes):
            whole = whole + x_ref[z, :, t]
        out_ref[:, t * extent:(t + 1) * extent] = whole.reshape(seats * strip, extent).T


def body(p_tiles, p_cols, q_tiles, q_cols):
    blocks, per_p, extent, _ = p_tiles.shape
    per_q = q_tiles.shape[1]
    planes, cols = lax.axis_size("plane"), lax.axis_size("col")
    tile_count = planes * SEATS // cols
    strip = extent // SEATS
    height = blocks * per_q * strip + 2 * SUB
    seat = ("pair", "core", "col")

    sliced = pl.pallas_call(
        slice_kernel,
        out_shape=jax.ShapeDtypeStruct((SEATS, height, extent), q_tiles.dtype),
        in_specs=[pl.BlockSpec(memory_space=pltpu.SMEM)] * 2 + [pl.BlockSpec(memory_space=pltpu.VMEM)],
        cost_estimate=pl.CostEstimate(flops=0, bytes_accessed=8 << 20, transcendentals=0),
        name="cut_columns",
    )(p_cols.T, q_cols, q_tiles)

    def along(values, step):
        hops = [(s, s ^ axes(s // cols % 2, cols)[step]) for s in range(SEATS)]
        return lax.ppermute(values, seat, hops)

    def across(values):
        return lax.ppermute(values, seat, [(s, s ^ cols) for s in range(SEATS)])

    def opposite(values):
        return lax.ppermute(values, seat, [(s, s ^ (SEATS - 1 - cols)) for s in range(SEATS)])

    def add(acc, sets, routes):
        return add_products(q_here, sets, routes, acc, tile_count, cols, strip)

    beside = across(p_tiles)
    first = [along(p_tiles, step) for step in range(3)] + [opposite(p_tiles)]
    sliced, *first[:3] = lax.optimization_barrier((sliced, *first[:3]))
    q_here = lax.all_to_all(sliced, seat, split_axis=0, concat_axis=0, tiled=True)
    second = [along(first[step], (step + 1) % 3) for step in range(3)]
    first = lax.optimization_barrier(first)
    sets = [p_tiles, beside] + first + [across(each) for each in first]
    steps = (1, 2, 3, 7)
    acc = add(
        None, sets, [(0, 0), (0, 1)] + [(step, 0) for step in steps] + [(step, 1) for step in steps]
    )
    crossed = [across(each) for each in second]
    acc = add(acc, second, [(4, 0), (5, 0), (6, 0)])
    acc = add(acc, crossed, [(4, 1), (5, 1), (6, 1)])
    every = ("plane",) + seat
    parts = acc.reshape(planes * SEATS, tile_count // cols, strip, extent)
    landed = lax.all_to_all(parts, every, split_axis=0, concat_axis=0, tiled=True)
    return pl.pallas_call(
        finish_kernel,
        out_shape=jax.ShapeDtypeStruct((extent, tile_count // cols * extent), jnp.float32),
        compiler_params=pltpu.CompilerParams(vmem_limit_bytes=16 << 20),
        name="turn",
    )(landed.reshape(planes, SEATS, tile_count // cols, strip, extent))


def solution(mesh):
    rows, cols = mesh.devices.shape
    pairs = SEATS // (2 * cols)
    shape = (rows // (2 * pairs), pairs, 2, cols)
    every = ("plane", "pair", "core", "col")
    inner = Mesh(mesh.devices.reshape(shape), every)
    placed = (
        P(every, None, None, None),
        P(every, None),
        P(every, None, None, None),
        P(every, None),
    )
    return jax.shard_map(
        body, mesh=inner, in_specs=placed, out_specs=P(every[:3], "col"), check_vma=False
    )
```

```python
import functools

import jax
import jax.numpy as jnp
from jax import lax
from jax.experimental import pallas as pl
from jax.experimental.pallas import tpu as pltpu
from jax.sharding import Mesh
from jax.sharding import PartitionSpec as P

SEATS = 16
SUB = 8


def axes(core, cols):
    bits = [bit for bit in (1, 2, 4, 8) if bit != cols]
    return bits[core:] + bits[:core]


def origin(step, swapped, seat, cols):
    first = lax.rem(seat // cols, 2)
    if swapped:
        seat, first = seat ^ cols, 1 - first
    masks = []
    for core in range(2):
        d = axes(core, cols)
        masks.append((0, d[0], d[1], d[2], d[0] ^ d[1], d[1] ^ d[2], d[2] ^ d[0], 7 * 2 + 1 - cols)[step])
    return seat ^ jnp.where(first == 0, masks[0], masks[1])


def slice_kernel(p_ids, q_ids, q_ref, out_ref):
    blocks, per_q, extent, _ = q_ref.shape
    per_p = p_ids.shape[0]
    strip = extent // SEATS
    rows = per_q * strip
    lane = lax.broadcasted_iota(jnp.int32, (2 * SUB, extent), 1)
    ids = jnp.zeros((2 * SUB, extent), jnp.int32)
    for f in range(blocks):
        for k in range(per_p + per_q):
            value = p_ids[k, f] if k < per_p else q_ids[f, k - per_p]
            ids = jnp.where(lane == f * (per_p + per_q) + k, value, ids)
    ids = ids.astype(out_ref.dtype)
    for f in range(blocks):
        flipped = [q_ref[f, k].astype(jnp.float32).T for k in range(per_q)]
        for j in range(SEATS):
            pieces = [tile[j * strip:(j + 1) * strip] for tile in flipped]
            out_ref[j, f * rows:(f + 1) * rows] = jnp.concatenate(pieces, axis=0).astype(out_ref.dtype)
    for j in range(SEATS):
        out_ref[j, blocks * rows:] = ids


def product_kernel(tile_count, cols, routes, q_ref, *rest):
    count = len(routes)
    p_refs, (acc_ref, wide_ids, ids, id_sem) = rest[:count], rest[-4:]
    blocks, per_p, extent, _ = p_refs[0].shape
    strip = acc_ref.shape[1]
    rows = (q_ref.shape[1] - 2 * SUB) // blocks
    per_q = rows // strip
    for s in range(SEATS):
        wide_ids[s:s + 1] = q_ref[s, blocks * rows:, :].astype(jnp.int32)[:1]
    id_copy = pltpu.make_async_copy(wide_ids, ids, id_sem)
    id_copy.start()
    if len(rest) == count + 4:
        acc_ref[...] = jnp.zeros_like(acc_ref)
    else:
        acc_ref[...] = rest[count][...]
    here = lax.axis_index(("pair", "core", "col"))
    id_copy.wait()
    for i in range(count):
        seat = origin(*routes[i], here, cols)
        for f in range(blocks):
            left = q_ref[seat, f * rows:(f + 1) * rows]
            first = f * (per_p + per_q)
            for k in range(per_p):
                product = jnp.dot(left, p_refs[i][f, k], preferred_element_type=jnp.float32)
                base = ids[seat, first + k] * tile_count
                for l in range(per_q):
                    spot = base + ids[seat, first + per_p + l]
                    acc_ref[spot] += product[l * strip:(l + 1) * strip]


def add_products(q_here, sets, routes, acc, tile_count, cols, strip):
    per_p, extent = sets[0].shape[1:3]
    operands = [q_here, *sets] + ([] if acc is None else [acc])
    rows = q_here.shape[1] - 2 * SUB
    return pl.pallas_call(
        functools.partial(product_kernel, tile_count, cols, routes),
        out_shape=jax.ShapeDtypeStruct((tile_count * tile_count, strip, extent), jnp.float32),
        in_specs=[pl.BlockSpec(memory_space=pltpu.VMEM)] * len(operands),
        out_specs=pl.BlockSpec(memory_space=pltpu.VMEM),
        scratch_shapes=[
            pltpu.VMEM((SEATS, extent), jnp.int32),
            pltpu.SMEM((SEATS, extent), jnp.int32),
            pltpu.SemaphoreType.DMA,
        ],
        input_output_aliases={} if acc is None else {len(operands) - 1: 0},
        cost_estimate=pl.CostEstimate(
            flops=2 * len(sets) * per_p * rows * extent * extent,
            bytes_accessed=len(sets) * (1 << 20),
            transcendentals=0,
        ),
        compiler_params=pltpu.CompilerParams(vmem_limit_bytes=16 << 20),
        name="products",
    )(*operands)


def finish_kernel(x_ref, out_ref):
    planes, seats, tiles, strip, extent = x_ref.shape
    for t in range(tiles):
        whole = x_ref[0, :, t]
        for z in range(1, planes):
            whole = whole + x_ref[z, :, t]
        out_ref[:, t * extent:(t + 1) * extent] = whole.reshape(seats * strip, extent).T


def body(p_tiles, p_cols, q_tiles, q_cols):
    blocks, per_p, extent, _ = p_tiles.shape
    per_q = q_tiles.shape[1]
    planes, cols = lax.axis_size("plane"), lax.axis_size("col")
    tile_count = planes * SEATS // cols
    strip = extent // SEATS
    height = blocks * per_q * strip + 2 * SUB
    seat = ("pair", "core", "col")

    sliced = pl.pallas_call(
        slice_kernel,
        out_shape=jax.ShapeDtypeStruct((SEATS, height, extent), q_tiles.dtype),
        in_specs=[pl.BlockSpec(memory_space=pltpu.SMEM)] * 2 + [pl.BlockSpec(memory_space=pltpu.VMEM)],
        cost_estimate=pl.CostEstimate(flops=0, bytes_accessed=8 << 20, transcendentals=0),
        name="cut_columns",
    )(p_cols.T, q_cols, q_tiles)

    def along(values, step):
        hops = [(s, s ^ axes(s // cols % 2, cols)[step]) for s in range(SEATS)]
        return lax.ppermute(values, seat, hops)

    def across(values):
        return lax.ppermute(values, seat, [(s, s ^ cols) for s in range(SEATS)])

    def add(acc, sets, routes):
        return add_products(q_here, sets, routes, acc, tile_count, cols, strip)

    first = [along(p_tiles, step) for step in range(3)]
    sliced, *first = lax.optimization_barrier((sliced, *first))
    q_here = lax.all_to_all(sliced, seat, split_axis=0, concat_axis=0, tiled=True)
    second = [along(first[step], (step + 1) % 3) for step in range(3)]
    sets = [p_tiles] + first + [across(each) for each in [p_tiles] + first]
    q_here, *second = lax.optimization_barrier((q_here, *second))
    third = along(second[0], 2)
    acc = add(None, sets, [(step, swapped) for swapped in (0, 1) for step in range(4)])
    sets = second + [across(each) for each in second]
    acc = add(acc, sets, [(step, swapped) for swapped in (0, 1) for step in (4, 5, 6)])
    acc = add(acc, [third, across(third)], [(7, 0), (7, 1)])
    every = ("plane",) + seat
    parts = acc.reshape(planes * SEATS, tile_count // cols, strip, extent)
    landed = lax.all_to_all(parts, every, split_axis=0, concat_axis=0, tiled=True)
    return pl.pallas_call(
        finish_kernel,
        out_shape=jax.ShapeDtypeStruct((extent, tile_count // cols * extent), jnp.float32),
        compiler_params=pltpu.CompilerParams(vmem_limit_bytes=16 << 20),
        name="turn",
    )(landed.reshape(planes, SEATS, tile_count // cols, strip, extent))


def solution(mesh):
    rows, cols = mesh.devices.shape
    pairs = SEATS // (2 * cols)
    shape = (rows // (2 * pairs), pairs, 2, cols)
    every = ("plane", "pair", "core", "col")
    inner = Mesh(mesh.devices.reshape(shape), every)
    placed = (
        P(every, None, None, None),
        P(every, None),
        P(every, None, None, None),
        P(every, None),
    )
    return jax.shard_map(
        body, mesh=inner, in_specs=placed, out_specs=P(every[:3], "col"), check_vma=False
    )
```

```python
import functools

import jax
import jax.numpy as jnp
from jax import lax
from jax.experimental import pallas as pl
from jax.experimental.pallas import tpu as pltpu
from jax.sharding import Mesh
from jax.sharding import PartitionSpec as P

SEATS = 16
SUB = 8
FLOOR = 100


def axes(core, cols):
    bits = [bit for bit in (1, 2, 4, 8) if bit != cols]
    return bits[core:] + bits[:core]


def origin(step, swapped, seat, cols):
    first = lax.rem(seat // cols, 2)
    if swapped:
        seat, first = seat ^ cols, 1 - first
    masks = []
    for core in range(2):
        d = axes(core, cols)
        masks.append((0, d[0], d[1], d[2], d[0] ^ d[1], d[1] ^ d[2], d[2] ^ d[0], 7 * 2 + 1 - cols)[step])
    return seat ^ jnp.where(first == 0, masks[0], masks[1])


def slice_kernel(p_ids, q_ids, q_ref, out_ref):
    blocks, per_q, extent, _ = q_ref.shape
    per_p = p_ids.shape[0]
    strip = extent // SEATS
    rows = per_q * strip
    lane = lax.broadcasted_iota(jnp.int32, (2 * SUB, extent), 1)
    ids = jnp.zeros((2 * SUB, extent), jnp.int32)
    for f in range(blocks):
        for k in range(per_p + per_q):
            value = p_ids[k, f] if k < per_p else q_ids[f, k - per_p]
            ids = jnp.where(lane == f * (per_p + per_q) + k, value, ids)
    ids = ids.astype(out_ref.dtype)
    for f in range(blocks):
        flipped = [q_ref[f, k].astype(jnp.float32).T for k in range(per_q)]
        for j in range(SEATS):
            pieces = [tile[j * strip:(j + 1) * strip] for tile in flipped]
            out_ref[j, f * rows:(f + 1) * rows] = jnp.concatenate(pieces, axis=0).astype(out_ref.dtype)
    for j in range(SEATS):
        out_ref[j, blocks * rows:] = ids


def product_kernel(tile_count, cols, routes, q_ref, *rest):
    count = len(routes)
    p_refs, (acc_ref, wide_ids, ids, id_sem) = rest[:count], rest[-4:]
    blocks, per_p, extent, _ = p_refs[0].shape
    strip = acc_ref.shape[1]
    rows = (q_ref.shape[1] - 2 * SUB) // blocks
    per_q = rows // strip
    for s in range(SEATS):
        wide_ids[s:s + 1] = q_ref[s, blocks * rows:, :].astype(jnp.int32)[:1]
    id_copy = pltpu.make_async_copy(wide_ids, ids, id_sem)
    id_copy.start()
    if len(rest) == count + 4:
        acc_ref[...] = jnp.zeros_like(acc_ref)
    else:
        acc_ref[...] = rest[count][...]
    here = lax.axis_index(("pair", "core", "col"))
    id_copy.wait()
    for i in range(count):
        seat = origin(*routes[i], here, cols)
        for f in range(blocks):
            left = q_ref[seat, f * rows:(f + 1) * rows]
            first = f * (per_p + per_q)
            for k in range(per_p):
                product = jnp.dot(left, p_refs[i][f, k], preferred_element_type=jnp.float32)
                base = ids[seat, first + k] * tile_count
                for l in range(per_q):
                    spot = base + ids[seat, first + per_p + l]
                    acc_ref[spot] += product[l * strip:(l + 1) * strip]


def add_products(q_here, sets, routes, acc, tile_count, cols, strip):
    per_p, extent = sets[0].shape[1:3]
    operands = [q_here, *sets] + ([] if acc is None else [acc])
    rows = q_here.shape[1] - 2 * SUB
    return pl.pallas_call(
        functools.partial(product_kernel, tile_count, cols, routes),
        out_shape=jax.ShapeDtypeStruct((tile_count * tile_count, strip, extent), jnp.float32),
        in_specs=[pl.BlockSpec(memory_space=pltpu.VMEM)] * len(operands),
        out_specs=pl.BlockSpec(memory_space=pltpu.VMEM),
        scratch_shapes=[
            pltpu.VMEM((SEATS, extent), jnp.int32),
            pltpu.SMEM((SEATS, extent), jnp.int32),
            pltpu.SemaphoreType.DMA,
        ],
        input_output_aliases={} if acc is None else {len(operands) - 1: 0},
        cost_estimate=pl.CostEstimate(
            flops=2 * len(sets) * per_p * rows * extent * extent,
            bytes_accessed=len(sets) * (1 << 20),
            transcendentals=0,
        ),
        compiler_params=pltpu.CompilerParams(vmem_limit_bytes=16 << 20),
        name="products",
    )(*operands)


def code_kernel(acc_ref, out_ref):
    tiles = acc_ref.shape[1]
    extra = 24 // tiles
    half = 1 << (15 + extra)
    for d in range(acc_ref.shape[0]):
        values = [acc_ref[d, t] for t in range(tiles)]
        left = functools.reduce(jnp.maximum, [jnp.abs(value) for value in values]) * 2.0**FLOOR
        scale = jnp.full(left.shape, 2.0 ** (FLOOR - 1) * half, jnp.float32)
        last = jnp.zeros(left.shape, jnp.int32)
        for i in reversed(range(7)):
            big = left >= 2.0 ** (1 << i)
            down = jnp.where(big, 2.0 ** -(1 << i), 1.0)
            left, scale = left * down, scale * down
            last = jnp.where(big, last + (1 << i), last)
        low = []
        for t, value in enumerate(values):
            whole = jnp.floor(value * scale + 0.5).astype(jnp.int32)
            whole = jnp.minimum(whole, half - 1) + half
            low.append(whole & 0xFFFF)
            last = last | ((whole >> 16) << (8 + extra * t))
        for j in range(tiles // 2):
            out_ref[d, j] = low[2 * j] | (low[2 * j + 1] << 16)
        out_ref[d, tiles // 2] = last


def finish_kernel(x_ref, out_ref):
    planes, seats, words, strip, extent = x_ref.shape
    tiles = 2 * (words - 1)
    extra = 24 // tiles
    half = 1 << (15 + extra)
    wholes = [None] * tiles
    for z in range(planes):
        last = x_ref[z, :, words - 1]
        scale = jnp.full(last.shape, 2.0 ** (1 - FLOOR) / half, jnp.float32)
        for i in range(7):
            scale = scale * jnp.where((last >> i) & 1 == 1, 2.0 ** (1 << i), 1.0)
        for t in range(tiles):
            whole = (x_ref[z, :, t // 2] >> (16 * (t % 2))) & 0xFFFF
            whole = whole | (((last >> (8 + extra * t)) & ((1 << extra) - 1)) << 16)
            value = (whole - half).astype(jnp.float32) * scale
            wholes[t] = value if z == 0 else wholes[t] + value
    for t in range(tiles):
        out_ref[:, t * extent:(t + 1) * extent] = wholes[t].reshape(seats * strip, extent).T


def body(p_tiles, p_cols, q_tiles, q_cols):
    blocks, per_p, extent, _ = p_tiles.shape
    per_q = q_tiles.shape[1]
    planes, cols = lax.axis_size("plane"), lax.axis_size("col")
    tile_count = planes * SEATS // cols
    strip = extent // SEATS
    height = blocks * per_q * strip + 2 * SUB
    seat = ("pair", "core", "col")

    sliced = pl.pallas_call(
        slice_kernel,
        out_shape=jax.ShapeDtypeStruct((SEATS, height, extent), q_tiles.dtype),
        in_specs=[pl.BlockSpec(memory_space=pltpu.SMEM)] * 2 + [pl.BlockSpec(memory_space=pltpu.VMEM)],
        cost_estimate=pl.CostEstimate(flops=0, bytes_accessed=8 << 20, transcendentals=0),
        name="cut_columns",
    )(p_cols.T, q_cols, q_tiles)

    def along(values, step):
        hops = [(s, s ^ axes(s // cols % 2, cols)[step]) for s in range(SEATS)]
        return lax.ppermute(values, seat, hops)

    def across(values):
        return lax.ppermute(values, seat, [(s, s ^ cols) for s in range(SEATS)])

    def add(acc, sets, routes):
        return add_products(q_here, sets, routes, acc, tile_count, cols, strip)

    first = [along(p_tiles, step) for step in range(3)]
    sliced, *first = lax.optimization_barrier((sliced, *first))
    q_here = lax.all_to_all(sliced, seat, split_axis=0, concat_axis=0, tiled=True)
    second = [along(first[step], (step + 1) % 3) for step in range(3)]
    sets = [p_tiles] + first + [across(each) for each in [p_tiles] + first]
    q_here, *second = lax.optimization_barrier((q_here, *second))
    third = along(second[0], 2)
    acc = add(None, sets, [(step, swapped) for swapped in (0, 1) for step in range(4)])
    third, acc = lax.optimization_barrier((third, acc))
    sets = second + [across(each) for each in second]
    acc = add(acc, sets, [(step, swapped) for swapped in (0, 1) for step in (4, 5, 6)])
    acc = add(acc, [third, across(third)], [(7, 0), (7, 1)])
    every = ("plane",) + seat
    tiles = tile_count // cols
    words = tiles // 2 + 1
    coded = pl.pallas_call(
        code_kernel,
        out_shape=jax.ShapeDtypeStruct((planes * SEATS, words, strip, extent), jnp.int32),
        compiler_params=pltpu.CompilerParams(vmem_limit_bytes=16 << 20),
        name="code",
    )(acc.reshape(planes * SEATS, tiles, strip, extent))
    landed = lax.all_to_all(coded, every, split_axis=0, concat_axis=0, tiled=True)
    return pl.pallas_call(
        finish_kernel,
        out_shape=jax.ShapeDtypeStruct((extent, tiles * extent), jnp.float32),
        compiler_params=pltpu.CompilerParams(vmem_limit_bytes=16 << 20),
        name="turn",
    )(landed.reshape(planes, SEATS, words, strip, extent))


def solution(mesh):
    rows, cols = mesh.devices.shape
    pairs = SEATS // (2 * cols)
    shape = (rows // (2 * pairs), pairs, 2, cols)
    every = ("plane", "pair", "core", "col")
    inner = Mesh(mesh.devices.reshape(shape), every)
    placed = (
        P(every, None, None, None),
        P(every, None),
        P(every, None, None, None),
        P(every, None),
    )
    return jax.shard_map(
        body, mesh=inner, in_specs=placed, out_specs=P(every[:3], "col"), check_vma=False
    )
```

```python
import functools

import jax
import jax.numpy as jnp
from jax import lax
from jax.experimental import pallas as pl
from jax.experimental.pallas import tpu as pltpu
from jax.sharding import Mesh
from jax.sharding import PartitionSpec as P

SEATS = 16
SUB = 8
FLOOR = 100


def axes(core, cols):
    bits = [bit for bit in (1, 2, 4, 8) if bit != cols]
    return bits[core:] + bits[:core]


def origin(step, swapped, seat, cols):
    first = lax.rem(seat // cols, 2)
    if swapped:
        seat, first = seat ^ cols, 1 - first
    masks = []
    for core in range(2):
        d = axes(core, cols)
        masks.append((0, d[0], d[1], d[2], d[0] ^ d[1], d[1] ^ d[2], d[2] ^ d[0], 7 * 2 + 1 - cols)[step])
    return seat ^ jnp.where(first == 0, masks[0], masks[1])


def slice_kernel(p_ids, q_ids, q_ref, out_ref):
    blocks, per_q, extent, _ = q_ref.shape
    per_p = p_ids.shape[0]
    strip = extent // SEATS
    rows = per_q * strip
    lane = lax.broadcasted_iota(jnp.int32, (2 * SUB, extent), 1)
    ids = jnp.zeros((2 * SUB, extent), jnp.int32)
    for f in range(blocks):
        for k in range(per_p + per_q):
            value = p_ids[k, f] if k < per_p else q_ids[f, k - per_p]
            ids = jnp.where(lane == f * (per_p + per_q) + k, value, ids)
    ids = ids.astype(out_ref.dtype)
    for f in range(blocks):
        flipped = [q_ref[f, k].astype(jnp.float32).T for k in range(per_q)]
        for j in range(SEATS):
            pieces = [tile[j * strip:(j + 1) * strip] for tile in flipped]
            out_ref[j, f * rows:(f + 1) * rows] = jnp.concatenate(pieces, axis=0).astype(out_ref.dtype)
    for j in range(SEATS):
        out_ref[j, blocks * rows:] = ids


def product_kernel(tile_count, cols, routes, first, coded, q_ref, *rest):
    count = len(routes)
    p_refs, (out_ref, wide_ids, ids, id_sem, *sums) = rest[:count], rest[count + (not first):]
    acc_ref = sums[0] if coded else out_ref
    blocks, per_p, extent, _ = p_refs[0].shape
    strip = acc_ref.shape[1]
    rows = (q_ref.shape[1] - 2 * SUB) // blocks
    per_q = rows // strip
    for s in range(SEATS):
        wide_ids[s:s + 1] = q_ref[s, blocks * rows:, :].astype(jnp.int32)[:1]
    id_copy = pltpu.make_async_copy(wide_ids, ids, id_sem)
    id_copy.start()
    if first:
        acc_ref[...] = jnp.zeros_like(acc_ref)
    else:
        acc_ref[...] = rest[count][...]
    here = lax.axis_index(("pair", "core", "col"))
    id_copy.wait()
    for i in range(count):
        seat = origin(*routes[i], here, cols)
        for f in range(blocks):
            left = q_ref[seat, f * rows:(f + 1) * rows]
            start = f * (per_p + per_q)
            for k in range(per_p):
                product = jnp.dot(left, p_refs[i][f, k], preferred_element_type=jnp.float32)
                base = ids[seat, start + k] * tile_count
                for l in range(per_q):
                    spot = base + ids[seat, start + per_p + l]
                    acc_ref[spot] += product[l * strip:(l + 1) * strip]
    if coded:
        code(acc_ref, out_ref, tile_count // cols)


def add_products(q_here, sets, routes, acc, tile_count, cols, coded=False):
    per_p, extent = sets[0].shape[1:3]
    rows = q_here.shape[1] - 2 * SUB
    sums = jax.ShapeDtypeStruct((tile_count * tile_count, extent // SEATS, extent), jnp.float32)
    made = sums
    if coded:
        shape = (tile_count * cols, tile_count // cols // 2 + 1) + sums.shape[1:]
        made = jax.ShapeDtypeStruct(shape, jnp.int32)
    operands = [q_here, *sets] + ([] if acc is None else [acc])
    return pl.pallas_call(
        functools.partial(product_kernel, tile_count, cols, routes, acc is None, coded),
        out_shape=made,
        in_specs=[pl.BlockSpec(memory_space=pltpu.VMEM)] * len(operands),
        out_specs=pl.BlockSpec(memory_space=pltpu.VMEM),
        scratch_shapes=[
            pltpu.VMEM((SEATS, extent), jnp.int32),
            pltpu.SMEM((SEATS, extent), jnp.int32),
            pltpu.SemaphoreType.DMA,
        ]
        + [pltpu.VMEM(sums.shape, sums.dtype)] * coded,
        input_output_aliases={} if acc is None or coded else {len(operands) - 1: 0},
        cost_estimate=pl.CostEstimate(
            flops=2 * len(sets) * per_p * rows * extent * extent,
            bytes_accessed=len(sets) * (1 << 20),
            transcendentals=0,
        ),
        compiler_params=pltpu.CompilerParams(vmem_limit_bytes=24 << 20),
        name="products",
    )(*operands)


def code(acc_ref, out_ref, tiles):
    extra = 24 // tiles
    half = 1 << (15 + extra)
    for d in range(out_ref.shape[0]):
        values = [acc_ref[d * tiles + t] for t in range(tiles)]
        left = functools.reduce(jnp.maximum, [jnp.abs(value) for value in values]) * 2.0**FLOOR
        scale = jnp.full(left.shape, 2.0 ** (FLOOR - 1) * half, jnp.float32)
        last = jnp.zeros(left.shape, jnp.int32)
        for i in reversed(range(7)):
            big = left >= 2.0 ** (1 << i)
            down = jnp.where(big, 2.0 ** -(1 << i), 1.0)
            left, scale = left * down, scale * down
            last = jnp.where(big, last + (1 << i), last)
        low = []
        for t, value in enumerate(values):
            whole = jnp.floor(value * scale + 0.5).astype(jnp.int32)
            whole = jnp.minimum(whole, half - 1) + half
            low.append(whole & 0xFFFF)
            last = last | ((whole >> 16) << (8 + extra * t))
        for j in range(tiles // 2):
            out_ref[d, j] = low[2 * j] | (low[2 * j + 1] << 16)
        out_ref[d, tiles // 2] = last


def finish_kernel(x_ref, out_ref):
    planes, seats, words, strip, extent = x_ref.shape
    tiles = 2 * (words - 1)
    extra = 24 // tiles
    half = 1 << (15 + extra)
    wholes = [None] * tiles
    for z in range(planes):
        last = x_ref[z, :, words - 1]
        scale = jnp.full(last.shape, 2.0 ** (1 - FLOOR) / half, jnp.float32)
        for i in range(7):
            scale = scale * jnp.where((last >> i) & 1 == 1, 2.0 ** (1 << i), 1.0)
        for t in range(tiles):
            whole = (x_ref[z, :, t // 2] >> (16 * (t % 2))) & 0xFFFF
            whole = whole | (((last >> (8 + extra * t)) & ((1 << extra) - 1)) << 16)
            value = (whole - half).astype(jnp.float32) * scale
            wholes[t] = value if z == 0 else wholes[t] + value
    for t in range(tiles):
        out_ref[:, t * extent:(t + 1) * extent] = wholes[t].reshape(seats * strip, extent).T


def body(p_tiles, p_cols, q_tiles, q_cols):
    blocks, per_p, extent, _ = p_tiles.shape
    per_q = q_tiles.shape[1]
    planes, cols = lax.axis_size("plane"), lax.axis_size("col")
    tile_count = planes * SEATS // cols
    strip = extent // SEATS
    height = blocks * per_q * strip + 2 * SUB
    seat = ("pair", "core", "col")

    sliced = pl.pallas_call(
        slice_kernel,
        out_shape=jax.ShapeDtypeStruct((SEATS, height, extent), q_tiles.dtype),
        in_specs=[pl.BlockSpec(memory_space=pltpu.SMEM)] * 2 + [pl.BlockSpec(memory_space=pltpu.VMEM)],
        cost_estimate=pl.CostEstimate(flops=0, bytes_accessed=8 << 20, transcendentals=0),
        name="cut_columns",
    )(p_cols.T, q_cols, q_tiles)

    def along(values, step):
        hops = [(s, s ^ axes(s // cols % 2, cols)[step]) for s in range(SEATS)]
        return lax.ppermute(values, seat, hops)

    def across(values):
        return lax.ppermute(values, seat, [(s, s ^ cols) for s in range(SEATS)])

    def add(acc, sets, routes, coded=False):
        return add_products(q_here, sets, routes, acc, tile_count, cols, coded)

    first = [along(p_tiles, step) for step in range(3)]
    sliced, *first = lax.optimization_barrier((sliced, *first))
    q_here = lax.all_to_all(sliced, seat, split_axis=0, concat_axis=0, tiled=True)
    second = [along(first[step], (step + 1) % 3) for step in range(3)]
    crossed = [across(each) for each in [p_tiles] + first]
    q_here, second, crossed = lax.optimization_barrier((q_here, second, crossed))
    third = along(second[0], 2)
    acc = add(
        None,
        [p_tiles] + first + crossed,
        [(step, swapped) for swapped in (0, 1) for step in range(4)],
    )
    third, acc = lax.optimization_barrier((third, acc))
    sets = second + [across(each) for each in second]
    acc = add(acc, sets, [(step, swapped) for swapped in (0, 1) for step in (4, 5, 6)])
    coded = add(acc, [third, across(third)], [(7, 0), (7, 1)], coded=True)
    every = ("plane",) + seat
    tiles = tile_count // cols
    landed = lax.all_to_all(coded, every, split_axis=0, concat_axis=0, tiled=True)
    return pl.pallas_call(
        finish_kernel,
        out_shape=jax.ShapeDtypeStruct((extent, tiles * extent), jnp.float32),
        compiler_params=pltpu.CompilerParams(vmem_limit_bytes=16 << 20),
        name="turn",
    )(landed.reshape((planes, SEATS) + landed.shape[1:]))


def solution(mesh):
    rows, cols = mesh.devices.shape
    pairs = SEATS // (2 * cols)
    shape = (rows // (2 * pairs), pairs, 2, cols)
    every = ("plane", "pair", "core", "col")
    inner = Mesh(mesh.devices.reshape(shape), every)
    placed = (
        P(every, None, None, None),
        P(every, None),
        P(every, None, None, None),
        P(every, None),
    )
    return jax.shard_map(
        body, mesh=inner, in_specs=placed, out_specs=P(every[:3], "col"), check_vma=False
    )
```

```python
import functools

import jax
import jax.numpy as jnp
from jax import lax
from jax.experimental import pallas as pl
from jax.experimental.pallas import tpu as pltpu
from jax.sharding import Mesh
from jax.sharding import PartitionSpec as P

SEATS = 16
SUB = 8
FLOOR = 100


def axes(core, cols):
    bits = [bit for bit in (1, 2, 4, 8) if bit != cols]
    return bits[core:] + bits[:core]


def origin(step, swapped, seat, cols):
    first = lax.rem(seat // cols, 2)
    if swapped:
        seat, first = seat ^ cols, 1 - first
    masks = []
    for core in range(2):
        d = axes(core, cols)
        masks.append((0, d[0], d[1], d[2], d[0] ^ d[1], d[1] ^ d[2], d[2] ^ d[0], 7 * 2 + 1 - cols)[step])
    return seat ^ jnp.where(first == 0, masks[0], masks[1])


def slice_kernel(p_ids, q_ids, q_ref, out_ref):
    blocks, per_q, extent, _ = q_ref.shape
    per_p = p_ids.shape[0]
    strip = extent // SEATS
    rows = per_q * strip
    lane = lax.broadcasted_iota(jnp.int32, (2 * SUB, extent), 1)
    ids = jnp.zeros((2 * SUB, extent), jnp.int32)
    for f in range(blocks):
        for k in range(per_p + per_q):
            value = p_ids[k, f] if k < per_p else q_ids[f, k - per_p]
            ids = jnp.where(lane == f * (per_p + per_q) + k, value, ids)
    ids = ids.astype(out_ref.dtype)
    for f in range(blocks):
        flipped = [q_ref[f, k].astype(jnp.float32).T for k in range(per_q)]
        for j in range(SEATS):
            pieces = [tile[j * strip:(j + 1) * strip] for tile in flipped]
            out_ref[j, f * rows:(f + 1) * rows] = jnp.concatenate(pieces, axis=0).astype(out_ref.dtype)
    for j in range(SEATS):
        out_ref[j, blocks * rows:] = ids


def start_kernel(*refs):
    refs[-1][...] = jnp.zeros_like(refs[-1])


def start_sums(after, shape):
    return pl.pallas_call(
        start_kernel,
        out_shape=jax.ShapeDtypeStruct(shape, jnp.float32),
        in_specs=[pl.BlockSpec(memory_space=pl.ANY)] * len(after),
        out_specs=pl.BlockSpec(memory_space=pltpu.VMEM),
        cost_estimate=pl.CostEstimate(flops=0, bytes_accessed=256 << 20, transcendentals=0),
        compiler_params=pltpu.CompilerParams(vmem_limit_bytes=4 << 20),
        name="start_sums",
    )(*after)


def product_kernel(tile_count, cols, routes, coded, q_ref, *rest):
    count = len(routes)
    p_refs, (out_ref, wide_ids, ids, id_sem, *sums) = rest[:count], rest[count + 1:]
    acc_ref = sums[0] if coded else out_ref
    blocks, per_p, extent, _ = p_refs[0].shape
    strip = acc_ref.shape[1]
    rows = (q_ref.shape[1] - 2 * SUB) // blocks
    per_q = rows // strip
    for s in range(SEATS):
        wide_ids[s:s + 1] = q_ref[s, blocks * rows:, :].astype(jnp.int32)[:1]
    id_copy = pltpu.make_async_copy(wide_ids, ids, id_sem)
    id_copy.start()
    acc_ref[...] = rest[count][...]
    here = lax.axis_index(("pair", "core", "col"))
    id_copy.wait()
    for i in range(count):
        seat = origin(*routes[i], here, cols)
        for f in range(blocks):
            left = q_ref[seat, f * rows:(f + 1) * rows]
            start = f * (per_p + per_q)
            for k in range(per_p):
                product = jnp.dot(left, p_refs[i][f, k], preferred_element_type=jnp.float32)
                base = ids[seat, start + k] * tile_count
                for l in range(per_q):
                    spot = base + ids[seat, start + per_p + l]
                    acc_ref[spot] += product[l * strip:(l + 1) * strip]
    if coded:
        code(acc_ref, out_ref, tile_count // cols)


def add_products(q_here, sets, routes, acc, tile_count, cols, coded=False):
    per_p, extent = sets[0].shape[1:3]
    rows = q_here.shape[1] - 2 * SUB
    sums = jax.ShapeDtypeStruct((tile_count * tile_count, extent // SEATS, extent), jnp.float32)
    made = sums
    if coded:
        shape = (tile_count * cols, tile_count // cols // 2 + 1) + sums.shape[1:]
        made = jax.ShapeDtypeStruct(shape, jnp.int32)
    operands = [q_here, *sets, acc]
    return pl.pallas_call(
        functools.partial(product_kernel, tile_count, cols, routes, coded),
        out_shape=made,
        in_specs=[pl.BlockSpec(memory_space=pltpu.VMEM)] * len(operands),
        out_specs=pl.BlockSpec(memory_space=pltpu.VMEM),
        scratch_shapes=[
            pltpu.VMEM((SEATS, extent), jnp.int32),
            pltpu.SMEM((SEATS, extent), jnp.int32),
            pltpu.SemaphoreType.DMA,
        ]
        + [pltpu.VMEM(sums.shape, sums.dtype)] * coded,
        input_output_aliases={} if coded else {len(operands) - 1: 0},
        cost_estimate=pl.CostEstimate(
            flops=2 * len(sets) * per_p * rows * extent * extent,
            bytes_accessed=len(sets) * (1 << 18),
            transcendentals=0,
        ),
        compiler_params=pltpu.CompilerParams(vmem_limit_bytes=24 << 20),
        name="products",
    )(*operands)


def code(acc_ref, out_ref, tiles):
    extra = 24 // tiles
    half = 1 << (15 + extra)
    for d in range(out_ref.shape[0]):
        values = [acc_ref[d * tiles + t] for t in range(tiles)]
        left = functools.reduce(jnp.maximum, [jnp.abs(value) for value in values]) * 2.0**FLOOR
        scale = jnp.full(left.shape, 2.0 ** (FLOOR - 1) * half, jnp.float32)
        last = jnp.zeros(left.shape, jnp.int32)
        for i in reversed(range(7)):
            big = left >= 2.0 ** (1 << i)
            down = jnp.where(big, 2.0 ** -(1 << i), 1.0)
            left, scale = left * down, scale * down
            last = jnp.where(big, last + (1 << i), last)
        low = []
        for t, value in enumerate(values):
            whole = jnp.floor(value * scale + 0.5).astype(jnp.int32)
            whole = jnp.minimum(whole, half - 1) + half
            low.append(whole & 0xFFFF)
            last = last | ((whole >> 16) << (8 + extra * t))
        for j in range(tiles // 2):
            out_ref[d, j] = low[2 * j] | (low[2 * j + 1] << 16)
        out_ref[d, tiles // 2] = last


def finish_kernel(x_ref, out_ref):
    planes, seats, words, strip, extent = x_ref.shape
    tiles = 2 * (words - 1)
    extra = 24 // tiles
    half = 1 << (15 + extra)
    wholes = [None] * tiles
    for z in range(planes):
        last = x_ref[z, :, words - 1]
        scale = jnp.full(last.shape, 2.0 ** (1 - FLOOR) / half, jnp.float32)
        for i in range(7):
            scale = scale * jnp.where((last >> i) & 1 == 1, 2.0 ** (1 << i), 1.0)
        for t in range(tiles):
            whole = (x_ref[z, :, t // 2] >> (16 * (t % 2))) & 0xFFFF
            whole = whole | (((last >> (8 + extra * t)) & ((1 << extra) - 1)) << 16)
            value = (whole - half).astype(jnp.float32) * scale
            wholes[t] = value if z == 0 else wholes[t] + value
    for t in range(tiles):
        out_ref[:, t * extent:(t + 1) * extent] = wholes[t].reshape(seats * strip, extent).T


def body(p_tiles, p_cols, q_tiles, q_cols):
    blocks, per_p, extent, _ = p_tiles.shape
    per_q = q_tiles.shape[1]
    planes, cols = lax.axis_size("plane"), lax.axis_size("col")
    tile_count = planes * SEATS // cols
    strip = extent // SEATS
    height = blocks * per_q * strip + 2 * SUB
    seat = ("pair", "core", "col")

    sliced = pl.pallas_call(
        slice_kernel,
        out_shape=jax.ShapeDtypeStruct((SEATS, height, extent), q_tiles.dtype),
        in_specs=[pl.BlockSpec(memory_space=pltpu.SMEM)] * 2 + [pl.BlockSpec(memory_space=pltpu.VMEM)],
        cost_estimate=pl.CostEstimate(flops=0, bytes_accessed=8 << 20, transcendentals=0),
        name="cut_columns",
    )(p_cols.T, q_cols, q_tiles)

    def along(values, step):
        hops = [(s, s ^ axes(s // cols % 2, cols)[step]) for s in range(SEATS)]
        return lax.ppermute(values, seat, hops)

    def across(values):
        return lax.ppermute(values, seat, [(s, s ^ cols) for s in range(SEATS)])

    def add(acc, sets, routes, coded=False):
        return add_products(q_here, sets, routes, acc, tile_count, cols, coded)

    first = [along(p_tiles, step) for step in range(3)]
    sliced, first = lax.optimization_barrier((sliced, first))
    second = [along(first[step], (step + 1) % 3) for step in range(3)]
    crossed = [across(each) for each in [p_tiles] + first]
    q_here = lax.all_to_all(sliced, seat, split_axis=0, concat_axis=0, tiled=True)
    acc = start_sums(second, (tile_count * tile_count, strip, extent))
    third = along(second[0], 2)
    q_here, second, acc = lax.optimization_barrier((q_here, second, acc))
    acc = add(
        acc,
        [p_tiles] + first + crossed,
        [(step, swapped) for swapped in (0, 1) for step in range(4)],
    )
    third, acc = lax.optimization_barrier((third, acc))
    sets = second + [across(each) for each in second]
    acc = add(acc, sets, [(step, swapped) for swapped in (0, 1) for step in (4, 5, 6)])
    coded = add(acc, [third, across(third)], [(7, 0), (7, 1)], coded=True)
    every = ("plane",) + seat
    tiles = tile_count // cols
    landed = lax.all_to_all(coded, every, split_axis=0, concat_axis=0, tiled=True)
    return pl.pallas_call(
        finish_kernel,
        out_shape=jax.ShapeDtypeStruct((extent, tiles * extent), jnp.float32),
        compiler_params=pltpu.CompilerParams(vmem_limit_bytes=16 << 20),
        name="turn",
    )(landed.reshape((planes, SEATS) + landed.shape[1:]))


def solution(mesh):
    rows, cols = mesh.devices.shape
    pairs = SEATS // (2 * cols)
    shape = (rows // (2 * pairs), pairs, 2, cols)
    every = ("plane", "pair", "core", "col")
    inner = Mesh(mesh.devices.reshape(shape), every)
    placed = (
        P(every, None, None, None),
        P(every, None),
        P(every, None, None, None),
        P(every, None),
    )
    return jax.shard_map(
        body, mesh=inner, in_specs=placed, out_specs=P(every[:3], "col"), check_vma=False
    )
```

```python
import functools

import jax
import jax.numpy as jnp
from jax import lax
from jax.experimental import pallas as pl
from jax.experimental.pallas import tpu as pltpu
from jax.sharding import Mesh
from jax.sharding import PartitionSpec as P

SEATS = 16
SUB = 8
FLOOR = 100


def axes(core, cols):
    bits = [bit for bit in (1, 2, 4, 8) if bit != cols]
    return bits[core:] + bits[:core]


def origin(step, swapped, seat, cols):
    first = lax.rem(seat // cols, 2)
    if swapped:
        seat, first = seat ^ cols, 1 - first
    masks = []
    for core in range(2):
        d = axes(core, cols)
        masks.append((0, d[0], d[1], d[2], d[0] ^ d[1], d[1] ^ d[2], d[2] ^ d[0], 7 * 2 + 1 - cols)[step])
    return seat ^ jnp.where(first == 0, masks[0], masks[1])


def slice_kernel(p_ids, q_ids, q_ref, out_ref):
    blocks, per_q, extent, _ = q_ref.shape
    per_p = p_ids.shape[0]
    strip = extent // SEATS
    rows = per_q * strip
    lane = lax.broadcasted_iota(jnp.int32, (2 * SUB, extent), 1)
    ids = jnp.zeros((2 * SUB, extent), jnp.int32)
    for f in range(blocks):
        for k in range(per_p + per_q):
            value = p_ids[k, f] if k < per_p else q_ids[f, k - per_p]
            ids = jnp.where(lane == f * (per_p + per_q) + k, value, ids)
    ids = ids.astype(out_ref.dtype)
    for f in range(blocks):
        flipped = [q_ref[f, k].astype(jnp.float32).T for k in range(per_q)]
        for j in range(SEATS):
            pieces = [tile[j * strip:(j + 1) * strip] for tile in flipped]
            out_ref[j, f * rows:(f + 1) * rows] = jnp.concatenate(pieces, axis=0).astype(out_ref.dtype)
    for j in range(SEATS):
        out_ref[j, blocks * rows:] = ids


def product_kernel(tile_count, cols, routes, first, coded, q_ref, *rest):
    count = len(routes)
    p_refs, (out_ref, wide_ids, ids, id_sem, *sums) = rest[:count], rest[count + (not first):]
    acc_ref = sums[0] if coded else out_ref
    blocks, per_p, extent, _ = p_refs[0].shape
    strip = acc_ref.shape[1]
    rows = (q_ref.shape[1] - 2 * SUB) // blocks
    per_q = rows // strip
    for s in range(SEATS):
        wide_ids[s:s + 1] = q_ref[s, blocks * rows:, :].astype(jnp.int32)[:1]
    id_copy = pltpu.make_async_copy(wide_ids, ids, id_sem)
    id_copy.start()
    if first:
        acc_ref[...] = jnp.zeros_like(acc_ref)
    else:
        acc_ref[...] = rest[count][...]
    here = lax.axis_index(("pair", "core", "col"))
    id_copy.wait()
    for i in range(count):
        seat = origin(*routes[i], here, cols)
        for f in range(blocks):
            left = q_ref[seat, f * rows:(f + 1) * rows]
            start = f * (per_p + per_q)
            for k in range(per_p):
                product = jnp.dot(left, p_refs[i][f, k], preferred_element_type=jnp.float32)
                base = ids[seat, start + k] * tile_count
                for l in range(per_q):
                    spot = base + ids[seat, start + per_p + l]
                    acc_ref[spot] += product[l * strip:(l + 1) * strip]
    if coded:
        code(acc_ref, out_ref, tile_count // cols)


def add_products(q_here, sets, routes, acc, tile_count, cols, coded=False):
    per_p, extent = sets[0].shape[1:3]
    rows = q_here.shape[1] - 2 * SUB
    sums = jax.ShapeDtypeStruct((tile_count * tile_count, extent // SEATS, extent), jnp.float32)
    made = sums
    if coded:
        shape = (tile_count * cols, tile_count // cols // 2 + 1) + sums.shape[1:]
        made = jax.ShapeDtypeStruct(shape, jnp.int32)
    operands = [q_here, *sets] + ([] if acc is None else [acc])
    return pl.pallas_call(
        functools.partial(product_kernel, tile_count, cols, routes, acc is None, coded),
        out_shape=made,
        in_specs=[pl.BlockSpec(memory_space=pltpu.VMEM)] * len(operands),
        out_specs=pl.BlockSpec(memory_space=pltpu.VMEM),
        scratch_shapes=[
            pltpu.VMEM((SEATS, extent), jnp.int32),
            pltpu.SMEM((SEATS, extent), jnp.int32),
            pltpu.SemaphoreType.DMA,
        ]
        + [pltpu.VMEM(sums.shape, sums.dtype)] * coded,
        input_output_aliases={} if acc is None or coded else {len(operands) - 1: 0},
        cost_estimate=pl.CostEstimate(
            flops=2 * len(sets) * per_p * rows * extent * extent,
            bytes_accessed=len(sets) * (1 << 18),
            transcendentals=0,
        ),
        compiler_params=pltpu.CompilerParams(vmem_limit_bytes=24 << 20),
        name="products",
    )(*operands)


def code(acc_ref, out_ref, tiles):
    extra = 24 // tiles
    half = 1 << (15 + extra)
    for d in range(out_ref.shape[0]):
        values = [acc_ref[d * tiles + t] for t in range(tiles)]
        left = functools.reduce(jnp.maximum, [jnp.abs(value) for value in values]) * 2.0**FLOOR
        scale = jnp.full(left.shape, 2.0 ** (FLOOR - 1) * half, jnp.float32)
        last = jnp.zeros(left.shape, jnp.int32)
        for i in reversed(range(7)):
            big = left >= 2.0 ** (1 << i)
            down = jnp.where(big, 2.0 ** -(1 << i), 1.0)
            left, scale = left * down, scale * down
            last = jnp.where(big, last + (1 << i), last)
        low = []
        for t, value in enumerate(values):
            whole = jnp.floor(value * scale + 0.5).astype(jnp.int32)
            whole = jnp.minimum(whole, half - 1) + half
            low.append(whole & 0xFFFF)
            last = last | ((whole >> 16) << (8 + extra * t))
        for j in range(tiles // 2):
            out_ref[d, j] = low[2 * j] | (low[2 * j + 1] << 16)
        out_ref[d, tiles // 2] = last


def finish_kernel(x_ref, out_ref):
    planes, seats, words, strip, extent = x_ref.shape
    tiles = 2 * (words - 1)
    extra = 24 // tiles
    half = 1 << (15 + extra)
    wholes = [None] * tiles
    for z in range(planes):
        last = x_ref[z, :, words - 1]
        scale = jnp.full(last.shape, 2.0 ** (1 - FLOOR) / half, jnp.float32)
        for i in range(7):
            scale = scale * jnp.where((last >> i) & 1 == 1, 2.0 ** (1 << i), 1.0)
        for t in range(tiles):
            whole = (x_ref[z, :, t // 2] >> (16 * (t % 2))) & 0xFFFF
            whole = whole | (((last >> (8 + extra * t)) & ((1 << extra) - 1)) << 16)
            value = (whole - half).astype(jnp.float32) * scale
            wholes[t] = value if z == 0 else wholes[t] + value
    for t in range(tiles):
        out_ref[:, t * extent:(t + 1) * extent] = wholes[t].reshape(seats * strip, extent).T


def body(p_tiles, p_cols, q_tiles, q_cols):
    blocks, per_p, extent, _ = p_tiles.shape
    per_q = q_tiles.shape[1]
    planes, cols = lax.axis_size("plane"), lax.axis_size("col")
    tile_count = planes * SEATS // cols
    strip = extent // SEATS
    height = blocks * per_q * strip + 2 * SUB
    seat = ("pair", "core", "col")

    sliced = pl.pallas_call(
        slice_kernel,
        out_shape=jax.ShapeDtypeStruct((SEATS, height, extent), q_tiles.dtype),
        in_specs=[pl.BlockSpec(memory_space=pltpu.SMEM)] * 2 + [pl.BlockSpec(memory_space=pltpu.VMEM)],
        cost_estimate=pl.CostEstimate(flops=0, bytes_accessed=8 << 20, transcendentals=0),
        name="cut_columns",
    )(p_cols.T, q_cols, q_tiles)

    def along(values, step):
        hops = [(s, s ^ axes(s // cols % 2, cols)[step]) for s in range(SEATS)]
        return lax.ppermute(values, seat, hops)

    def across(values):
        return lax.ppermute(values, seat, [(s, s ^ cols) for s in range(SEATS)])

    def add(acc, sets, routes, coded=False):
        return add_products(q_here, sets, routes, acc, tile_count, cols, coded)

    first = [along(p_tiles, step) for step in range(3)]
    sliced, first = lax.optimization_barrier((sliced, first))
    second = [along(first[step], (step + 1) % 3) for step in range(3)]
    sliced, second = lax.optimization_barrier((sliced, second))
    third = along(second[0], 2)
    crossed = [across(each) for each in [p_tiles] + first]
    q_here = lax.all_to_all(sliced, seat, split_axis=0, concat_axis=0, tiled=True)
    q_here, second = lax.optimization_barrier((q_here, second))
    acc = add(
        None,
        [p_tiles] + first + crossed,
        [(step, swapped) for swapped in (0, 1) for step in range(4)],
    )
    third, acc = lax.optimization_barrier((third, acc))
    sets = second + [across(each) for each in second]
    acc = add(acc, sets, [(step, swapped) for swapped in (0, 1) for step in (4, 5, 6)])
    coded = add(acc, [third, across(third)], [(7, 0), (7, 1)], coded=True)
    every = ("plane",) + seat
    tiles = tile_count // cols
    landed = lax.all_to_all(coded, every, split_axis=0, concat_axis=0, tiled=True)
    return pl.pallas_call(
        finish_kernel,
        out_shape=jax.ShapeDtypeStruct((extent, tiles * extent), jnp.float32),
        compiler_params=pltpu.CompilerParams(vmem_limit_bytes=16 << 20),
        name="turn",
    )(landed.reshape((planes, SEATS) + landed.shape[1:]))


def solution(mesh):
    rows, cols = mesh.devices.shape
    pairs = SEATS // (2 * cols)
    shape = (rows // (2 * pairs), pairs, 2, cols)
    every = ("plane", "pair", "core", "col")
    inner = Mesh(mesh.devices.reshape(shape), every)
    placed = (
        P(every, None, None, None),
        P(every, None),
        P(every, None, None, None),
        P(every, None),
    )
    return jax.shard_map(
        body, mesh=inner, in_specs=placed, out_specs=P(every[:3], "col"), check_vma=False
    )
```

```python
import functools

import jax
import jax.numpy as jnp
from jax import lax
from jax.experimental import pallas as pl
from jax.experimental.pallas import tpu as pltpu
from jax.sharding import Mesh
from jax.sharding import PartitionSpec as P

SEATS = 16
SUB = 8
FLOOR = 100


def axes(core, cols):
    bits = [bit for bit in (1, 2, 4, 8) if bit != cols]
    return bits[core:] + bits[:core]


def origin(step, swapped, seat, cols):
    first = lax.rem(seat // cols, 2)
    if swapped:
        seat, first = seat ^ cols, 1 - first
    masks = []
    for core in range(2):
        d = axes(core, cols)
        masks.append((0, d[0], d[1], d[2], d[0] ^ d[1], d[1] ^ d[2], d[2] ^ d[0], 7 * 2 + 1 - cols)[step])
    return seat ^ jnp.where(first == 0, masks[0], masks[1])


def slice_kernel(p_ids, q_ids, q_ref, out_ref):
    blocks, per_q, extent, _ = q_ref.shape
    per_p = p_ids.shape[0]
    strip = extent // SEATS
    rows = per_q * strip
    lane = lax.broadcasted_iota(jnp.int32, (2 * SUB, extent), 1)
    ids = jnp.zeros((2 * SUB, extent), jnp.int32)
    for f in range(blocks):
        for k in range(per_p + per_q):
            value = p_ids[k, f] if k < per_p else q_ids[f, k - per_p]
            ids = jnp.where(lane == f * (per_p + per_q) + k, value, ids)
    ids = ids.astype(out_ref.dtype)
    for f in range(blocks):
        flipped = [q_ref[f, k].astype(jnp.float32).T for k in range(per_q)]
        for j in range(SEATS):
            pieces = [tile[j * strip:(j + 1) * strip] for tile in flipped]
            out_ref[j, f * rows:(f + 1) * rows] = jnp.concatenate(pieces, axis=0).astype(out_ref.dtype)
    for j in range(SEATS):
        out_ref[j, blocks * rows:] = ids


def product_kernel(tile_count, cols, routes, first, coded, q_ref, *rest):
    count = len(routes)
    p_refs, (out_ref, wide_ids, ids, id_sem, *sums) = rest[:count], rest[count + (not first):]
    acc_ref = sums[0] if coded else out_ref
    blocks, per_p, extent, _ = p_refs[0].shape
    strip = acc_ref.shape[1]
    rows = (q_ref.shape[1] - 2 * SUB) // blocks
    per_q = rows // strip
    for s in range(SEATS):
        wide_ids[s:s + 1] = q_ref[s, blocks * rows:, :].astype(jnp.int32)[:1]
    id_copy = pltpu.make_async_copy(wide_ids, ids, id_sem)
    id_copy.start()
    if first:
        acc_ref[...] = jnp.zeros_like(acc_ref)
    else:
        acc_ref[...] = rest[count][...]
    here = lax.axis_index(("pair", "core", "col"))
    id_copy.wait()
    for i in range(count):
        seat = origin(*routes[i], here, cols)
        for f in range(blocks):
            left = q_ref[seat, f * rows:(f + 1) * rows]
            start = f * (per_p + per_q)
            right = jnp.concatenate([p_refs[i][f, k] for k in range(per_p)], axis=1)
            product = jnp.dot(left, right, preferred_element_type=jnp.float32)
            for k in range(per_p):
                base = ids[seat, start + k] * tile_count
                for l in range(per_q):
                    spot = base + ids[seat, start + per_p + l]
                    acc_ref[spot] += product[l * strip:(l + 1) * strip, k * extent:(k + 1) * extent]
    if coded:
        code(acc_ref, out_ref, tile_count // cols)


def add_products(q_here, sets, routes, acc, tile_count, cols, coded=False):
    per_p, extent = sets[0].shape[1:3]
    rows = q_here.shape[1] - 2 * SUB
    sums = jax.ShapeDtypeStruct((tile_count * tile_count, extent // SEATS, extent), jnp.float32)
    made = sums
    if coded:
        shape = (tile_count * cols, tile_count // cols // 2 + 1) + sums.shape[1:]
        made = jax.ShapeDtypeStruct(shape, jnp.int32)
    operands = [q_here, *sets] + ([] if acc is None else [acc])
    return pl.pallas_call(
        functools.partial(product_kernel, tile_count, cols, routes, acc is None, coded),
        out_shape=made,
        in_specs=[pl.BlockSpec(memory_space=pltpu.VMEM)] * len(operands),
        out_specs=pl.BlockSpec(memory_space=pltpu.VMEM),
        scratch_shapes=[
            pltpu.VMEM((SEATS, extent), jnp.int32),
            pltpu.SMEM((SEATS, extent), jnp.int32),
            pltpu.SemaphoreType.DMA,
        ]
        + [pltpu.VMEM(sums.shape, sums.dtype)] * coded,
        input_output_aliases={} if acc is None or coded else {len(operands) - 1: 0},
        cost_estimate=pl.CostEstimate(
            flops=2 * len(sets) * per_p * rows * extent * extent,
            bytes_accessed=len(sets) * (1 << 18),
            transcendentals=0,
        ),
        compiler_params=pltpu.CompilerParams(vmem_limit_bytes=24 << 20),
        name="products",
    )(*operands)


def code(acc_ref, out_ref, tiles):
    extra = 24 // tiles
    half = 1 << (15 + extra)
    for d in range(out_ref.shape[0]):
        values = [acc_ref[d * tiles + t] for t in range(tiles)]
        left = functools.reduce(jnp.maximum, [jnp.abs(value) for value in values]) * 2.0**FLOOR
        scale = jnp.full(left.shape, 2.0 ** (FLOOR - 1) * half, jnp.float32)
        last = jnp.zeros(left.shape, jnp.int32)
        for i in reversed(range(7)):
            big = left >= 2.0 ** (1 << i)
            down = jnp.where(big, 2.0 ** -(1 << i), 1.0)
            left, scale = left * down, scale * down
            last = jnp.where(big, last + (1 << i), last)
        low = []
        for t, value in enumerate(values):
            whole = jnp.floor(value * scale + 0.5).astype(jnp.int32)
            whole = jnp.minimum(whole, half - 1) + half
            low.append(whole & 0xFFFF)
            last = last | ((whole >> 16) << (8 + extra * t))
        for j in range(tiles // 2):
            out_ref[d, j] = low[2 * j] | (low[2 * j + 1] << 16)
        out_ref[d, tiles // 2] = last


def finish_kernel(x_ref, out_ref):
    planes, seats, words, strip, extent = x_ref.shape
    tiles = 2 * (words - 1)
    extra = 24 // tiles
    half = 1 << (15 + extra)
    wholes = [None] * tiles
    for z in range(planes):
        last = x_ref[z, :, words - 1]
        scale = jnp.full(last.shape, 2.0 ** (1 - FLOOR) / half, jnp.float32)
        for i in range(7):
            scale = scale * jnp.where((last >> i) & 1 == 1, 2.0 ** (1 << i), 1.0)
        for t in range(tiles):
            whole = (x_ref[z, :, t // 2] >> (16 * (t % 2))) & 0xFFFF
            whole = whole | (((last >> (8 + extra * t)) & ((1 << extra) - 1)) << 16)
            value = (whole - half).astype(jnp.float32) * scale
            wholes[t] = value if z == 0 else wholes[t] + value
    for t in range(tiles):
        out_ref[:, t * extent:(t + 1) * extent] = wholes[t].reshape(seats * strip, extent).T


def body(p_tiles, p_cols, q_tiles, q_cols):
    blocks, per_p, extent, _ = p_tiles.shape
    per_q = q_tiles.shape[1]
    planes, cols = lax.axis_size("plane"), lax.axis_size("col")
    tile_count = planes * SEATS // cols
    strip = extent // SEATS
    height = blocks * per_q * strip + 2 * SUB
    seat = ("pair", "core", "col")

    sliced = pl.pallas_call(
        slice_kernel,
        out_shape=jax.ShapeDtypeStruct((SEATS, height, extent), q_tiles.dtype),
        in_specs=[pl.BlockSpec(memory_space=pltpu.SMEM)] * 2 + [pl.BlockSpec(memory_space=pltpu.VMEM)],
        cost_estimate=pl.CostEstimate(flops=0, bytes_accessed=8 << 20, transcendentals=0),
        name="cut_columns",
    )(p_cols.T, q_cols, q_tiles)

    def along(values, step):
        hops = [(s, s ^ axes(s // cols % 2, cols)[step]) for s in range(SEATS)]
        return lax.ppermute(values, seat, hops)

    def across(values):
        return lax.ppermute(values, seat, [(s, s ^ cols) for s in range(SEATS)])

    def add(acc, sets, routes, coded=False):
        return add_products(q_here, sets, routes, acc, tile_count, cols, coded)

    first = [along(p_tiles, step) for step in range(3)]
    sliced, first = lax.optimization_barrier((sliced, first))
    q_here = lax.all_to_all(sliced, seat, split_axis=0, concat_axis=0, tiled=True)
    second = [along(first[step], (step + 1) % 3) for step in range(3)]
    crossed = [across(each) for each in [p_tiles] + first]
    acc = add(
        None, [p_tiles] + first + crossed[:2], [(0, 0), (1, 0), (2, 0), (3, 0), (0, 1), (1, 1)]
    )
    second, acc = lax.optimization_barrier((second, acc))
    third = along(second[0], 2)
    sets = second + crossed[2:] + [across(each) for each in second]
    acc = add(acc, sets, [(4, 0), (5, 0), (6, 0), (2, 1), (3, 1), (4, 1), (5, 1), (6, 1)])
    third, acc = lax.optimization_barrier((third, acc))
    beside = across(third)
    acc = add(acc, [third], [(7, 0)])
    coded = add(acc, [beside], [(7, 1)], coded=True)
    every = ("plane",) + seat
    tiles = tile_count // cols
    landed = lax.all_to_all(coded, every, split_axis=0, concat_axis=0, tiled=True)
    return pl.pallas_call(
        finish_kernel,
        out_shape=jax.ShapeDtypeStruct((extent, tiles * extent), jnp.float32),
        compiler_params=pltpu.CompilerParams(vmem_limit_bytes=16 << 20),
        name="turn",
    )(landed.reshape((planes, SEATS) + landed.shape[1:]))


def solution(mesh):
    rows, cols = mesh.devices.shape
    pairs = SEATS // (2 * cols)
    shape = (rows // (2 * pairs), pairs, 2, cols)
    every = ("plane", "pair", "core", "col")
    inner = Mesh(mesh.devices.reshape(shape), every)
    placed = (
        P(every, None, None, None),
        P(every, None),
        P(every, None, None, None),
        P(every, None),
    )
    return jax.shard_map(
        body, mesh=inner, in_specs=placed, out_specs=P(every[:3], "col"), check_vma=False
    )
```

```python
import functools

import jax
import jax.numpy as jnp
from jax import lax
from jax.experimental import pallas as pl
from jax.experimental.pallas import tpu as pltpu
from jax.sharding import Mesh
from jax.sharding import PartitionSpec as P

SEATS = 16
SUB = 8
FLOOR = 100


def axes(core, cols):
    bits = [bit for bit in (1, 2, 4, 8) if bit != cols]
    return [bits[core], bits[1 - core], bits[2]]


def origin(step, swapped, seat, cols):
    first = lax.rem(seat // cols, 2)
    if swapped:
        seat, first = seat ^ cols, 1 - first
    masks = []
    for core in range(2):
        d = axes(core, cols)
        masks.append((0, d[0], d[1], d[2], d[0] ^ d[1], d[1] ^ d[2], d[2] ^ d[0], 7 * 2 + 1 - cols)[step])
    return seat ^ jnp.where(first == 0, masks[0], masks[1])


def slice_kernel(p_ids, q_ids, q_ref, out_ref):
    blocks, per_q, extent, _ = q_ref.shape
    per_p = p_ids.shape[0]
    strip = extent // SEATS
    rows = per_q * strip
    lane = lax.broadcasted_iota(jnp.int32, (2 * SUB, extent), 1)
    ids = jnp.zeros((2 * SUB, extent), jnp.int32)
    for f in range(blocks):
        for k in range(per_p + per_q):
            value = p_ids[k, f] if k < per_p else q_ids[f, k - per_p]
            ids = jnp.where(lane == f * (per_p + per_q) + k, value, ids)
    ids = ids.astype(out_ref.dtype)
    for f in range(blocks):
        flipped = [q_ref[f, k].astype(jnp.float32).T for k in range(per_q)]
        for j in range(SEATS):
            pieces = [tile[j * strip:(j + 1) * strip] for tile in flipped]
            out_ref[j, f * rows:(f + 1) * rows] = jnp.concatenate(pieces, axis=0).astype(out_ref.dtype)
    for j in range(SEATS):
        out_ref[j, blocks * rows:] = ids


def product_kernel(tile_count, cols, routes, first, coded, q_ref, *rest):
    count = len(routes)
    p_refs, (out_ref, wide_ids, ids, id_sem, *sums) = rest[:count], rest[count + (not first):]
    acc_ref = sums[0] if coded else out_ref
    blocks, per_p, extent, _ = p_refs[0].shape
    strip = acc_ref.shape[1]
    rows = (q_ref.shape[1] - 2 * SUB) // blocks
    per_q = rows // strip
    for s in range(SEATS):
        wide_ids[s:s + 1] = q_ref[s, blocks * rows:, :].astype(jnp.int32)[:1]
    id_copy = pltpu.make_async_copy(wide_ids, ids, id_sem)
    id_copy.start()
    if first:
        acc_ref[...] = jnp.zeros_like(acc_ref)
    else:
        acc_ref[...] = rest[count][...]
    here = lax.axis_index(("pair", "core", "col"))
    id_copy.wait()
    for i in range(count):
        seat = origin(*routes[i], here, cols)
        for f in range(blocks):
            left = q_ref[seat, f * rows:(f + 1) * rows]
            start = f * (per_p + per_q)
            right = jnp.concatenate([p_refs[i][f, k] for k in range(per_p)], axis=1)
            product = jnp.dot(left, right, preferred_element_type=jnp.float32)
            for k in range(per_p):
                base = ids[seat, start + k] * tile_count
                for l in range(per_q):
                    spot = base + ids[seat, start + per_p + l]
                    acc_ref[spot] += product[l * strip:(l + 1) * strip, k * extent:(k + 1) * extent]
    if coded:
        code(acc_ref, out_ref, tile_count // cols)


def add_products(q_here, sets, routes, acc, tile_count, cols, coded=False):
    per_p, extent = sets[0].shape[1:3]
    rows = q_here.shape[1] - 2 * SUB
    sums = jax.ShapeDtypeStruct((tile_count * tile_count, extent // SEATS, extent), jnp.float32)
    made = sums
    if coded:
        shape = (tile_count * cols, tile_count // cols // 2 + 1) + sums.shape[1:]
        made = jax.ShapeDtypeStruct(shape, jnp.int32)
    operands = [q_here, *sets] + ([] if acc is None else [acc])
    return pl.pallas_call(
        functools.partial(product_kernel, tile_count, cols, routes, acc is None, coded),
        out_shape=made,
        in_specs=[pl.BlockSpec(memory_space=pltpu.VMEM)] * len(operands),
        out_specs=pl.BlockSpec(memory_space=pltpu.VMEM),
        scratch_shapes=[
            pltpu.VMEM((SEATS, extent), jnp.int32),
            pltpu.SMEM((SEATS, extent), jnp.int32),
            pltpu.SemaphoreType.DMA,
        ]
        + [pltpu.VMEM(sums.shape, sums.dtype)] * coded,
        input_output_aliases={} if acc is None or coded else {len(operands) - 1: 0},
        cost_estimate=pl.CostEstimate(
            flops=2 * len(sets) * per_p * rows * extent * extent,
            bytes_accessed=len(sets) * (1 << 18),
            transcendentals=0,
        ),
        compiler_params=pltpu.CompilerParams(vmem_limit_bytes=24 << 20),
        name="products",
    )(*operands)


def code(acc_ref, out_ref, tiles):
    extra = 24 // tiles
    half = 1 << (15 + extra)
    for d in range(out_ref.shape[0]):
        values = [acc_ref[d * tiles + t] for t in range(tiles)]
        left = functools.reduce(jnp.maximum, [jnp.abs(value) for value in values]) * 2.0**FLOOR
        scale = jnp.full(left.shape, 2.0 ** (FLOOR - 1) * half, jnp.float32)
        last = jnp.zeros(left.shape, jnp.int32)
        for i in reversed(range(7)):
            big = left >= 2.0 ** (1 << i)
            down = jnp.where(big, 2.0 ** -(1 << i), 1.0)
            left, scale = left * down, scale * down
            last = jnp.where(big, last + (1 << i), last)
        low = []
        for t, value in enumerate(values):
            whole = jnp.floor(value * scale + 0.5).astype(jnp.int32)
            whole = jnp.minimum(whole, half - 1) + half
            low.append(whole & 0xFFFF)
            last = last | ((whole >> 16) << (8 + extra * t))
        for j in range(tiles // 2):
            out_ref[d, j] = low[2 * j] | (low[2 * j + 1] << 16)
        out_ref[d, tiles // 2] = last


def finish_kernel(x_ref, out_ref):
    planes, seats, words, strip, extent = x_ref.shape
    tiles = 2 * (words - 1)
    extra = 24 // tiles
    half = 1 << (15 + extra)
    wholes = [None] * tiles
    for z in range(planes):
        last = x_ref[z, :, words - 1]
        scale = jnp.full(last.shape, 2.0 ** (1 - FLOOR) / half, jnp.float32)
        for i in range(7):
            scale = scale * jnp.where((last >> i) & 1 == 1, 2.0 ** (1 << i), 1.0)
        for t in range(tiles):
            whole = (x_ref[z, :, t // 2] >> (16 * (t % 2))) & 0xFFFF
            whole = whole | (((last >> (8 + extra * t)) & ((1 << extra) - 1)) << 16)
            value = (whole - half).astype(jnp.float32) * scale
            wholes[t] = value if z == 0 else wholes[t] + value
    for t in range(tiles):
        out_ref[:, t * extent:(t + 1) * extent] = wholes[t].reshape(seats * strip, extent).T


def body(p_tiles, p_cols, q_tiles, q_cols):
    blocks, per_p, extent, _ = p_tiles.shape
    per_q = q_tiles.shape[1]
    planes, cols = lax.axis_size("plane"), lax.axis_size("col")
    tile_count = planes * SEATS // cols
    strip = extent // SEATS
    height = blocks * per_q * strip + 2 * SUB
    seat = ("pair", "core", "col")

    sliced = pl.pallas_call(
        slice_kernel,
        out_shape=jax.ShapeDtypeStruct((SEATS, height, extent), q_tiles.dtype),
        in_specs=[pl.BlockSpec(memory_space=pltpu.SMEM)] * 2 + [pl.BlockSpec(memory_space=pltpu.VMEM)],
        cost_estimate=pl.CostEstimate(flops=0, bytes_accessed=8 << 20, transcendentals=0),
        name="cut_columns",
    )(p_cols.T, q_cols, q_tiles)

    def along(values, step):
        hops = [(s, s ^ axes(s // cols % 2, cols)[step]) for s in range(SEATS)]
        return lax.ppermute(values, seat, hops)

    def across(values):
        return lax.ppermute(values, seat, [(s, s ^ cols) for s in range(SEATS)])

    def add(acc, sets, routes, coded=False):
        return add_products(q_here, sets, routes, acc, tile_count, cols, coded)

    one = along(p_tiles, 0)
    sliced, one = lax.optimization_barrier((sliced, one))
    q_here = lax.all_to_all(sliced, seat, split_axis=0, concat_axis=0, tiled=True)
    second = [along(p_tiles, 1), along(p_tiles, 2), along(one, 1)]
    acc = add(
        None, [p_tiles, one, across(p_tiles), across(one)], [(0, 0), (1, 0), (0, 1), (1, 1)]
    )
    second, acc = lax.optimization_barrier((second, acc))
    third = [along(second[1], 1), along(second[1], 0), along(second[2], 2)]
    sets = second + [across(each) for each in second]
    acc = add(acc, sets, [(step, swapped) for swapped in (0, 1) for step in (2, 3, 4)])
    third, acc = lax.optimization_barrier((third, acc))
    crossed = [across(each) for each in third]
    acc = add(acc, third, [(5, 0), (6, 0), (7, 0)])
    coded = add(acc, crossed, [(5, 1), (6, 1), (7, 1)], coded=True)
    every = ("plane",) + seat
    tiles = tile_count // cols
    landed = lax.all_to_all(coded, every, split_axis=0, concat_axis=0, tiled=True)
    return pl.pallas_call(
        finish_kernel,
        out_shape=jax.ShapeDtypeStruct((extent, tiles * extent), jnp.float32),
        compiler_params=pltpu.CompilerParams(vmem_limit_bytes=16 << 20),
        name="turn",
    )(landed.reshape((planes, SEATS) + landed.shape[1:]))


def solution(mesh):
    rows, cols = mesh.devices.shape
    pairs = SEATS // (2 * cols)
    shape = (rows // (2 * pairs), pairs, 2, cols)
    every = ("plane", "pair", "core", "col")
    inner = Mesh(mesh.devices.reshape(shape), every)
    placed = (
        P(every, None, None, None),
        P(every, None),
        P(every, None, None, None),
        P(every, None),
    )
    return jax.shard_map(
        body, mesh=inner, in_specs=placed, out_specs=P(every[:3], "col"), check_vma=False
    )
```

```python
import functools

import jax
import jax.numpy as jnp
from jax import lax
from jax.experimental import pallas as pl
from jax.experimental.pallas import tpu as pltpu
from jax.sharding import Mesh
from jax.sharding import PartitionSpec as P

SEATS = 16
SUB = 8
FLOOR = 100


def axes(core, cols):
    bits = [bit for bit in (1, 2, 4, 8) if bit != cols]
    return bits[core:] + bits[:core]


def pack_kernel(cols, p_ids, q_ids, p_ref, q_ref, own_ref, *rest):
    out_refs, strips = rest[:3], rest[3]
    blocks, per_q, extent, _ = q_ref.shape
    per_p = p_ids.shape[0]
    strip = extent // SEATS
    rows = per_q * strip
    lane = lax.broadcasted_iota(jnp.int32, (2 * SUB, extent), 1)
    ids = jnp.zeros((2 * SUB, extent), jnp.int32)
    for f in range(blocks):
        for k in range(per_p + per_q):
            value = p_ids[k, f] if k < per_p else q_ids[f, k - per_p]
            ids = jnp.where(lane == f * (per_p + per_q) + k, value, ids)
    ids = ids.astype(p_ref.dtype)
    for f in range(blocks):
        flipped = [q_ref[f, k].astype(jnp.float32).T for k in range(per_q)]
        for j in range(SEATS):
            pieces = [tile[j * strip:(j + 1) * strip] for tile in flipped]
            strips[j, f * rows:(f + 1) * rows] = jnp.concatenate(pieces, axis=0).astype(strips.dtype)
    here = lax.axis_index(("pair", "core", "col"))
    core = lax.axis_index("core")
    paths = [[()], [(0,), (0, 1), (0, 1, 2)], [(1,), (1, 2)], [(2,), (2, 0)]]
    for path, out_ref in zip(paths, (own_ref, *out_refs)):
        spots = []
        for steps in path:
            masks = [sum(axes(c, cols)[step] for step in steps) for c in range(2)]
            to = here ^ jnp.where(core == 0, masks[0], masks[1])
            spots += [to, to ^ cols]
        place = 0
        for to in spots[:-2]:
            out_ref[place:place + blocks * rows] = strips[to]
            place += blocks * rows
        for f in range(blocks):
            for k in range(per_p):
                out_ref[place:place + extent] = p_ref[f, k]
                place += extent
        out_ref[place:place + 2 * SUB] = ids
        place += 2 * SUB
        for to in (spots[-1], spots[-2]):
            out_ref[place:place + blocks * rows] = strips[to]
            place += blocks * rows


def rest_kernel(skip, in_ref, out_ref, sem):
    copy = pltpu.make_async_copy(in_ref.at[skip:], out_ref, sem)
    copy.start()
    copy.wait()


def rest_of(packet, skip):
    height, extent = packet.shape
    return pl.pallas_call(
        functools.partial(rest_kernel, skip),
        out_shape=jax.ShapeDtypeStruct((height - skip, extent), packet.dtype),
        in_specs=[pl.BlockSpec(memory_space=pl.ANY)],
        out_specs=pl.BlockSpec(memory_space=pl.ANY),
        scratch_shapes=[pltpu.SemaphoreType.DMA],
        compiler_params=pltpu.CompilerParams(vmem_limit_bytes=1 << 20),
        name="rest_of_packet",
    )(packet)


def product_kernel(sizes, tile_count, passed, first, coded, *refs):
    count = len(passed)
    packets, (out_ref, wide_ids, ids, id_sem, *sums) = refs[:count], refs[count + (not first):]
    acc_ref = sums[0] if coded else out_ref
    blocks, per_p, per_q = sizes
    strip, extent = acc_ref.shape[1:]
    rows = per_q * strip
    places = []
    for i, (before, swapped) in enumerate(passed):
        tiles = 2 * before * blocks * rows
        indices = tiles + blocks * per_p * extent
        mine = swapped * blocks * rows if before else indices + 2 * SUB + (1 - swapped) * blocks * rows
        places.append((tiles, mine))
        wide_ids[i:i + 1] = packets[i][indices:indices + 2 * SUB].astype(jnp.int32)[:1]
    id_copy = pltpu.make_async_copy(wide_ids, ids, id_sem)
    id_copy.start()
    if first:
        acc_ref[...] = jnp.zeros_like(acc_ref)
    else:
        acc_ref[...] = refs[count][...]
    id_copy.wait()
    for i, (tiles, mine) in enumerate(places):
        for f in range(blocks):
            left = packets[i][mine + f * rows:mine + (f + 1) * rows]
            base = tiles + f * per_p * extent
            right = [packets[i][base + k * extent:base + (k + 1) * extent] for k in range(per_p)]
            product = jnp.dot(
                left, jnp.concatenate(right, axis=1), preferred_element_type=jnp.float32
            )
            start = f * (per_p + per_q)
            for k in range(per_p):
                row = ids[i, start + k] * tile_count
                for l in range(per_q):
                    spot = row + ids[i, start + per_p + l]
                    acc_ref[spot] += product[l * strip:(l + 1) * strip, k * extent:(k + 1) * extent]
    if coded:
        code(acc_ref, out_ref, out_ref.shape[1] * 2 - 2)


def code(acc_ref, out_ref, tiles):
    extra = 24 // tiles
    half = 1 << (15 + extra)
    for d in range(out_ref.shape[0]):
        values = [acc_ref[d * tiles + t] for t in range(tiles)]
        left = functools.reduce(jnp.maximum, [jnp.abs(value) for value in values]) * 2.0**FLOOR
        scale = jnp.full(left.shape, 2.0 ** (FLOOR - 1) * half, jnp.float32)
        last = jnp.zeros(left.shape, jnp.int32)
        for i in reversed(range(7)):
            big = left >= 2.0 ** (1 << i)
            down = jnp.where(big, 2.0 ** -(1 << i), 1.0)
            left, scale = left * down, scale * down
            last = jnp.where(big, last + (1 << i), last)
        low = []
        for t, value in enumerate(values):
            whole = jnp.floor(value * scale + 0.5).astype(jnp.int32)
            whole = jnp.minimum(whole, half - 1) + half
            low.append(whole & 0xFFFF)
            last = last | ((whole >> 16) << (8 + extra * t))
        for j in range(tiles // 2):
            out_ref[d, j] = low[2 * j] | (low[2 * j + 1] << 16)
        out_ref[d, tiles // 2] = last


def add_products(sizes, tile_count, cols, packets, passed, acc, coded=False):
    blocks, per_p, per_q = sizes
    extent = packets[0].shape[1]
    sums = jax.ShapeDtypeStruct((tile_count * tile_count, extent // SEATS, extent), jnp.float32)
    made = sums
    if coded:
        shape = (tile_count * cols, tile_count // cols // 2 + 1) + sums.shape[1:]
        made = jax.ShapeDtypeStruct(shape, jnp.int32)
    operands = [*packets] + ([] if acc is None else [acc])
    return pl.pallas_call(
        functools.partial(product_kernel, sizes, tile_count, passed, acc is None, coded),
        out_shape=made,
        in_specs=[pl.BlockSpec(memory_space=pltpu.VMEM)] * len(operands),
        out_specs=pl.BlockSpec(memory_space=pltpu.VMEM),
        scratch_shapes=[
            pltpu.VMEM((SEATS, extent), jnp.int32),
            pltpu.SMEM((SEATS, extent), jnp.int32),
            pltpu.SemaphoreType.DMA,
        ]
        + [pltpu.VMEM(sums.shape, sums.dtype)] * coded,
        input_output_aliases={} if acc is None or coded else {len(operands) - 1: 0},
        cost_estimate=pl.CostEstimate(
            flops=2 * len(packets) * blocks * per_p * per_q * extent**3 // SEATS,
            bytes_accessed=len(packets) * (1 << 20),
            transcendentals=0,
        ),
        compiler_params=pltpu.CompilerParams(vmem_limit_bytes=24 << 20),
        name="products",
    )(*operands)


def finish_kernel(x_ref, out_ref):
    planes, seats, words, strip, extent = x_ref.shape
    tiles = 2 * (words - 1)
    extra = 24 // tiles
    half = 1 << (15 + extra)
    wholes = [None] * tiles
    for z in range(planes):
        last = x_ref[z, :, words - 1]
        scale = jnp.full(last.shape, 2.0 ** (1 - FLOOR) / half, jnp.float32)
        for i in range(7):
            scale = scale * jnp.where((last >> i) & 1 == 1, 2.0 ** (1 << i), 1.0)
        for t in range(tiles):
            whole = (x_ref[z, :, t // 2] >> (16 * (t % 2))) & 0xFFFF
            whole = whole | (((last >> (8 + extra * t)) & ((1 << extra) - 1)) << 16)
            value = (whole - half).astype(jnp.float32) * scale
            wholes[t] = value if z == 0 else wholes[t] + value
    for t in range(tiles):
        out_ref[:, t * extent:(t + 1) * extent] = wholes[t].reshape(seats * strip, extent).T


def body(p_tiles, p_cols, q_tiles, q_cols):
    blocks, per_p, extent, _ = p_tiles.shape
    per_q = q_tiles.shape[1]
    planes, cols = lax.axis_size("plane"), lax.axis_size("col")
    tile_count = planes * SEATS // cols
    strips = 2 * blocks * per_q * extent // SEATS
    whole = blocks * per_p * extent + 2 * SUB + strips
    seat = ("pair", "core", "col")

    own, *out = pl.pallas_call(
        functools.partial(pack_kernel, cols),
        out_shape=[
            jax.ShapeDtypeStruct((whole + passed * strips, extent), p_tiles.dtype)
            for passed in (0, 2, 1, 1)
        ],
        in_specs=[pl.BlockSpec(memory_space=pltpu.SMEM)] * 2
        + [pl.BlockSpec(memory_space=pltpu.VMEM)] * 2,
        scratch_shapes=[pltpu.VMEM((SEATS, strips // 2, extent), p_tiles.dtype)],
        name="pack",
    )(p_cols.T, q_cols, p_tiles, q_tiles)

    def along(values, step):
        hops = [(s, s ^ axes(s // cols % 2, cols)[step]) for s in range(SEATS)]
        return lax.ppermute(values, seat, hops)

    def across(values):
        return lax.ppermute(values, seat, [(s, s ^ cols) for s in range(SEATS)])

    def add(acc, packets, passed, coded=False):
        sizes = (blocks, per_p, per_q)
        return add_products(sizes, tile_count, cols, packets, passed, acc, coded)

    first = [along(out[step], step) for step in range(3)]
    second = [along(rest_of(first[step], strips), (step + 1) % 3) for step in range(3)]
    crossed = [across(each) for each in [own] + first]
    acc = add(
        None, [own] + first + crossed[:2], [(0, 0), (2, 0), (1, 0), (1, 0), (0, 1), (2, 1)]
    )
    second, acc = lax.optimization_barrier((second, acc))
    third = along(rest_of(second[0], strips), 2)
    acc = add(
        acc,
        second + crossed[2:] + [across(each) for each in second],
        [(1, 0), (0, 0), (0, 0), (1, 1), (1, 1), (1, 1), (0, 1), (0, 1)],
    )
    third, acc = lax.optimization_barrier((third, acc))
    beside = across(third)
    acc = add(acc, [third], [(0, 0)])
    coded = add(acc, [beside], [(0, 1)], coded=True)
    every = ("plane",) + seat
    tiles = tile_count // cols
    landed = lax.all_to_all(coded, every, split_axis=0, concat_axis=0, tiled=True)
    return pl.pallas_call(
        finish_kernel,
        out_shape=jax.ShapeDtypeStruct((extent, tiles * extent), jnp.float32),
        compiler_params=pltpu.CompilerParams(vmem_limit_bytes=16 << 20),
        name="turn",
    )(landed.reshape((planes, SEATS) + landed.shape[1:]))


def solution(mesh):
    rows, cols = mesh.devices.shape
    pairs = SEATS // (2 * cols)
    shape = (rows // (2 * pairs), pairs, 2, cols)
    every = ("plane", "pair", "core", "col")
    inner = Mesh(mesh.devices.reshape(shape), every)
    placed = (
        P(every, None, None, None),
        P(every, None),
        P(every, None, None, None),
        P(every, None),
    )
    return jax.shard_map(
        body, mesh=inner, in_specs=placed, out_specs=P(every[:3], "col"), check_vma=False
    )
```

```python
import functools

import jax
import jax.numpy as jnp
from jax import lax
from jax.experimental import pallas as pl
from jax.experimental.pallas import tpu as pltpu
from jax.sharding import Mesh
from jax.sharding import PartitionSpec as P

SEATS = 16
SUB = 8
FLOOR = 100


def axes(core, cols):
    bits = [bit for bit in (1, 2, 4, 8) if bit != cols]
    return bits[core:] + bits[:core]


def pack_kernel(cols, p_ids, q_ids, p_ref, q_ref, own_ref, *rest):
    out_refs, strips = rest[:4], rest[4]
    blocks, per_q, extent, _ = q_ref.shape
    per_p = p_ids.shape[0]
    strip = extent // SEATS
    rows = per_q * strip
    lane = lax.broadcasted_iota(jnp.int32, (2 * SUB, extent), 1)
    ids = jnp.zeros((2 * SUB, extent), jnp.int32)
    for f in range(blocks):
        for k in range(per_p + per_q):
            value = p_ids[k, f] if k < per_p else q_ids[f, k - per_p]
            ids = jnp.where(lane == f * (per_p + per_q) + k, value, ids)
    ids = ids.astype(p_ref.dtype)
    for f in range(blocks):
        flipped = [q_ref[f, k].astype(jnp.float32).T for k in range(per_q)]
        for j in range(SEATS):
            pieces = [tile[j * strip:(j + 1) * strip] for tile in flipped]
            strips[j, f * rows:(f + 1) * rows] = jnp.concatenate(pieces, axis=0).astype(strips.dtype)
    here = lax.axis_index(("pair", "core", "col"))
    core = lax.axis_index("core")
    paths = [[()], [(0,), (0, 1)], [(1,), (1, 2)], [(2,), (2, 0)], [(0, 1, 2)]]
    for path, out_ref in zip(paths, (own_ref, *out_refs)):
        spots = []
        for steps in path:
            masks = [sum(axes(c, cols)[step] for step in steps) for c in range(2)]
            to = here ^ jnp.where(core == 0, masks[0], masks[1])
            spots += [to, to ^ cols]
        place = 0
        for to in spots[:-2]:
            out_ref[place:place + blocks * rows] = strips[to]
            place += blocks * rows
        for f in range(blocks):
            for k in range(per_p):
                out_ref[place:place + extent] = p_ref[f, k]
                place += extent
        out_ref[place:place + 2 * SUB] = ids
        place += 2 * SUB
        for to in (spots[-1], spots[-2]):
            out_ref[place:place + blocks * rows] = strips[to]
            place += blocks * rows


def rest_kernel(skip, in_ref, out_ref, sem):
    copy = pltpu.make_async_copy(in_ref.at[skip:], out_ref, sem)
    copy.start()
    copy.wait()


def rest_of(packet, skip):
    height, extent = packet.shape
    return pl.pallas_call(
        functools.partial(rest_kernel, skip),
        out_shape=jax.ShapeDtypeStruct((height - skip, extent), packet.dtype),
        in_specs=[pl.BlockSpec(memory_space=pl.ANY)],
        out_specs=pl.BlockSpec(memory_space=pl.ANY),
        scratch_shapes=[pltpu.SemaphoreType.DMA],
        compiler_params=pltpu.CompilerParams(vmem_limit_bytes=1 << 20),
        name="rest_of_packet",
    )(packet)


def product_kernel(sizes, tile_count, passed, first, coded, *refs):
    count = len(passed)
    packets, (out_ref, wide_ids, ids, id_sem, *sums) = refs[:count], refs[count + (not first):]
    acc_ref = sums[0] if coded else out_ref
    blocks, per_p, per_q = sizes
    strip, extent = acc_ref.shape[1:]
    rows = per_q * strip
    places = []
    for i, (before, swapped) in enumerate(passed):
        tiles = 2 * before * blocks * rows
        indices = tiles + blocks * per_p * extent
        mine = swapped * blocks * rows if before else indices + 2 * SUB + (1 - swapped) * blocks * rows
        places.append((tiles, mine))
        wide_ids[i:i + 1] = packets[i][indices:indices + 2 * SUB].astype(jnp.int32)[:1]
    id_copy = pltpu.make_async_copy(wide_ids, ids, id_sem)
    id_copy.start()
    if first:
        acc_ref[...] = jnp.zeros_like(acc_ref)
    else:
        acc_ref[...] = refs[count][...]
    id_copy.wait()
    for i, (tiles, mine) in enumerate(places):
        for f in range(blocks):
            left = packets[i][mine + f * rows:mine + (f + 1) * rows]
            base = tiles + f * per_p * extent
            right = [packets[i][base + k * extent:base + (k + 1) * extent] for k in range(per_p)]
            product = jnp.dot(
                left, jnp.concatenate(right, axis=1), preferred_element_type=jnp.float32
            )
            start = f * (per_p + per_q)
            for k in range(per_p):
                row = ids[i, start + k] * tile_count
                for l in range(per_q):
                    spot = row + ids[i, start + per_p + l]
                    acc_ref[spot] += product[l * strip:(l + 1) * strip, k * extent:(k + 1) * extent]
    if coded:
        code(acc_ref, out_ref, out_ref.shape[1] * 2 - 2)


def code(acc_ref, out_ref, tiles):
    extra = 24 // tiles
    half = 1 << (15 + extra)
    for d in range(out_ref.shape[0]):
        values = [acc_ref[d * tiles + t] for t in range(tiles)]
        left = functools.reduce(jnp.maximum, [jnp.abs(value) for value in values]) * 2.0**FLOOR
        scale = jnp.full(left.shape, 2.0 ** (FLOOR - 1) * half, jnp.float32)
        last = jnp.zeros(left.shape, jnp.int32)
        for i in reversed(range(7)):
            big = left >= 2.0 ** (1 << i)
            down = jnp.where(big, 2.0 ** -(1 << i), 1.0)
            left, scale = left * down, scale * down
            last = jnp.where(big, last + (1 << i), last)
        low = []
        for t, value in enumerate(values):
            whole = jnp.floor(value * scale + 0.5).astype(jnp.int32)
            whole = jnp.minimum(whole, half - 1) + half
            low.append(whole & 0xFFFF)
            last = last | ((whole >> 16) << (8 + extra * t))
        for j in range(tiles // 2):
            out_ref[d, j] = low[2 * j] | (low[2 * j + 1] << 16)
        out_ref[d, tiles // 2] = last


def add_products(sizes, tile_count, cols, packets, passed, acc, coded=False):
    blocks, per_p, per_q = sizes
    extent = packets[0].shape[1]
    sums = jax.ShapeDtypeStruct((tile_count * tile_count, extent // SEATS, extent), jnp.float32)
    made = sums
    if coded:
        shape = (tile_count * cols, tile_count // cols // 2 + 1) + sums.shape[1:]
        made = jax.ShapeDtypeStruct(shape, jnp.int32)
    operands = [*packets] + ([] if acc is None else [acc])
    return pl.pallas_call(
        functools.partial(product_kernel, sizes, tile_count, passed, acc is None, coded),
        out_shape=made,
        in_specs=[pl.BlockSpec(memory_space=pltpu.VMEM)] * len(operands),
        out_specs=pl.BlockSpec(memory_space=pltpu.VMEM),
        scratch_shapes=[
            pltpu.VMEM((SEATS, extent), jnp.int32),
            pltpu.SMEM((SEATS, extent), jnp.int32),
            pltpu.SemaphoreType.DMA,
        ]
        + [pltpu.VMEM(sums.shape, sums.dtype)] * coded,
        input_output_aliases={} if acc is None or coded else {len(operands) - 1: 0},
        cost_estimate=pl.CostEstimate(
            flops=2 * len(packets) * blocks * per_p * per_q * extent**3 // SEATS,
            bytes_accessed=len(packets) * (1 << 20),
            transcendentals=0,
        ),
        compiler_params=pltpu.CompilerParams(vmem_limit_bytes=24 << 20),
        name="products",
    )(*operands)


def finish_kernel(x_ref, out_ref):
    planes, seats, words, strip, extent = x_ref.shape
    tiles = 2 * (words - 1)
    extra = 24 // tiles
    half = 1 << (15 + extra)
    wholes = [None] * tiles
    for z in range(planes):
        last = x_ref[z, :, words - 1]
        scale = jnp.full(last.shape, 2.0 ** (1 - FLOOR) / half, jnp.float32)
        for i in range(7):
            scale = scale * jnp.where((last >> i) & 1 == 1, 2.0 ** (1 << i), 1.0)
        for t in range(tiles):
            whole = (x_ref[z, :, t // 2] >> (16 * (t % 2))) & 0xFFFF
            whole = whole | (((last >> (8 + extra * t)) & ((1 << extra) - 1)) << 16)
            value = (whole - half).astype(jnp.float32) * scale
            wholes[t] = value if z == 0 else wholes[t] + value
    for t in range(tiles):
        out_ref[:, t * extent:(t + 1) * extent] = wholes[t].reshape(seats * strip, extent).T


def body(p_tiles, p_cols, q_tiles, q_cols):
    blocks, per_p, extent, _ = p_tiles.shape
    per_q = q_tiles.shape[1]
    planes, cols = lax.axis_size("plane"), lax.axis_size("col")
    tile_count = planes * SEATS // cols
    strips = 2 * blocks * per_q * extent // SEATS
    whole = blocks * per_p * extent + 2 * SUB + strips
    seat = ("pair", "core", "col")

    own, *out = pl.pallas_call(
        functools.partial(pack_kernel, cols),
        out_shape=[
            jax.ShapeDtypeStruct((whole + passed * strips, extent), p_tiles.dtype)
            for passed in (0, 1, 1, 1, 0)
        ],
        in_specs=[pl.BlockSpec(memory_space=pltpu.SMEM)] * 2
        + [pl.BlockSpec(memory_space=pltpu.VMEM)] * 2,
        scratch_shapes=[pltpu.VMEM((SEATS, strips // 2, extent), p_tiles.dtype)],
        name="pack",
    )(p_cols.T, q_cols, p_tiles, q_tiles)

    def along(values, step):
        hops = [(s, s ^ axes(s // cols % 2, cols)[step]) for s in range(SEATS)]
        return lax.ppermute(values, seat, hops)

    def across(values):
        return lax.ppermute(values, seat, [(s, s ^ cols) for s in range(SEATS)])

    def add(acc, packets, passed, coded=False):
        sizes = (blocks, per_p, per_q)
        return add_products(sizes, tile_count, cols, packets, passed, acc, coded)

    def opposite(values):
        return lax.ppermute(values, seat, [(s, s ^ (SEATS - 1 - cols)) for s in range(SEATS)])

    first = [along(out[step], step) for step in range(3)]
    beside = across(own)
    far = opposite(out[3])
    second = [along(rest_of(first[step], strips), (step + 1) % 3) for step in range(3)]
    acc = add(None, [own, beside] + first, [(0, 0), (0, 1), (1, 0), (1, 0), (1, 0)])
    second, acc = lax.optimization_barrier((second, acc))
    crossed = [across(each) for each in [far] + first]
    more = [across(each) for each in second]
    acc = add(
        acc, [far] + second + crossed, [(0, 0)] * 4 + [(0, 1)] + [(1, 1)] * 3
    )
    coded = add(acc, more, [(0, 1)] * 3, coded=True)
    every = ("plane",) + seat
    tiles = tile_count // cols
    landed = lax.all_to_all(coded, every, split_axis=0, concat_axis=0, tiled=True)
    return pl.pallas_call(
        finish_kernel,
        out_shape=jax.ShapeDtypeStruct((extent, tiles * extent), jnp.float32),
        compiler_params=pltpu.CompilerParams(vmem_limit_bytes=16 << 20),
        name="turn",
    )(landed.reshape((planes, SEATS) + landed.shape[1:]))


def solution(mesh):
    rows, cols = mesh.devices.shape
    pairs = SEATS // (2 * cols)
    shape = (rows // (2 * pairs), pairs, 2, cols)
    every = ("plane", "pair", "core", "col")
    inner = Mesh(mesh.devices.reshape(shape), every)
    placed = (
        P(every, None, None, None),
        P(every, None),
        P(every, None, None, None),
        P(every, None),
    )
    return jax.shard_map(
        body, mesh=inner, in_specs=placed, out_specs=P(every[:3], "col"), check_vma=False
    )
```

```python
import functools

import jax
import jax.numpy as jnp
from jax import lax
from jax.experimental import pallas as pl
from jax.experimental.pallas import tpu as pltpu
from jax.sharding import Mesh
from jax.sharding import PartitionSpec as P

SEATS = 16
SUB = 8
FLOOR = 100


def axes(core, cols):
    bits = [bit for bit in (1, 2, 4, 8) if bit != cols]
    return bits[core:] + bits[:core]


def pack_kernel(cols, p_ids, q_ids, p_ref, q_ref, own_ref, *rest):
    out_refs, strips = rest[:4], rest[4]
    blocks, per_q, extent, _ = q_ref.shape
    per_p = p_ids.shape[0]
    strip = extent // SEATS
    rows = per_q * strip
    lane = lax.broadcasted_iota(jnp.int32, (2 * SUB, extent), 1)
    ids = jnp.zeros((2 * SUB, extent), jnp.int32)
    for f in range(blocks):
        for k in range(per_p + per_q):
            value = p_ids[k, f] if k < per_p else q_ids[f, k - per_p]
            ids = jnp.where(lane == f * (per_p + per_q) + k, value, ids)
    ids = ids.astype(p_ref.dtype)
    for f in range(blocks):
        flipped = [q_ref[f, k].astype(jnp.float32).T for k in range(per_q)]
        for j in range(SEATS):
            pieces = [tile[j * strip:(j + 1) * strip] for tile in flipped]
            strips[j, f * rows:(f + 1) * rows] = jnp.concatenate(pieces, axis=0).astype(strips.dtype)
    here = lax.axis_index(("pair", "core", "col"))
    core = lax.axis_index("core")
    paths = [[()], [(0,), (0, 1)], [(1,), (1, 2)], [(2,), (2, 0)], [(0, 1, 2)]]
    for path, out_ref in zip(paths, (own_ref, *out_refs)):
        spots = []
        for steps in path:
            masks = [sum(axes(c, cols)[step] for step in steps) for c in range(2)]
            to = here ^ jnp.where(core == 0, masks[0], masks[1])
            spots += [to, to ^ cols]
        place = 0
        for to in spots[:-2]:
            out_ref[place:place + blocks * rows] = strips[to]
            place += blocks * rows
        for f in range(blocks):
            for k in range(per_p):
                out_ref[place:place + extent] = p_ref[f, k]
                place += extent
        out_ref[place:place + 2 * SUB] = ids
        place += 2 * SUB
        for to in (spots[-1], spots[-2]):
            out_ref[place:place + blocks * rows] = strips[to]
            place += blocks * rows


def rest_kernel(skip, in_ref, out_ref, sem):
    copy = pltpu.make_async_copy(in_ref.at[skip:], out_ref, sem)
    copy.start()
    copy.wait()


def rest_of(packet, skip):
    height, extent = packet.shape
    return pl.pallas_call(
        functools.partial(rest_kernel, skip),
        out_shape=jax.ShapeDtypeStruct((height - skip, extent), packet.dtype),
        in_specs=[pl.BlockSpec(memory_space=pl.ANY)],
        out_specs=pl.BlockSpec(memory_space=pl.ANY),
        scratch_shapes=[pltpu.SemaphoreType.DMA],
        compiler_params=pltpu.CompilerParams(vmem_limit_bytes=1 << 20),
        name="rest_of_packet",
    )(packet)


def product_kernel(sizes, tile_count, passed, first, coded, *refs):
    count = len(passed)
    packets, (out_ref, wide_ids, ids, id_sem, *sums) = refs[:count], refs[count + (not first):]
    acc_ref = sums[0] if coded else out_ref
    blocks, per_p, per_q = sizes
    strip, extent = acc_ref.shape[1:]
    rows = per_q * strip
    places = []
    for i, (before, swapped) in enumerate(passed):
        tiles = 2 * before * blocks * rows
        indices = tiles + blocks * per_p * extent
        mine = swapped * blocks * rows if before else indices + 2 * SUB + (1 - swapped) * blocks * rows
        places.append((tiles, mine))
        wide_ids[i:i + 1] = packets[i][indices:indices + 2 * SUB].astype(jnp.int32)[:1]
    id_copy = pltpu.make_async_copy(wide_ids, ids, id_sem)
    id_copy.start()
    if first:
        acc_ref[...] = jnp.zeros_like(acc_ref)
    else:
        acc_ref[...] = refs[count][...]
    id_copy.wait()
    for i, (tiles, mine) in enumerate(places):
        for f in range(blocks):
            left = packets[i][mine + f * rows:mine + (f + 1) * rows]
            base = tiles + f * per_p * extent
            right = [packets[i][base + k * extent:base + (k + 1) * extent] for k in range(per_p)]
            product = jnp.dot(
                left, jnp.concatenate(right, axis=1), preferred_element_type=jnp.float32
            )
            start = f * (per_p + per_q)
            for k in range(per_p):
                row = ids[i, start + k] * tile_count
                for l in range(per_q):
                    spot = row + ids[i, start + per_p + l]
                    acc_ref[spot] += product[l * strip:(l + 1) * strip, k * extent:(k + 1) * extent]
    if coded:
        code(acc_ref, out_ref, out_ref.shape[1] * 2 - 2)


def code(acc_ref, out_ref, tiles):
    extra = 24 // tiles
    half = 1 << (15 + extra)
    for d in range(out_ref.shape[0]):
        values = [acc_ref[d * tiles + t] for t in range(tiles)]
        left = functools.reduce(jnp.maximum, [jnp.abs(value) for value in values]) * 2.0**FLOOR
        scale = jnp.full(left.shape, 2.0 ** (FLOOR - 1) * half, jnp.float32)
        last = jnp.zeros(left.shape, jnp.int32)
        for i in reversed(range(7)):
            big = left >= 2.0 ** (1 << i)
            down = jnp.where(big, 2.0 ** -(1 << i), 1.0)
            left, scale = left * down, scale * down
            last = jnp.where(big, last + (1 << i), last)
        low = []
        for t, value in enumerate(values):
            whole = jnp.floor(value * scale + 0.5).astype(jnp.int32)
            whole = jnp.minimum(whole, half - 1) + half
            low.append(whole & 0xFFFF)
            last = last | ((whole >> 16) << (8 + extra * t))
        for j in range(tiles // 2):
            out_ref[d, j] = low[2 * j] | (low[2 * j + 1] << 16)
        out_ref[d, tiles // 2] = last


def add_products(sizes, tile_count, cols, packets, passed, acc, coded=False):
    blocks, per_p, per_q = sizes
    extent = packets[0].shape[1]
    sums = jax.ShapeDtypeStruct((tile_count * tile_count, extent // SEATS, extent), jnp.float32)
    made = sums
    if coded:
        shape = (tile_count * cols, tile_count // cols // 2 + 1) + sums.shape[1:]
        made = jax.ShapeDtypeStruct(shape, jnp.int32)
    operands = [*packets] + ([] if acc is None else [acc])
    return pl.pallas_call(
        functools.partial(product_kernel, sizes, tile_count, passed, acc is None, coded),
        out_shape=made,
        in_specs=[pl.BlockSpec(memory_space=pltpu.VMEM)] * len(operands),
        out_specs=pl.BlockSpec(memory_space=pltpu.VMEM),
        scratch_shapes=[
            pltpu.VMEM((SEATS, extent), jnp.int32),
            pltpu.SMEM((SEATS, extent), jnp.int32),
            pltpu.SemaphoreType.DMA,
        ]
        + [pltpu.VMEM(sums.shape, sums.dtype)] * coded,
        input_output_aliases={} if acc is None or coded else {len(operands) - 1: 0},
        cost_estimate=pl.CostEstimate(
            flops=2 * len(packets) * blocks * per_p * per_q * extent**3 // SEATS,
            bytes_accessed=len(packets) * (1 << 20),
            transcendentals=0,
        ),
        compiler_params=pltpu.CompilerParams(vmem_limit_bytes=24 << 20),
        name="products",
    )(*operands)


def finish_kernel(x_ref, out_ref):
    planes, seats, words, strip, extent = x_ref.shape
    tiles = 2 * (words - 1)
    extra = 24 // tiles
    half = 1 << (15 + extra)
    wholes = [None] * tiles
    for z in range(planes):
        last = x_ref[z, :, words - 1]
        scale = jnp.full(last.shape, 2.0 ** (1 - FLOOR) / half, jnp.float32)
        for i in range(7):
            scale = scale * jnp.where((last >> i) & 1 == 1, 2.0 ** (1 << i), 1.0)
        for t in range(tiles):
            whole = (x_ref[z, :, t // 2] >> (16 * (t % 2))) & 0xFFFF
            whole = whole | (((last >> (8 + extra * t)) & ((1 << extra) - 1)) << 16)
            value = (whole - half).astype(jnp.float32) * scale
            wholes[t] = value if z == 0 else wholes[t] + value
    for t in range(tiles):
        out_ref[:, t * extent:(t + 1) * extent] = wholes[t].reshape(seats * strip, extent).T


def body(p_tiles, p_cols, q_tiles, q_cols):
    blocks, per_p, extent, _ = p_tiles.shape
    per_q = q_tiles.shape[1]
    planes, cols = lax.axis_size("plane"), lax.axis_size("col")
    tile_count = planes * SEATS // cols
    strips = 2 * blocks * per_q * extent // SEATS
    whole = blocks * per_p * extent + 2 * SUB + strips
    seat = ("pair", "core", "col")

    own, *out = pl.pallas_call(
        functools.partial(pack_kernel, cols),
        out_shape=[
            jax.ShapeDtypeStruct((whole + passed * strips, extent), p_tiles.dtype)
            for passed in (0, 1, 1, 1, 0)
        ],
        in_specs=[pl.BlockSpec(memory_space=pltpu.SMEM)] * 2
        + [pl.BlockSpec(memory_space=pltpu.VMEM)] * 2,
        scratch_shapes=[pltpu.VMEM((SEATS, strips // 2, extent), p_tiles.dtype)],
        name="pack",
    )(p_cols.T, q_cols, p_tiles, q_tiles)

    def along(values, step):
        hops = [(s, s ^ axes(s // cols % 2, cols)[step]) for s in range(SEATS)]
        return lax.ppermute(values, seat, hops)

    def across(values):
        return lax.ppermute(values, seat, [(s, s ^ cols) for s in range(SEATS)])

    def add(acc, packets, passed, coded=False):
        sizes = (blocks, per_p, per_q)
        return add_products(sizes, tile_count, cols, packets, passed, acc, coded)

    def opposite(values):
        return lax.ppermute(values, seat, [(s, s ^ (SEATS - 1 - cols)) for s in range(SEATS)])

    first = [along(out[step], step) for step in range(3)]
    beside = across(own)
    far = opposite(out[3])
    second = [along(rest_of(first[step], strips), (step + 1) % 3) for step in range(3)]
    acc = add(None, [own, beside] + first, [(0, 0), (0, 1), (1, 0), (1, 0), (1, 0)])
    first[2], second, acc = lax.optimization_barrier((first[2], second, acc))
    acc = add(
        acc,
        [far, across(far), across(first[0])] + second,
        [(0, 0), (0, 1), (1, 1), (0, 0), (0, 0), (0, 0)],
    )
    crossed = [across(each) for each in first[1:] + second]
    coded = add(acc, crossed, [(1, 1), (1, 1), (0, 1), (0, 1), (0, 1)], coded=True)
    every = ("plane",) + seat
    tiles = tile_count // cols
    landed = lax.all_to_all(coded, every, split_axis=0, concat_axis=0, tiled=True)
    return pl.pallas_call(
        finish_kernel,
        out_shape=jax.ShapeDtypeStruct((extent, tiles * extent), jnp.float32),
        compiler_params=pltpu.CompilerParams(vmem_limit_bytes=16 << 20),
        name="turn",
    )(landed.reshape((planes, SEATS) + landed.shape[1:]))


def solution(mesh):
    rows, cols = mesh.devices.shape
    pairs = SEATS // (2 * cols)
    shape = (rows // (2 * pairs), pairs, 2, cols)
    every = ("plane", "pair", "core", "col")
    inner = Mesh(mesh.devices.reshape(shape), every)
    placed = (
        P(every, None, None, None),
        P(every, None),
        P(every, None, None, None),
        P(every, None),
    )
    return jax.shard_map(
        body, mesh=inner, in_specs=placed, out_specs=P(every[:3], "col"), check_vma=False
    )
```

```python
import functools

import jax
import jax.numpy as jnp
from jax import lax
from jax.experimental import pallas as pl
from jax.experimental.pallas import tpu as pltpu
from jax.sharding import Mesh
from jax.sharding import PartitionSpec as P

SEATS = 16
SUB = 8
FLOOR = 100


def axes(core, cols):
    bits = [bit for bit in (1, 2, 4, 8) if bit != cols]
    return bits[core:] + bits[:core]


def pack_kernel(cols, p_ids, q_ids, p_ref, q_ref, own_ref, *rest):
    out_refs, strips = rest[:4], rest[4]
    blocks, per_q, extent, _ = q_ref.shape
    per_p = p_ids.shape[0]
    strip = extent // SEATS
    rows = per_q * strip
    lane = lax.broadcasted_iota(jnp.int32, (2 * SUB, extent), 1)
    ids = jnp.zeros((2 * SUB, extent), jnp.int32)
    for f in range(blocks):
        for k in range(per_p + per_q):
            value = p_ids[k, f] if k < per_p else q_ids[f, k - per_p]
            ids = jnp.where(lane == f * (per_p + per_q) + k, value, ids)
    ids = ids.astype(p_ref.dtype)
    for f in range(blocks):
        flipped = [q_ref[f, k].astype(jnp.float32).T for k in range(per_q)]
        for j in range(SEATS):
            pieces = [tile[j * strip:(j + 1) * strip] for tile in flipped]
            strips[j, f * rows:(f + 1) * rows] = jnp.concatenate(pieces, axis=0).astype(strips.dtype)
    here = lax.axis_index(("pair", "core", "col"))
    core = lax.axis_index("core")
    paths = [[()], [(0,), (0, 1)], [(1,), (1, 2)], [(2,), (2, 0)], [(0, 1, 2)]]
    for path, out_ref in zip(paths, (own_ref, *out_refs)):
        spots = []
        for steps in path:
            masks = [sum(axes(c, cols)[step] for step in steps) for c in range(2)]
            to = here ^ jnp.where(core == 0, masks[0], masks[1])
            spots += [to, to ^ cols]
        place = 0
        for to in spots[:-2]:
            out_ref[place:place + blocks * rows] = strips[to]
            place += blocks * rows
        for f in range(blocks):
            for k in range(per_p):
                out_ref[place:place + extent] = p_ref[f, k]
                place += extent
        out_ref[place:place + 2 * SUB] = ids
        place += 2 * SUB
        for to in (spots[-1], spots[-2]):
            out_ref[place:place + blocks * rows] = strips[to]
            place += blocks * rows


def rest_kernel(skip, in_ref, out_ref, sem):
    copy = pltpu.make_async_copy(in_ref.at[skip:], out_ref, sem)
    copy.start()
    copy.wait()


def rest_of(packet, skip):
    height, extent = packet.shape
    return pl.pallas_call(
        functools.partial(rest_kernel, skip),
        out_shape=jax.ShapeDtypeStruct((height - skip, extent), packet.dtype),
        in_specs=[pl.BlockSpec(memory_space=pl.ANY)],
        out_specs=pl.BlockSpec(memory_space=pl.ANY),
        scratch_shapes=[pltpu.SemaphoreType.DMA],
        compiler_params=pltpu.CompilerParams(vmem_limit_bytes=1 << 20),
        name="rest_of_packet",
    )(packet)


def product_kernel(sizes, tile_count, passed, first, coded, *refs):
    count = len(passed)
    packets, (out_ref, wide_ids, ids, id_sem, *sums) = refs[:count], refs[count + (not first):]
    acc_ref = sums[0] if coded else out_ref
    blocks, per_p, per_q = sizes
    strip, extent = acc_ref.shape[1:]
    rows = per_q * strip
    places = []
    for i, (before, swapped) in enumerate(passed):
        tiles = 2 * before * blocks * rows
        indices = tiles + blocks * per_p * extent
        mine = swapped * blocks * rows if before else indices + 2 * SUB + (1 - swapped) * blocks * rows
        places.append((tiles, mine))
        wide_ids[i:i + 1] = packets[i][indices:indices + 2 * SUB].astype(jnp.int32)[:1]
    id_copy = pltpu.make_async_copy(wide_ids, ids, id_sem)
    id_copy.start()
    if first:
        acc_ref[...] = jnp.zeros_like(acc_ref)
    else:
        acc_ref[...] = refs[count][...]
    id_copy.wait()
    for i, (tiles, mine) in enumerate(places):
        for f in range(blocks):
            left = packets[i][mine + f * rows:mine + (f + 1) * rows]
            base = tiles + f * per_p * extent
            right = [packets[i][base + k * extent:base + (k + 1) * extent] for k in range(per_p)]
            product = jnp.dot(
                left, jnp.concatenate(right, axis=1), preferred_element_type=jnp.float32
            )
            start = f * (per_p + per_q)
            spots = [
                ids[i, start + k] * tile_count + ids[i, start + per_p + l]
                for k in range(per_p)
                for l in range(per_q)
            ]
            before = [acc_ref[spot] for spot in spots]
            for n, spot in enumerate(spots):
                k, l = divmod(n, per_q)
                term = product[l * strip:(l + 1) * strip, k * extent:(k + 1) * extent]
                acc_ref[spot] = before[n] + term
    if coded:
        code(acc_ref, out_ref, out_ref.shape[1] * 2 - 2)


def code(acc_ref, out_ref, tiles):
    extra = 24 // tiles
    half = 1 << (15 + extra)
    for d in range(out_ref.shape[0]):
        values = [acc_ref[d * tiles + t] for t in range(tiles)]
        left = functools.reduce(jnp.maximum, [jnp.abs(value) for value in values]) * 2.0**FLOOR
        scale = jnp.full(left.shape, 2.0 ** (FLOOR - 1) * half, jnp.float32)
        last = jnp.zeros(left.shape, jnp.int32)
        for i in reversed(range(7)):
            big = left >= 2.0 ** (1 << i)
            down = jnp.where(big, 2.0 ** -(1 << i), 1.0)
            left, scale = left * down, scale * down
            last = jnp.where(big, last + (1 << i), last)
        low = []
        for t, value in enumerate(values):
            whole = jnp.floor(value * scale + 0.5).astype(jnp.int32)
            whole = jnp.minimum(whole, half - 1) + half
            low.append(whole & 0xFFFF)
            last = last | ((whole >> 16) << (8 + extra * t))
        for j in range(tiles // 2):
            out_ref[d, j] = low[2 * j] | (low[2 * j + 1] << 16)
        out_ref[d, tiles // 2] = last


def add_products(sizes, tile_count, cols, packets, passed, acc, coded=False):
    blocks, per_p, per_q = sizes
    extent = packets[0].shape[1]
    sums = jax.ShapeDtypeStruct((tile_count * tile_count, extent // SEATS, extent), jnp.float32)
    made = sums
    if coded:
        shape = (tile_count * cols, tile_count // cols // 2 + 1) + sums.shape[1:]
        made = jax.ShapeDtypeStruct(shape, jnp.int32)
    operands = [*packets] + ([] if acc is None else [acc])
    return pl.pallas_call(
        functools.partial(product_kernel, sizes, tile_count, passed, acc is None, coded),
        out_shape=made,
        in_specs=[pl.BlockSpec(memory_space=pltpu.VMEM)] * len(operands),
        out_specs=pl.BlockSpec(memory_space=pltpu.VMEM),
        scratch_shapes=[
            pltpu.VMEM((SEATS, extent), jnp.int32),
            pltpu.SMEM((SEATS, extent), jnp.int32),
            pltpu.SemaphoreType.DMA,
        ]
        + [pltpu.VMEM(sums.shape, sums.dtype)] * coded,
        input_output_aliases={} if acc is None or coded else {len(operands) - 1: 0},
        cost_estimate=pl.CostEstimate(
            flops=2 * len(packets) * blocks * per_p * per_q * extent**3 // SEATS,
            bytes_accessed=len(packets) * (1 << 20),
            transcendentals=0,
        ),
        compiler_params=pltpu.CompilerParams(vmem_limit_bytes=24 << 20),
        name="products",
    )(*operands)


def finish_kernel(x_ref, out_ref):
    planes, seats, words, strip, extent = x_ref.shape
    tiles = 2 * (words - 1)
    extra = 24 // tiles
    half = 1 << (15 + extra)
    wholes = [None] * tiles
    for z in range(planes):
        last = x_ref[z, :, words - 1]
        scale = jnp.full(last.shape, 2.0 ** (1 - FLOOR) / half, jnp.float32)
        for i in range(7):
            scale = scale * jnp.where((last >> i) & 1 == 1, 2.0 ** (1 << i), 1.0)
        for t in range(tiles):
            whole = (x_ref[z, :, t // 2] >> (16 * (t % 2))) & 0xFFFF
            whole = whole | (((last >> (8 + extra * t)) & ((1 << extra) - 1)) << 16)
            value = (whole - half).astype(jnp.float32) * scale
            wholes[t] = value if z == 0 else wholes[t] + value
    for t in range(tiles):
        out_ref[:, t * extent:(t + 1) * extent] = wholes[t].reshape(seats * strip, extent).T


def body(p_tiles, p_cols, q_tiles, q_cols):
    blocks, per_p, extent, _ = p_tiles.shape
    per_q = q_tiles.shape[1]
    planes, cols = lax.axis_size("plane"), lax.axis_size("col")
    tile_count = planes * SEATS // cols
    strips = 2 * blocks * per_q * extent // SEATS
    whole = blocks * per_p * extent + 2 * SUB + strips
    seat = ("pair", "core", "col")

    own, *out = pl.pallas_call(
        functools.partial(pack_kernel, cols),
        out_shape=[
            jax.ShapeDtypeStruct((whole + passed * strips, extent), p_tiles.dtype)
            for passed in (0, 1, 1, 1, 0)
        ],
        in_specs=[pl.BlockSpec(memory_space=pltpu.SMEM)] * 2
        + [pl.BlockSpec(memory_space=pltpu.VMEM)] * 2,
        scratch_shapes=[pltpu.VMEM((SEATS, strips // 2, extent), p_tiles.dtype)],
        name="pack",
    )(p_cols.T, q_cols, p_tiles, q_tiles)

    def along(values, step):
        hops = [(s, s ^ axes(s // cols % 2, cols)[step]) for s in range(SEATS)]
        return lax.ppermute(values, seat, hops)

    def across(values):
        return lax.ppermute(values, seat, [(s, s ^ cols) for s in range(SEATS)])

    def add(acc, packets, passed, coded=False):
        sizes = (blocks, per_p, per_q)
        return add_products(sizes, tile_count, cols, packets, passed, acc, coded)

    def opposite(values):
        return lax.ppermute(values, seat, [(s, s ^ (SEATS - 1 - cols)) for s in range(SEATS)])

    first = [along(out[step], step) for step in range(3)]
    beside = across(own)
    far = opposite(out[3])
    second = [along(rest_of(first[step], strips), (step + 1) % 3) for step in range(3)]
    acc = add(None, [own, beside] + first, [(0, 0), (0, 1), (1, 0), (1, 0), (1, 0)])
    first[2], second, acc = lax.optimization_barrier((first[2], second, acc))
    acc = add(
        acc,
        [far, across(far), across(first[0])] + second,
        [(0, 0), (0, 1), (1, 1), (0, 0), (0, 0), (0, 0)],
    )
    crossed = [across(each) for each in first[1:] + second]
    coded = add(acc, crossed, [(1, 1), (1, 1), (0, 1), (0, 1), (0, 1)], coded=True)
    every = ("plane",) + seat
    tiles = tile_count // cols
    landed = lax.all_to_all(coded, every, split_axis=0, concat_axis=0, tiled=True)
    return pl.pallas_call(
        finish_kernel,
        out_shape=jax.ShapeDtypeStruct((extent, tiles * extent), jnp.float32),
        compiler_params=pltpu.CompilerParams(vmem_limit_bytes=16 << 20),
        name="turn",
    )(landed.reshape((planes, SEATS) + landed.shape[1:]))


def solution(mesh):
    rows, cols = mesh.devices.shape
    pairs = SEATS // (2 * cols)
    shape = (rows // (2 * pairs), pairs, 2, cols)
    every = ("plane", "pair", "core", "col")
    inner = Mesh(mesh.devices.reshape(shape), every)
    placed = (
        P(every, None, None, None),
        P(every, None),
        P(every, None, None, None),
        P(every, None),
    )
    return jax.shard_map(
        body, mesh=inner, in_specs=placed, out_specs=P(every[:3], "col"), check_vma=False
    )
```

```python
import functools

import jax
import jax.numpy as jnp
from jax import lax
from jax.experimental import pallas as pl
from jax.experimental.pallas import tpu as pltpu
from jax.sharding import Mesh
from jax.sharding import PartitionSpec as P

SEATS = 16
SUB = 8
FLOOR = 100


def axes(core, cols):
    bits = [bit for bit in (1, 2, 4, 8) if bit != cols]
    return bits[core:] + bits[:core]


def pack_kernel(cols, p_ids, q_ids, p_ref, q_ref, *rest):
    out_refs, (strips, ids, sems) = rest[:-3], rest[-3:]
    blocks, per_q, extent, _ = q_ref.shape
    per_p = p_ids.shape[0]
    strip = extent // SEATS
    rows = per_q * strip
    height, tiles = blocks * rows, p_ref.shape[0]
    here = lax.axis_index(("pair", "core", "col"))
    core = lax.axis_index("core")
    paths = [[()], [(0,), (0, 1)], [(1,), (1, 2)], [(2,), (2, 0)], [(0, 1, 2)]]
    copies, later = [], []
    for path, out_ref in zip(paths, out_refs):
        spots = []
        for steps in path:
            masks = [sum(axes(c, cols)[step] for step in steps) for c in range(2)]
            to = here ^ jnp.where(core == 0, masks[0], masks[1])
            spots += [to, to ^ cols]
        place = 0
        for to in spots[:-2]:
            later.append((strips.at[to], out_ref.at[place:place + height]))
            place += height
        copies.append((p_ref, out_ref.at[place:place + tiles]))
        place += tiles
        later.append((ids, out_ref.at[place:place + 2 * SUB]))
        place += 2 * SUB
        for to in (spots[-1], spots[-2]):
            later.append((strips.at[to], out_ref.at[place:place + height]))
            place += height
    copies = [
        pltpu.make_async_copy(source, target, sems.at[n])
        for n, (source, target) in enumerate(copies + later)
    ]
    for copy in copies[:len(paths)]:
        copy.start()
    lane = lax.broadcasted_iota(jnp.int32, ids.shape, 1)
    words = jnp.zeros(ids.shape, jnp.int32)
    for f in range(blocks):
        for k in range(per_p + per_q):
            value = p_ids[k, f] if k < per_p else q_ids[f, k - per_p]
            words = jnp.where(lane == f * (per_p + per_q) + k, value, words)
    ids[...] = words.astype(ids.dtype)
    for f in range(blocks):
        flipped = [q_ref[f, k].astype(jnp.float32).T for k in range(per_q)]
        for j in range(SEATS):
            pieces = [tile[j * strip:(j + 1) * strip] for tile in flipped]
            strips[j, f * rows:(f + 1) * rows] = jnp.concatenate(pieces, axis=0).astype(strips.dtype)
    for copy in copies[len(paths):]:
        copy.start()
    for copy in copies:
        copy.wait()


def rest_kernel(skip, in_ref, out_ref, sem):
    copy = pltpu.make_async_copy(in_ref.at[skip:], out_ref, sem)
    copy.start()
    copy.wait()


def rest_of(packet, skip):
    height, extent = packet.shape
    return pl.pallas_call(
        functools.partial(rest_kernel, skip),
        out_shape=jax.ShapeDtypeStruct((height - skip, extent), packet.dtype),
        in_specs=[pl.BlockSpec(memory_space=pl.ANY)],
        out_specs=pl.BlockSpec(memory_space=pl.ANY),
        scratch_shapes=[pltpu.SemaphoreType.DMA],
        compiler_params=pltpu.CompilerParams(vmem_limit_bytes=1 << 20),
        name="rest_of_packet",
    )(packet)


def product_kernel(sizes, tile_count, passed, first, coded, *refs):
    count = len(passed)
    packets, (out_ref, wide_ids, ids, id_sem, *sums) = refs[:count], refs[count + (not first):]
    acc_ref = sums[0] if coded else out_ref
    blocks, per_p, per_q = sizes
    strip, extent = acc_ref.shape[1:]
    rows = per_q * strip
    places = []
    for i, (before, swapped) in enumerate(passed):
        tiles = 2 * before * blocks * rows
        indices = tiles + blocks * per_p * extent
        mine = swapped * blocks * rows if before else indices + 2 * SUB + (1 - swapped) * blocks * rows
        places.append((tiles, mine))
        wide_ids[i:i + 1] = packets[i][indices:indices + 2 * SUB].astype(jnp.int32)[:1]
    id_copy = pltpu.make_async_copy(wide_ids, ids, id_sem)
    id_copy.start()
    if first:
        acc_ref[...] = jnp.zeros_like(acc_ref)
    else:
        acc_ref[...] = refs[count][...]
    id_copy.wait()
    for i, (tiles, mine) in enumerate(places):
        for f in range(blocks):
            left = packets[i][mine + f * rows:mine + (f + 1) * rows]
            base = tiles + f * per_p * extent
            right = [packets[i][base + k * extent:base + (k + 1) * extent] for k in range(per_p)]
            product = jnp.dot(
                left, jnp.concatenate(right, axis=1), preferred_element_type=jnp.float32
            )
            start = f * (per_p + per_q)
            spots = [
                ids[i, start + k] * tile_count + ids[i, start + per_p + l]
                for k in range(per_p)
                for l in range(per_q)
            ]
            before = [acc_ref[spot] for spot in spots]
            for n, spot in enumerate(spots):
                k, l = divmod(n, per_q)
                term = product[l * strip:(l + 1) * strip, k * extent:(k + 1) * extent]
                acc_ref[spot] = before[n] + term
    if coded:
        code(acc_ref, out_ref, out_ref.shape[1] * 2 - 2)


def code(acc_ref, out_ref, tiles):
    extra = 24 // tiles
    half = 1 << (15 + extra)
    for d in range(out_ref.shape[0]):
        values = [acc_ref[d * tiles + t] for t in range(tiles)]
        left = functools.reduce(jnp.maximum, [jnp.abs(value) for value in values]) * 2.0**FLOOR
        scale = jnp.full(left.shape, 2.0 ** (FLOOR - 1) * half, jnp.float32)
        last = jnp.zeros(left.shape, jnp.int32)
        for i in reversed(range(7)):
            big = left >= 2.0 ** (1 << i)
            down = jnp.where(big, 2.0 ** -(1 << i), 1.0)
            left, scale = left * down, scale * down
            last = jnp.where(big, last + (1 << i), last)
        low = []
        for t, value in enumerate(values):
            whole = jnp.floor(value * scale + 0.5).astype(jnp.int32)
            whole = jnp.minimum(whole, half - 1) + half
            low.append(whole & 0xFFFF)
            last = last | ((whole >> 16) << (8 + extra * t))
        for j in range(tiles // 2):
            out_ref[d, j] = low[2 * j] | (low[2 * j + 1] << 16)
        out_ref[d, tiles // 2] = last


def add_products(sizes, tile_count, cols, packets, passed, acc, coded=False):
    blocks, per_p, per_q = sizes
    extent = packets[0].shape[1]
    sums = jax.ShapeDtypeStruct((tile_count * tile_count, extent // SEATS, extent), jnp.float32)
    made = sums
    if coded:
        shape = (tile_count * cols, tile_count // cols // 2 + 1) + sums.shape[1:]
        made = jax.ShapeDtypeStruct(shape, jnp.int32)
    operands = [*packets] + ([] if acc is None else [acc])
    return pl.pallas_call(
        functools.partial(product_kernel, sizes, tile_count, passed, acc is None, coded),
        out_shape=made,
        in_specs=[pl.BlockSpec(memory_space=pltpu.VMEM)] * len(operands),
        out_specs=pl.BlockSpec(memory_space=pltpu.VMEM),
        scratch_shapes=[
            pltpu.VMEM((SEATS, extent), jnp.int32),
            pltpu.SMEM((SEATS, extent), jnp.int32),
            pltpu.SemaphoreType.DMA,
        ]
        + [pltpu.VMEM(sums.shape, sums.dtype)] * coded,
        input_output_aliases={} if acc is None or coded else {len(operands) - 1: 0},
        cost_estimate=pl.CostEstimate(
            flops=2 * len(packets) * blocks * per_p * per_q * extent**3 // SEATS,
            bytes_accessed=len(packets) * (1 << 20),
            transcendentals=0,
        ),
        compiler_params=pltpu.CompilerParams(vmem_limit_bytes=24 << 20),
        name="products",
    )(*operands)


def finish_kernel(x_ref, out_ref):
    planes, seats, words, strip, extent = x_ref.shape
    tiles = 2 * (words - 1)
    extra = 24 // tiles
    half = 1 << (15 + extra)
    wholes = [None] * tiles
    for z in range(planes):
        last = x_ref[z, :, words - 1]
        scale = jnp.full(last.shape, 2.0 ** (1 - FLOOR) / half, jnp.float32)
        for i in range(7):
            scale = scale * jnp.where((last >> i) & 1 == 1, 2.0 ** (1 << i), 1.0)
        for t in range(tiles):
            whole = (x_ref[z, :, t // 2] >> (16 * (t % 2))) & 0xFFFF
            whole = whole | (((last >> (8 + extra * t)) & ((1 << extra) - 1)) << 16)
            value = (whole - half).astype(jnp.float32) * scale
            wholes[t] = value if z == 0 else wholes[t] + value
    for t in range(tiles):
        out_ref[:, t * extent:(t + 1) * extent] = wholes[t].reshape(seats * strip, extent).T


def body(p_tiles, p_cols, q_tiles, q_cols):
    blocks, per_p, extent, _ = p_tiles.shape
    per_q = q_tiles.shape[1]
    planes, cols = lax.axis_size("plane"), lax.axis_size("col")
    tile_count = planes * SEATS // cols
    strips = 2 * blocks * per_q * extent // SEATS
    whole = blocks * per_p * extent + 2 * SUB + strips
    seat = ("pair", "core", "col")

    own, *out = pl.pallas_call(
        functools.partial(pack_kernel, cols),
        out_shape=[
            jax.ShapeDtypeStruct((whole + passed * strips, extent), p_tiles.dtype)
            for passed in (0, 1, 1, 1, 0)
        ],
        in_specs=[pl.BlockSpec(memory_space=pltpu.SMEM)] * 2
        + [pl.BlockSpec(memory_space=pl.ANY), pl.BlockSpec(memory_space=pltpu.VMEM)],
        out_specs=[pl.BlockSpec(memory_space=pl.ANY)] * 5,
        scratch_shapes=[
            pltpu.VMEM((SEATS, strips // 2, extent), p_tiles.dtype),
            pltpu.VMEM((2 * SUB, extent), p_tiles.dtype),
            pltpu.SemaphoreType.DMA((26,)),
        ],
        name="pack",
    )(p_cols.T, q_cols, p_tiles.reshape(-1, extent), q_tiles)

    def along(values, step):
        hops = [(s, s ^ axes(s // cols % 2, cols)[step]) for s in range(SEATS)]
        return lax.ppermute(values, seat, hops)

    def across(values):
        return lax.ppermute(values, seat, [(s, s ^ cols) for s in range(SEATS)])

    def add(acc, packets, passed, coded=False):
        sizes = (blocks, per_p, per_q)
        return add_products(sizes, tile_count, cols, packets, passed, acc, coded)

    def opposite(values):
        return lax.ppermute(values, seat, [(s, s ^ (SEATS - 1 - cols)) for s in range(SEATS)])

    first = [along(out[step], step) for step in range(3)]
    beside = across(own)
    far = opposite(out[3])
    second = [along(rest_of(first[step], strips), (step + 1) % 3) for step in range(3)]
    acc = add(None, [own, beside] + first, [(0, 0), (0, 1), (1, 0), (1, 0), (1, 0)])
    first[2], second, acc = lax.optimization_barrier((first[2], second, acc))
    acc = add(
        acc,
        [far, across(far), across(first[0])] + second,
        [(0, 0), (0, 1), (1, 1), (0, 0), (0, 0), (0, 0)],
    )
    crossed = [across(each) for each in first[1:] + second]
    coded = add(acc, crossed, [(1, 1), (1, 1), (0, 1), (0, 1), (0, 1)], coded=True)
    every = ("plane",) + seat
    tiles = tile_count // cols
    landed = lax.all_to_all(coded, every, split_axis=0, concat_axis=0, tiled=True)
    return pl.pallas_call(
        finish_kernel,
        out_shape=jax.ShapeDtypeStruct((extent, tiles * extent), jnp.float32),
        compiler_params=pltpu.CompilerParams(vmem_limit_bytes=16 << 20),
        name="turn",
    )(landed.reshape((planes, SEATS) + landed.shape[1:]))


def solution(mesh):
    rows, cols = mesh.devices.shape
    pairs = SEATS // (2 * cols)
    shape = (rows // (2 * pairs), pairs, 2, cols)
    every = ("plane", "pair", "core", "col")
    inner = Mesh(mesh.devices.reshape(shape), every)
    placed = (
        P(every, None, None, None),
        P(every, None),
        P(every, None, None, None),
        P(every, None),
    )
    return jax.shard_map(
        body, mesh=inner, in_specs=placed, out_specs=P(every[:3], "col"), check_vma=False
    )
```

```python
import functools

import jax
import jax.numpy as jnp
from jax import lax
from jax.experimental import pallas as pl
from jax.experimental.pallas import tpu as pltpu
from jax.sharding import Mesh
from jax.sharding import PartitionSpec as P

SEATS = 16
SUB = 8
FLOOR = 100


def axes(core, cols):
    bits = [bit for bit in (1, 2, 4, 8) if bit != cols]
    return bits[core:] + bits[:core]


def pack_kernel(cols, p_ids, q_ids, p_ref, q_ref, *rest):
    out_refs, (strips, ids, sems) = rest[:-3], rest[-3:]
    blocks, per_q, extent, _ = q_ref.shape
    per_p = p_ids.shape[0]
    strip = extent // SEATS
    rows = per_q * strip
    height, tiles = blocks * rows, p_ref.shape[0]
    here = lax.axis_index(("pair", "core", "col"))
    core = lax.axis_index("core")
    paths = [[()], [(0,), (0, 1)], [(1,), (1, 2)], [(2,), (2, 0)], [(0, 1, 2)]]
    copies, later = [], []
    for path, out_ref in zip(paths, out_refs):
        spots = []
        for steps in path:
            masks = [sum(axes(c, cols)[step] for step in steps) for c in range(2)]
            to = here ^ jnp.where(core == 0, masks[0], masks[1])
            spots += [to, to ^ cols]
        place = 0
        for to in spots[:-2]:
            later.append((strips.at[to], out_ref.at[place:place + height]))
            place += height
        copies.append((p_ref, out_ref.at[place:place + tiles]))
        place += tiles
        later.append((ids, out_ref.at[place:place + 2 * SUB]))
        place += 2 * SUB
        for to in (spots[-1], spots[-2]):
            later.append((strips.at[to], out_ref.at[place:place + height]))
            place += height
    copies = [
        pltpu.make_async_copy(source, target, sems.at[n])
        for n, (source, target) in enumerate(copies + later)
    ]
    for copy in copies[:len(paths)]:
        copy.start()
    lane = lax.broadcasted_iota(jnp.int32, ids.shape, 1)
    words = jnp.zeros(ids.shape, jnp.int32)
    for f in range(blocks):
        for k in range(per_p + per_q):
            value = p_ids[k, f] if k < per_p else q_ids[f, k - per_p]
            words = jnp.where(lane == f * (per_p + per_q) + k, value, words)
    ids[...] = words.astype(ids.dtype)
    for f in range(blocks):
        flipped = [q_ref[f, k].astype(jnp.float32).T for k in range(per_q)]
        for j in range(SEATS):
            pieces = [tile[j * strip:(j + 1) * strip] for tile in flipped]
            strips[j, f * rows:(f + 1) * rows] = jnp.concatenate(pieces, axis=0).astype(strips.dtype)
    for copy in copies[len(paths):]:
        copy.start()
    for copy in copies:
        copy.wait()


def rest_kernel(skip, in_ref, out_ref, sem):
    copy = pltpu.make_async_copy(in_ref.at[skip:], out_ref, sem)
    copy.start()
    copy.wait()


def rest_of(packet, skip):
    height, extent = packet.shape
    return pl.pallas_call(
        functools.partial(rest_kernel, skip),
        out_shape=jax.ShapeDtypeStruct((height - skip, extent), packet.dtype),
        in_specs=[pl.BlockSpec(memory_space=pl.ANY)],
        out_specs=pl.BlockSpec(memory_space=pl.ANY),
        scratch_shapes=[pltpu.SemaphoreType.DMA],
        compiler_params=pltpu.CompilerParams(vmem_limit_bytes=1 << 20),
        name="rest_of_packet",
    )(packet)


def product_kernel(sizes, tile_count, passed, first, coded, *refs):
    count = len(passed)
    packets, (out_ref, wide_ids, ids, id_sem, *sums) = refs[:count], refs[count + (not first):]
    acc_ref = sums[0] if coded else out_ref
    blocks, per_p, per_q = sizes
    strip, extent = acc_ref.shape[1:]
    rows = per_q * strip
    places = []
    for i, (before, swapped) in enumerate(passed):
        tiles = 2 * before * blocks * rows
        indices = tiles + blocks * per_p * extent
        mine = swapped * blocks * rows if before else indices + 2 * SUB + (1 - swapped) * blocks * rows
        places.append((tiles, mine))
        wide_ids[i:i + 1] = packets[i][indices:indices + 2 * SUB].astype(jnp.int32)[:1]
    id_copy = pltpu.make_async_copy(wide_ids, ids, id_sem)
    id_copy.start()
    if first:
        acc_ref[...] = jnp.zeros_like(acc_ref)
    else:
        acc_ref[...] = refs[count][...]
    id_copy.wait()
    for i, (tiles, mine) in enumerate(places):
        for f in range(blocks):
            left = packets[i][mine + f * rows:mine + (f + 1) * rows]
            base = tiles + f * per_p * extent
            right = [packets[i][base + k * extent:base + (k + 1) * extent] for k in range(per_p)]
            product = jnp.dot(
                left, jnp.concatenate(right, axis=1), preferred_element_type=jnp.float32
            )
            start = f * (per_p + per_q)
            spots = [
                ids[i, start + k] * tile_count + ids[i, start + per_p + l]
                for k in range(per_p)
                for l in range(per_q)
            ]
            before = [acc_ref[spot] for spot in spots]
            for n, spot in enumerate(spots):
                k, l = divmod(n, per_q)
                term = product[l * strip:(l + 1) * strip, k * extent:(k + 1) * extent]
                acc_ref[spot] = before[n] + term
    if coded:
        code(acc_ref, out_ref, out_ref.shape[1] * 2 - 2)


def code(acc_ref, out_ref, tiles):
    extra = 24 // tiles
    half = 1 << (15 + extra)
    for d in range(out_ref.shape[0]):
        values = [acc_ref[d * tiles + t] for t in range(tiles)]
        left = functools.reduce(jnp.maximum, [jnp.abs(value) for value in values]) * 2.0**FLOOR
        scale = jnp.full(left.shape, 2.0 ** (FLOOR - 1) * half, jnp.float32)
        last = jnp.zeros(left.shape, jnp.int32)
        for i in reversed(range(7)):
            big = left >= 2.0 ** (1 << i)
            down = jnp.where(big, 2.0 ** -(1 << i), 1.0)
            left, scale = left * down, scale * down
            last = jnp.where(big, last + (1 << i), last)
        low = []
        for t, value in enumerate(values):
            whole = jnp.floor(value * scale + 0.5).astype(jnp.int32)
            whole = jnp.minimum(whole, half - 1) + half
            low.append(whole & 0xFFFF)
            last = last | ((whole >> 16) << (8 + extra * t))
        for j in range(tiles // 2):
            out_ref[d, j] = low[2 * j] | (low[2 * j + 1] << 16)
        out_ref[d, tiles // 2] = last


def add_products(sizes, tile_count, cols, packets, passed, acc, coded=False):
    blocks, per_p, per_q = sizes
    extent = packets[0].shape[1]
    sums = jax.ShapeDtypeStruct((tile_count * tile_count, extent // SEATS, extent), jnp.float32)
    made = sums
    if coded:
        shape = (tile_count * cols, tile_count // cols // 2 + 1) + sums.shape[1:]
        made = jax.ShapeDtypeStruct(shape, jnp.int32)
    operands = [*packets] + ([] if acc is None else [acc])
    return pl.pallas_call(
        functools.partial(product_kernel, sizes, tile_count, passed, acc is None, coded),
        out_shape=made,
        in_specs=[pl.BlockSpec(memory_space=pltpu.VMEM)] * len(operands),
        out_specs=pl.BlockSpec(memory_space=pltpu.VMEM),
        scratch_shapes=[
            pltpu.VMEM((SEATS, extent), jnp.int32),
            pltpu.SMEM((SEATS, extent), jnp.int32),
            pltpu.SemaphoreType.DMA,
        ]
        + [pltpu.VMEM(sums.shape, sums.dtype)] * coded,
        input_output_aliases={} if acc is None or coded else {len(operands) - 1: 0},
        cost_estimate=pl.CostEstimate(
            flops=2 * len(packets) * blocks * per_p * per_q * extent**3 // SEATS,
            bytes_accessed=len(packets) * (1 << 20),
            transcendentals=0,
        ),
        compiler_params=pltpu.CompilerParams(vmem_limit_bytes=24 << 20),
        name="products",
    )(*operands)


def finish_kernel(x_ref, out_ref):
    planes, seats, words, strip, extent = x_ref.shape
    tiles = 2 * (words - 1)
    extra = 24 // tiles
    half = 1 << (15 + extra)
    wholes = [None] * tiles
    for z in range(planes):
        last = x_ref[z, :, words - 1]
        scale = jnp.full(last.shape, 2.0 ** (1 - FLOOR) / half, jnp.float32)
        for i in range(7):
            scale = scale * jnp.where((last >> i) & 1 == 1, 2.0 ** (1 << i), 1.0)
        for t in range(tiles):
            whole = (x_ref[z, :, t // 2] >> (16 * (t % 2))) & 0xFFFF
            whole = whole | (((last >> (8 + extra * t)) & ((1 << extra) - 1)) << 16)
            value = (whole - half).astype(jnp.float32) * scale
            wholes[t] = value if z == 0 else wholes[t] + value
    for t in range(tiles):
        out_ref[:, t * extent:(t + 1) * extent] = wholes[t].reshape(seats * strip, extent).T


def body(p_tiles, p_cols, q_tiles, q_cols):
    blocks, per_p, extent, _ = p_tiles.shape
    per_q = q_tiles.shape[1]
    planes, cols = lax.axis_size("plane"), lax.axis_size("col")
    tile_count = planes * SEATS // cols
    strips = 2 * blocks * per_q * extent // SEATS
    whole = blocks * per_p * extent + 2 * SUB + strips
    seat = ("pair", "core", "col")

    own, *out = pl.pallas_call(
        functools.partial(pack_kernel, cols),
        out_shape=[
            jax.ShapeDtypeStruct((whole + passed * strips, extent), p_tiles.dtype)
            for passed in (0, 1, 1, 1, 0)
        ],
        in_specs=[pl.BlockSpec(memory_space=pltpu.SMEM)] * 2
        + [pl.BlockSpec(memory_space=pltpu.VMEM)] * 2,
        out_specs=[pl.BlockSpec(memory_space=pl.ANY)] * 5,
        scratch_shapes=[
            pltpu.VMEM((SEATS, strips // 2, extent), p_tiles.dtype),
            pltpu.VMEM((2 * SUB, extent), p_tiles.dtype),
            pltpu.SemaphoreType.DMA((26,)),
        ],
        name="pack",
    )(p_cols.T, q_cols, p_tiles.reshape(-1, extent), q_tiles)

    def along(values, step):
        hops = [(s, s ^ axes(s // cols % 2, cols)[step]) for s in range(SEATS)]
        return lax.ppermute(values, seat, hops)

    def across(values):
        return lax.ppermute(values, seat, [(s, s ^ cols) for s in range(SEATS)])

    def add(acc, packets, passed, coded=False):
        sizes = (blocks, per_p, per_q)
        return add_products(sizes, tile_count, cols, packets, passed, acc, coded)

    def opposite(values):
        return lax.ppermute(values, seat, [(s, s ^ (SEATS - 1 - cols)) for s in range(SEATS)])

    first = [along(out[step], step) for step in range(3)]
    beside = across(own)
    far = opposite(out[3])
    second = [along(rest_of(first[step], strips), (step + 1) % 3) for step in range(3)]
    acc = add(None, [own, beside] + first, [(0, 0), (0, 1), (1, 0), (1, 0), (1, 0)])
    first[2], second, acc = lax.optimization_barrier((first[2], second, acc))
    acc = add(
        acc,
        [far, across(far), across(first[0])] + second,
        [(0, 0), (0, 1), (1, 1), (0, 0), (0, 0), (0, 0)],
    )
    crossed = [across(each) for each in first[1:] + second]
    coded = add(acc, crossed, [(1, 1), (1, 1), (0, 1), (0, 1), (0, 1)], coded=True)
    every = ("plane",) + seat
    tiles = tile_count // cols
    landed = lax.all_to_all(coded, every, split_axis=0, concat_axis=0, tiled=True)
    return pl.pallas_call(
        finish_kernel,
        out_shape=jax.ShapeDtypeStruct((extent, tiles * extent), jnp.float32),
        compiler_params=pltpu.CompilerParams(vmem_limit_bytes=16 << 20),
        name="turn",
    )(landed.reshape((planes, SEATS) + landed.shape[1:]))


def solution(mesh):
    rows, cols = mesh.devices.shape
    pairs = SEATS // (2 * cols)
    shape = (rows // (2 * pairs), pairs, 2, cols)
    every = ("plane", "pair", "core", "col")
    inner = Mesh(mesh.devices.reshape(shape), every)
    placed = (
        P(every, None, None, None),
        P(every, None),
        P(every, None, None, None),
        P(every, None),
    )
    return jax.shard_map(
        body, mesh=inner, in_specs=placed, out_specs=P(every[:3], "col"), check_vma=False
    )
```

```python
import functools

import jax
import jax.numpy as jnp
from jax import lax
from jax.experimental import pallas as pl
from jax.experimental.pallas import tpu as pltpu
from jax.sharding import Mesh
from jax.sharding import PartitionSpec as P

SEATS = 16
SUB = 8
FLOOR = 100


def axes(core, cols):
    bits = [bit for bit in (1, 2, 4, 8) if bit != cols]
    return bits[core:] + bits[:core]


def pack_kernel(cols, p_ids, q_ids, p_ref, q_ref, own_ref, *rest):
    out_refs, strips = rest[:3], rest[3]
    blocks, per_q, extent, _ = q_ref.shape
    per_p = p_ids.shape[0]
    strip = extent // SEATS
    rows = per_q * strip
    lane = lax.broadcasted_iota(jnp.int32, (2 * SUB, extent), 1)
    ids = jnp.zeros((2 * SUB, extent), jnp.int32)
    for f in range(blocks):
        for k in range(per_p + per_q):
            value = p_ids[k, f] if k < per_p else q_ids[f, k - per_p]
            ids = jnp.where(lane == f * (per_p + per_q) + k, value, ids)
    ids = ids.astype(p_ref.dtype)
    for f in range(blocks):
        flipped = [q_ref[f, k].astype(jnp.float32).T for k in range(per_q)]
        for j in range(SEATS):
            pieces = [tile[j * strip:(j + 1) * strip] for tile in flipped]
            strips[j, f * rows:(f + 1) * rows] = jnp.concatenate(pieces, axis=0).astype(strips.dtype)
    here = lax.axis_index(("pair", "core", "col"))
    core = lax.axis_index("core")
    paths = [[()], [(0,), (0, 1), (0, 1, 2)], [(1,), (1, 2)], [(2,), (2, 0)]]
    for path, out_ref in zip(paths, (own_ref, *out_refs)):
        spots = []
        for steps in path:
            masks = [sum(axes(c, cols)[step] for step in steps) for c in range(2)]
            to = here ^ jnp.where(core == 0, masks[0], masks[1])
            spots += [to, to ^ cols]
        place = 0
        for to in spots[:-2]:
            out_ref[place:place + blocks * rows] = strips[to]
            place += blocks * rows
        for f in range(blocks):
            for k in range(per_p):
                out_ref[place:place + extent] = p_ref[f, k]
                place += extent
        out_ref[place:place + 2 * SUB] = ids
        place += 2 * SUB
        for to in (spots[-1], spots[-2]):
            out_ref[place:place + blocks * rows] = strips[to]
            place += blocks * rows


def rest_kernel(skip, in_ref, out_ref, sem):
    copy = pltpu.make_async_copy(in_ref.at[skip:], out_ref, sem)
    copy.start()
    copy.wait()


def rest_of(packet, skip):
    height, extent = packet.shape
    return pl.pallas_call(
        functools.partial(rest_kernel, skip),
        out_shape=jax.ShapeDtypeStruct((height - skip, extent), packet.dtype),
        in_specs=[pl.BlockSpec(memory_space=pl.ANY)],
        out_specs=pl.BlockSpec(memory_space=pl.ANY),
        scratch_shapes=[pltpu.SemaphoreType.DMA],
        compiler_params=pltpu.CompilerParams(vmem_limit_bytes=1 << 20),
        name="rest_of_packet",
    )(packet)


def product_kernel(sizes, tile_count, passed, first, coded, *refs):
    count = len(passed)
    packets, (out_ref, wide_ids, ids, id_sem, *sums) = refs[:count], refs[count + (not first):]
    acc_ref = sums[0] if coded else out_ref
    blocks, per_p, per_q = sizes
    strip, extent = acc_ref.shape[1:]
    rows = per_q * strip
    places = []
    for i, (before, swapped) in enumerate(passed):
        tiles = 2 * before * blocks * rows
        indices = tiles + blocks * per_p * extent
        mine = swapped * blocks * rows if before else indices + 2 * SUB + (1 - swapped) * blocks * rows
        places.append((tiles, mine))
        wide_ids[i:i + 1] = packets[i][indices:indices + 2 * SUB].astype(jnp.int32)[:1]
    id_copy = pltpu.make_async_copy(wide_ids, ids, id_sem)
    id_copy.start()
    if first:
        acc_ref[...] = jnp.zeros_like(acc_ref)
    else:
        acc_ref[...] = refs[count][...]
    id_copy.wait()
    for i, (tiles, mine) in enumerate(places):
        for f in range(blocks):
            left = packets[i][mine + f * rows:mine + (f + 1) * rows]
            base = tiles + f * per_p * extent
            right = [packets[i][base + k * extent:base + (k + 1) * extent] for k in range(per_p)]
            product = jnp.dot(
                left, jnp.concatenate(right, axis=1), preferred_element_type=jnp.float32
            )
            start = f * (per_p + per_q)
            spots = [
                ids[i, start + k] * tile_count + ids[i, start + per_p + l]
                for k in range(per_p)
                for l in range(per_q)
            ]
            before = [acc_ref[spot] for spot in spots]
            for n, spot in enumerate(spots):
                k, l = divmod(n, per_q)
                term = product[l * strip:(l + 1) * strip, k * extent:(k + 1) * extent]
                acc_ref[spot] = before[n] + term
    if coded:
        code(acc_ref, out_ref, out_ref.shape[1] * 2 - 2)


def code(acc_ref, out_ref, tiles):
    extra = 24 // tiles
    half = 1 << (15 + extra)
    for d in range(out_ref.shape[0]):
        values = [acc_ref[d * tiles + t] for t in range(tiles)]
        left = functools.reduce(jnp.maximum, [jnp.abs(value) for value in values]) * 2.0**FLOOR
        scale = jnp.full(left.shape, 2.0 ** (FLOOR - 1) * half, jnp.float32)
        last = jnp.zeros(left.shape, jnp.int32)
        for i in reversed(range(7)):
            big = left >= 2.0 ** (1 << i)
            down = jnp.where(big, 2.0 ** -(1 << i), 1.0)
            left, scale = left * down, scale * down
            last = jnp.where(big, last + (1 << i), last)
        low = []
        for t, value in enumerate(values):
            whole = jnp.floor(value * scale + 0.5).astype(jnp.int32)
            whole = jnp.minimum(whole, half - 1) + half
            low.append(whole & 0xFFFF)
            last = last | ((whole >> 16) << (8 + extra * t))
        for j in range(tiles // 2):
            out_ref[d, j] = low[2 * j] | (low[2 * j + 1] << 16)
        out_ref[d, tiles // 2] = last


def add_products(sizes, tile_count, cols, packets, passed, acc, coded=False):
    blocks, per_p, per_q = sizes
    extent = packets[0].shape[1]
    sums = jax.ShapeDtypeStruct((tile_count * tile_count, extent // SEATS, extent), jnp.float32)
    made = sums
    if coded:
        shape = (tile_count * cols, tile_count // cols // 2 + 1) + sums.shape[1:]
        made = jax.ShapeDtypeStruct(shape, jnp.int32)
    operands = [*packets] + ([] if acc is None else [acc])
    return pl.pallas_call(
        functools.partial(product_kernel, sizes, tile_count, passed, acc is None, coded),
        out_shape=made,
        in_specs=[pl.BlockSpec(memory_space=pltpu.VMEM)] * len(operands),
        out_specs=pl.BlockSpec(memory_space=pltpu.VMEM),
        scratch_shapes=[
            pltpu.VMEM((SEATS, extent), jnp.int32),
            pltpu.SMEM((SEATS, extent), jnp.int32),
            pltpu.SemaphoreType.DMA,
        ]
        + [pltpu.VMEM(sums.shape, sums.dtype)] * coded,
        input_output_aliases={} if acc is None or coded else {len(operands) - 1: 0},
        cost_estimate=pl.CostEstimate(
            flops=2 * len(packets) * blocks * per_p * per_q * extent**3 // SEATS,
            bytes_accessed=len(packets) * (1 << 20),
            transcendentals=0,
        ),
        compiler_params=pltpu.CompilerParams(vmem_limit_bytes=24 << 20),
        name="products",
    )(*operands)


def finish_kernel(x_ref, out_ref):
    planes, seats, words, strip, extent = x_ref.shape
    tiles = 2 * (words - 1)
    extra = 24 // tiles
    half = 1 << (15 + extra)
    wholes = [None] * tiles
    for z in range(planes):
        last = x_ref[z, :, words - 1]
        scale = jnp.full(last.shape, 2.0 ** (1 - FLOOR) / half, jnp.float32)
        for i in range(7):
            scale = scale * jnp.where((last >> i) & 1 == 1, 2.0 ** (1 << i), 1.0)
        for t in range(tiles):
            whole = (x_ref[z, :, t // 2] >> (16 * (t % 2))) & 0xFFFF
            whole = whole | (((last >> (8 + extra * t)) & ((1 << extra) - 1)) << 16)
            value = (whole - half).astype(jnp.float32) * scale
            wholes[t] = value if z == 0 else wholes[t] + value
    for t in range(tiles):
        out_ref[:, t * extent:(t + 1) * extent] = wholes[t].reshape(seats * strip, extent).T


def body(p_tiles, p_cols, q_tiles, q_cols):
    blocks, per_p, extent, _ = p_tiles.shape
    per_q = q_tiles.shape[1]
    planes, cols = lax.axis_size("plane"), lax.axis_size("col")
    tile_count = planes * SEATS // cols
    strips = 2 * blocks * per_q * extent // SEATS
    whole = blocks * per_p * extent + 2 * SUB + strips
    seat = ("pair", "core", "col")

    own, *out = pl.pallas_call(
        functools.partial(pack_kernel, cols),
        out_shape=[
            jax.ShapeDtypeStruct((whole + passed * strips, extent), p_tiles.dtype)
            for passed in (0, 2, 1, 1)
        ],
        in_specs=[pl.BlockSpec(memory_space=pltpu.SMEM)] * 2
        + [pl.BlockSpec(memory_space=pltpu.VMEM)] * 2,
        scratch_shapes=[pltpu.VMEM((SEATS, strips // 2, extent), p_tiles.dtype)],
        name="pack",
    )(p_cols.T, q_cols, p_tiles, q_tiles)

    def along(values, step):
        hops = [(s, s ^ axes(s // cols % 2, cols)[step]) for s in range(SEATS)]
        return lax.ppermute(values, seat, hops)

    def across(values):
        return lax.ppermute(values, seat, [(s, s ^ cols) for s in range(SEATS)])

    def add(acc, packets, passed, coded=False):
        sizes = (blocks, per_p, per_q)
        return add_products(sizes, tile_count, cols, packets, passed, acc, coded)

    first = [along(out[step], step) for step in range(3)]
    second = [along(rest_of(first[step], strips), (step + 1) % 3) for step in range(3)]
    third = along(rest_of(second[0], strips), 2)
    beside = across(own)
    acc = add(None, [own, beside] + first, [(0, 0), (0, 1), (2, 0), (1, 0), (1, 0)])
    first[2], acc = lax.optimization_barrier((first[2], acc))
    crossed = [across(each) for each in first]
    second[1:], acc = lax.optimization_barrier((second[1:], acc))
    more = [across(each) for each in second]
    acc = add(acc, second + crossed[:2], [(1, 0), (0, 0), (0, 0), (2, 1), (1, 1)])
    third, acc = lax.optimization_barrier((third, acc))
    beside = across(third)
    acc = add(acc, [third, crossed[2]] + more, [(0, 0), (1, 1), (1, 1), (0, 1), (0, 1)])
    coded = add(acc, [beside], [(0, 1)], coded=True)
    every = ("plane",) + seat
    tiles = tile_count // cols
    landed = lax.all_to_all(coded, every, split_axis=0, concat_axis=0, tiled=True)
    return pl.pallas_call(
        finish_kernel,
        out_shape=jax.ShapeDtypeStruct((extent, tiles * extent), jnp.float32),
        compiler_params=pltpu.CompilerParams(vmem_limit_bytes=16 << 20),
        name="turn",
    )(landed.reshape((planes, SEATS) + landed.shape[1:]))


def solution(mesh):
    rows, cols = mesh.devices.shape
    pairs = SEATS // (2 * cols)
    shape = (rows // (2 * pairs), pairs, 2, cols)
    every = ("plane", "pair", "core", "col")
    inner = Mesh(mesh.devices.reshape(shape), every)
    placed = (
        P(every, None, None, None),
        P(every, None),
        P(every, None, None, None),
        P(every, None),
    )
    return jax.shard_map(
        body, mesh=inner, in_specs=placed, out_specs=P(every[:3], "col"), check_vma=False
    )
```

```python
import functools

import jax
import jax.numpy as jnp
from jax import lax
from jax.experimental import pallas as pl
from jax.experimental.pallas import tpu as pltpu
from jax.sharding import Mesh
from jax.sharding import PartitionSpec as P

SEATS = 16
SUB = 8
FLOOR = 100


def axes(core, cols):
    bits = [bit for bit in (1, 2, 4, 8) if bit != cols]
    return bits[core:] + bits[:core]


def pack_kernel(cols, p_ids, q_ids, p_ref, q_ref, own_ref, *rest):
    out_refs, strips = rest[:4], rest[4]
    blocks, per_q, extent, _ = q_ref.shape
    per_p = p_ids.shape[0]
    strip = extent // SEATS
    rows = per_q * strip
    lane = lax.broadcasted_iota(jnp.int32, (2 * SUB, extent), 1)
    ids = jnp.zeros((2 * SUB, extent), jnp.int32)
    for f in range(blocks):
        for k in range(per_p + per_q):
            value = p_ids[k, f] if k < per_p else q_ids[f, k - per_p]
            ids = jnp.where(lane == f * (per_p + per_q) + k, value, ids)
    ids = ids.astype(p_ref.dtype)
    for f in range(blocks):
        flipped = [q_ref[f, k].astype(jnp.float32).T for k in range(per_q)]
        for j in range(SEATS):
            pieces = [tile[j * strip:(j + 1) * strip] for tile in flipped]
            strips[j, f * rows:(f + 1) * rows] = jnp.concatenate(pieces, axis=0).astype(strips.dtype)
    here = lax.axis_index(("pair", "core", "col"))
    core = lax.axis_index("core")
    paths = [[()], [(0,), (0, 1)], [(1,), (1, 2)], [(2,), (2, 0)], [(0, 1, 2)]]
    for path, out_ref in zip(paths, (own_ref, *out_refs)):
        spots = []
        for steps in path:
            masks = [sum(axes(c, cols)[step] for step in steps) for c in range(2)]
            to = here ^ jnp.where(core == 0, masks[0], masks[1])
            spots += [to, to ^ cols]
        place = 0
        for to in spots[:-2]:
            out_ref[place:place + blocks * rows] = strips[to]
            place += blocks * rows
        for f in range(blocks):
            for k in range(per_p):
                out_ref[place:place + extent] = p_ref[f, k]
                place += extent
        out_ref[place:place + 2 * SUB] = ids
        place += 2 * SUB
        for to in (spots[-1], spots[-2]):
            out_ref[place:place + blocks * rows] = strips[to]
            place += blocks * rows


def rest_kernel(skip, in_ref, out_ref, sem):
    copy = pltpu.make_async_copy(in_ref.at[skip:], out_ref, sem)
    copy.start()
    copy.wait()


def rest_of(packet, skip):
    height, extent = packet.shape
    return pl.pallas_call(
        functools.partial(rest_kernel, skip),
        out_shape=jax.ShapeDtypeStruct((height - skip, extent), packet.dtype),
        in_specs=[pl.BlockSpec(memory_space=pl.ANY)],
        out_specs=pl.BlockSpec(memory_space=pl.ANY),
        scratch_shapes=[pltpu.SemaphoreType.DMA],
        compiler_params=pltpu.CompilerParams(vmem_limit_bytes=1 << 20),
        name="rest_of_packet",
    )(packet)


def product_kernel(sizes, tile_count, passed, first, coded, *refs):
    count = len(passed)
    packets, (out_ref, wide_ids, ids, id_sem, *sums) = refs[:count], refs[count + (not first):]
    acc_ref = sums[0] if coded else out_ref
    blocks, per_p, per_q = sizes
    strip, extent = acc_ref.shape[1:]
    rows = per_q * strip
    places = []
    for i, (before, swapped) in enumerate(passed):
        tiles = 2 * before * blocks * rows
        indices = tiles + blocks * per_p * extent
        mine = swapped * blocks * rows if before else indices + 2 * SUB + (1 - swapped) * blocks * rows
        places.append((tiles, mine))
        wide_ids[i:i + 1] = packets[i][indices:indices + 2 * SUB].astype(jnp.int32)[:1]
    id_copy = pltpu.make_async_copy(wide_ids, ids, id_sem)
    id_copy.start()
    if first:
        acc_ref[...] = jnp.zeros_like(acc_ref)
    else:
        acc_ref[...] = refs[count][...]
    id_copy.wait()
    for i, (tiles, mine) in enumerate(places):
        for f in range(blocks):
            left = packets[i][mine + f * rows:mine + (f + 1) * rows]
            base = tiles + f * per_p * extent
            right = [packets[i][base + k * extent:base + (k + 1) * extent] for k in range(per_p)]
            product = jnp.dot(
                left, jnp.concatenate(right, axis=1), preferred_element_type=jnp.float32
            )
            start = f * (per_p + per_q)
            spots = [
                ids[i, start + k] * tile_count + ids[i, start + per_p + l]
                for k in range(per_p)
                for l in range(per_q)
            ]
            before = [acc_ref[spot] for spot in spots]
            for n, spot in enumerate(spots):
                k, l = divmod(n, per_q)
                term = product[l * strip:(l + 1) * strip, k * extent:(k + 1) * extent]
                acc_ref[spot] = before[n] + term
    if coded:
        code(acc_ref, out_ref, out_ref.shape[1] * 2 - 2)


def code(acc_ref, out_ref, tiles):
    extra = 24 // tiles
    half = 1 << (15 + extra)
    for d in range(out_ref.shape[0]):
        values = [acc_ref[d * tiles + t] for t in range(tiles)]
        left = functools.reduce(jnp.maximum, [jnp.abs(value) for value in values]) * 2.0**FLOOR
        scale = jnp.full(left.shape, 2.0 ** (FLOOR - 1) * half, jnp.float32)
        last = jnp.zeros(left.shape, jnp.int32)
        for i in reversed(range(7)):
            big = left >= 2.0 ** (1 << i)
            down = jnp.where(big, 2.0 ** -(1 << i), 1.0)
            left, scale = left * down, scale * down
            last = jnp.where(big, last + (1 << i), last)
        low = []
        for t, value in enumerate(values):
            whole = jnp.floor(value * scale + 0.5).astype(jnp.int32)
            whole = jnp.minimum(whole, half - 1) + half
            low.append(whole & 0xFFFF)
            last = last | ((whole >> 16) << (8 + extra * t))
        for j in range(tiles // 2):
            out_ref[d, j] = low[2 * j] | (low[2 * j + 1] << 16)
        out_ref[d, tiles // 2] = last


def add_products(sizes, tile_count, cols, packets, passed, acc, coded=False):
    blocks, per_p, per_q = sizes
    extent = packets[0].shape[1]
    sums = jax.ShapeDtypeStruct((tile_count * tile_count, extent // SEATS, extent), jnp.float32)
    made = sums
    if coded:
        shape = (tile_count * cols, tile_count // cols // 2 + 1) + sums.shape[1:]
        made = jax.ShapeDtypeStruct(shape, jnp.int32)
    operands = [*packets] + ([] if acc is None else [acc])
    return pl.pallas_call(
        functools.partial(product_kernel, sizes, tile_count, passed, acc is None, coded),
        out_shape=made,
        in_specs=[pl.BlockSpec(memory_space=pltpu.VMEM)] * len(operands),
        out_specs=pl.BlockSpec(memory_space=pltpu.VMEM),
        scratch_shapes=[
            pltpu.VMEM((SEATS, extent), jnp.int32),
            pltpu.SMEM((SEATS, extent), jnp.int32),
            pltpu.SemaphoreType.DMA,
        ]
        + [pltpu.VMEM(sums.shape, sums.dtype)] * coded,
        input_output_aliases={} if acc is None or coded else {len(operands) - 1: 0},
        cost_estimate=pl.CostEstimate(
            flops=2 * len(packets) * blocks * per_p * per_q * extent**3 // SEATS,
            bytes_accessed=len(packets) * (1 << 20),
            transcendentals=0,
        ),
        compiler_params=pltpu.CompilerParams(vmem_limit_bytes=24 << 20),
        name="products",
    )(*operands)


def finish_kernel(x_ref, out_ref):
    planes, seats, words, strip, extent = x_ref.shape
    tiles = 2 * (words - 1)
    extra = 24 // tiles
    half = 1 << (15 + extra)
    wholes = [None] * tiles
    for z in range(planes):
        last = x_ref[z, :, words - 1]
        scale = jnp.full(last.shape, 2.0 ** (1 - FLOOR) / half, jnp.float32)
        for i in range(7):
            scale = scale * jnp.where((last >> i) & 1 == 1, 2.0 ** (1 << i), 1.0)
        for t in range(tiles):
            whole = (x_ref[z, :, t // 2] >> (16 * (t % 2))) & 0xFFFF
            whole = whole | (((last >> (8 + extra * t)) & ((1 << extra) - 1)) << 16)
            value = (whole - half).astype(jnp.float32) * scale
            wholes[t] = value if z == 0 else wholes[t] + value
    for t in range(tiles):
        out_ref[:, t * extent:(t + 1) * extent] = wholes[t].reshape(seats * strip, extent).T


def body(p_tiles, p_cols, q_tiles, q_cols):
    blocks, per_p, extent, _ = p_tiles.shape
    per_q = q_tiles.shape[1]
    planes, cols = lax.axis_size("plane"), lax.axis_size("col")
    tile_count = planes * SEATS // cols
    strips = 2 * blocks * per_q * extent // SEATS
    whole = blocks * per_p * extent + 2 * SUB + strips
    seat = ("pair", "core", "col")

    own, *out = pl.pallas_call(
        functools.partial(pack_kernel, cols),
        out_shape=[
            jax.ShapeDtypeStruct((whole + passed * strips, extent), p_tiles.dtype)
            for passed in (0, 1, 1, 1, 0)
        ],
        in_specs=[pl.BlockSpec(memory_space=pltpu.SMEM)] * 2
        + [pl.BlockSpec(memory_space=pltpu.VMEM)] * 2,
        scratch_shapes=[pltpu.VMEM((SEATS, strips // 2, extent), p_tiles.dtype)],
        name="pack",
    )(p_cols.T, q_cols, p_tiles, q_tiles)

    def along(values, step):
        hops = [(s, s ^ axes(s // cols % 2, cols)[step]) for s in range(SEATS)]
        return lax.ppermute(values, seat, hops)

    def across(values):
        return lax.ppermute(values, seat, [(s, s ^ cols) for s in range(SEATS)])

    def add(acc, packets, passed, coded=False):
        sizes = (blocks, per_p, per_q)
        return add_products(sizes, tile_count, cols, packets, passed, acc, coded)

    def opposite(values):
        return lax.ppermute(values, seat, [(s, s ^ (SEATS - 1 - cols)) for s in range(SEATS)])

    first = [along(out[step], step) for step in range(3)]
    beside = across(own)
    far = opposite(out[3])
    second = [along(rest_of(first[step], strips), (step + 1) % 3) for step in range(3)]
    acc = add(None, [own, beside] + first, [(0, 0), (0, 1), (1, 0), (1, 0), (1, 0)])
    first[2], far, second, acc = lax.optimization_barrier((first[2], far, second, acc))
    crossed = [across(each) for each in first + [far] + second]
    acc = add(acc, crossed[:2] + [far] + second, [(1, 1), (1, 1), (0, 0), (0, 0), (0, 0), (0, 0)])
    acc = add(acc, crossed[2:5], [(1, 1), (0, 1), (0, 1)])
    coded = add(acc, crossed[5:], [(0, 1), (0, 1)], coded=True)
    every = ("plane",) + seat
    tiles = tile_count // cols
    landed = lax.all_to_all(coded, every, split_axis=0, concat_axis=0, tiled=True)
    return pl.pallas_call(
        finish_kernel,
        out_shape=jax.ShapeDtypeStruct((extent, tiles * extent), jnp.float32),
        compiler_params=pltpu.CompilerParams(vmem_limit_bytes=16 << 20),
        name="turn",
    )(landed.reshape((planes, SEATS) + landed.shape[1:]))


def solution(mesh):
    rows, cols = mesh.devices.shape
    pairs = SEATS // (2 * cols)
    shape = (rows // (2 * pairs), pairs, 2, cols)
    every = ("plane", "pair", "core", "col")
    inner = Mesh(mesh.devices.reshape(shape), every)
    placed = (
        P(every, None, None, None),
        P(every, None),
        P(every, None, None, None),
        P(every, None),
    )
    return jax.shard_map(
        body, mesh=inner, in_specs=placed, out_specs=P(every[:3], "col"), check_vma=False
    )
```

```python
import functools

import jax
import jax.numpy as jnp
from jax import lax
from jax.experimental import pallas as pl
from jax.experimental.pallas import tpu as pltpu
from jax.sharding import Mesh
from jax.sharding import PartitionSpec as P

SEATS = 16
SUB = 8
FLOOR = 100


def axes(core, cols):
    bits = [bit for bit in (1, 2, 4, 8) if bit != cols]
    return bits[core:] + bits[:core]


def pack_kernel(cols, p_ids, q_ids, p_ref, q_ref, own_ref, *rest):
    out_refs, strips = rest[:4], rest[4]
    blocks, per_q, extent, _ = q_ref.shape
    per_p = p_ids.shape[0]
    strip = extent // SEATS
    rows = per_q * strip
    lane = lax.broadcasted_iota(jnp.int32, (2 * SUB, extent), 1)
    ids = jnp.zeros((2 * SUB, extent), jnp.int32)
    for f in range(blocks):
        for k in range(per_p + per_q):
            value = p_ids[k, f] if k < per_p else q_ids[f, k - per_p]
            ids = jnp.where(lane == f * (per_p + per_q) + k, value, ids)
    ids = ids.astype(p_ref.dtype)
    for f in range(blocks):
        flipped = [q_ref[f, k].astype(jnp.float32).T for k in range(per_q)]
        for j in range(SEATS):
            pieces = [tile[j * strip:(j + 1) * strip] for tile in flipped]
            strips[j, f * rows:(f + 1) * rows] = jnp.concatenate(pieces, axis=0).astype(strips.dtype)
    here = lax.axis_index(("pair", "core", "col"))
    core = lax.axis_index("core")
    paths = [[()], [(0,), (0, 1)], [(1,), (1, 2)], [(2,), (2, 0)], [(0, 1, 2)]]
    for path, out_ref in zip(paths, (own_ref, *out_refs)):
        spots = []
        for steps in path:
            masks = [sum(axes(c, cols)[step] for step in steps) for c in range(2)]
            to = here ^ jnp.where(core == 0, masks[0], masks[1])
            spots += [to, to ^ cols]
        place = 0
        for to in spots[:-2]:
            out_ref[place:place + blocks * rows] = strips[to]
            place += blocks * rows
        for f in range(blocks):
            for k in range(per_p):
                out_ref[place:place + extent] = p_ref[f, k]
                place += extent
        out_ref[place:place + 2 * SUB] = ids
        place += 2 * SUB
        for to in (spots[-1], spots[-2]):
            out_ref[place:place + blocks * rows] = strips[to]
            place += blocks * rows


def rest_kernel(skip, in_ref, out_ref, sem):
    copy = pltpu.make_async_copy(in_ref.at[skip:], out_ref, sem)
    copy.start()
    copy.wait()


def rest_of(packet, skip):
    height, extent = packet.shape
    return pl.pallas_call(
        functools.partial(rest_kernel, skip),
        out_shape=jax.ShapeDtypeStruct((height - skip, extent), packet.dtype),
        in_specs=[pl.BlockSpec(memory_space=pl.ANY)],
        out_specs=pl.BlockSpec(memory_space=pl.ANY),
        scratch_shapes=[pltpu.SemaphoreType.DMA],
        compiler_params=pltpu.CompilerParams(vmem_limit_bytes=1 << 20),
        name="rest_of_packet",
    )(packet)


def product_kernel(sizes, tile_count, passed, first, coded, *refs):
    count = len(passed)
    packets, (out_ref, wide_ids, ids, id_sem, *sums) = refs[:count], refs[count + (not first):]
    acc_ref = sums[0] if coded else out_ref
    blocks, per_p, per_q = sizes
    strip, extent = acc_ref.shape[1:]
    rows = per_q * strip
    places = []
    for i, (before, swapped) in enumerate(passed):
        tiles = 2 * before * blocks * rows
        indices = tiles + blocks * per_p * extent
        mine = swapped * blocks * rows if before else indices + 2 * SUB + (1 - swapped) * blocks * rows
        places.append((tiles, mine))
        wide_ids[i:i + 1] = packets[i][indices:indices + 2 * SUB].astype(jnp.int32)[:1]
    id_copy = pltpu.make_async_copy(wide_ids, ids, id_sem)
    id_copy.start()
    if first:
        acc_ref[...] = jnp.zeros_like(acc_ref)
    else:
        acc_ref[...] = refs[count][...]
    id_copy.wait()
    for i, (tiles, mine) in enumerate(places):
        for f in range(blocks):
            left = packets[i][mine + f * rows:mine + (f + 1) * rows]
            base = tiles + f * per_p * extent
            right = [packets[i][base + k * extent:base + (k + 1) * extent] for k in range(per_p)]
            product = jnp.dot(
                left, jnp.concatenate(right, axis=1), preferred_element_type=jnp.float32
            )
            start = f * (per_p + per_q)
            spots = [
                ids[i, start + k] * tile_count + ids[i, start + per_p + l]
                for k in range(per_p)
                for l in range(per_q)
            ]
            before = [acc_ref[spot] for spot in spots]
            for n, spot in enumerate(spots):
                k, l = divmod(n, per_q)
                term = product[l * strip:(l + 1) * strip, k * extent:(k + 1) * extent]
                acc_ref[spot] = before[n] + term
    if coded:
        code(acc_ref, out_ref, out_ref.shape[1] * 2 - 2)


def code(acc_ref, out_ref, tiles):
    extra = 24 // tiles
    half = 1 << (15 + extra)
    for d in range(out_ref.shape[0]):
        values = [acc_ref[d * tiles + t] for t in range(tiles)]
        left = functools.reduce(jnp.maximum, [jnp.abs(value) for value in values]) * 2.0**FLOOR
        scale = jnp.full(left.shape, 2.0 ** (FLOOR - 1) * half, jnp.float32)
        last = jnp.zeros(left.shape, jnp.int32)
        for i in reversed(range(7)):
            big = left >= 2.0 ** (1 << i)
            down = jnp.where(big, 2.0 ** -(1 << i), 1.0)
            left, scale = left * down, scale * down
            last = jnp.where(big, last + (1 << i), last)
        low = []
        for t, value in enumerate(values):
            whole = jnp.floor(value * scale + 0.5).astype(jnp.int32)
            whole = jnp.minimum(whole, half - 1) + half
            low.append(whole & 0xFFFF)
            last = last | ((whole >> 16) << (8 + extra * t))
        for j in range(tiles // 2):
            out_ref[d, j] = low[2 * j] | (low[2 * j + 1] << 16)
        out_ref[d, tiles // 2] = last


def add_products(sizes, tile_count, cols, packets, passed, acc, coded=False):
    blocks, per_p, per_q = sizes
    extent = packets[0].shape[1]
    sums = jax.ShapeDtypeStruct((tile_count * tile_count, extent // SEATS, extent), jnp.float32)
    made = sums
    if coded:
        shape = (tile_count * cols, tile_count // cols // 2 + 1) + sums.shape[1:]
        made = jax.ShapeDtypeStruct(shape, jnp.int32)
    operands = [*packets] + ([] if acc is None else [acc])
    return pl.pallas_call(
        functools.partial(product_kernel, sizes, tile_count, passed, acc is None, coded),
        out_shape=made,
        in_specs=[pl.BlockSpec(memory_space=pltpu.VMEM)] * len(operands),
        out_specs=pl.BlockSpec(memory_space=pltpu.VMEM),
        scratch_shapes=[
            pltpu.VMEM((SEATS, extent), jnp.int32),
            pltpu.SMEM((SEATS, extent), jnp.int32),
            pltpu.SemaphoreType.DMA,
        ]
        + [pltpu.VMEM(sums.shape, sums.dtype)] * coded,
        input_output_aliases={} if acc is None or coded else {len(operands) - 1: 0},
        cost_estimate=pl.CostEstimate(
            flops=2 * len(packets) * blocks * per_p * per_q * extent**3 // SEATS,
            bytes_accessed=len(packets) * (1 << 20),
            transcendentals=0,
        ),
        compiler_params=pltpu.CompilerParams(vmem_limit_bytes=24 << 20),
        name="products",
    )(*operands)


def finish_kernel(x_ref, out_ref):
    planes, seats, words, strip, extent = x_ref.shape
    tiles = 2 * (words - 1)
    extra = 24 // tiles
    half = 1 << (15 + extra)
    wholes = [None] * tiles
    for z in range(planes):
        last = x_ref[z, :, words - 1]
        scale = jnp.full(last.shape, 2.0 ** (1 - FLOOR) / half, jnp.float32)
        for i in range(7):
            scale = scale * jnp.where((last >> i) & 1 == 1, 2.0 ** (1 << i), 1.0)
        for t in range(tiles):
            whole = (x_ref[z, :, t // 2] >> (16 * (t % 2))) & 0xFFFF
            whole = whole | (((last >> (8 + extra * t)) & ((1 << extra) - 1)) << 16)
            value = (whole - half).astype(jnp.float32) * scale
            wholes[t] = value if z == 0 else wholes[t] + value
    for t in range(tiles):
        out_ref[:, t * extent:(t + 1) * extent] = wholes[t].reshape(seats * strip, extent).T


def body(p_tiles, p_cols, q_tiles, q_cols):
    blocks, per_p, extent, _ = p_tiles.shape
    per_q = q_tiles.shape[1]
    planes, cols = lax.axis_size("plane"), lax.axis_size("col")
    tile_count = planes * SEATS // cols
    strips = 2 * blocks * per_q * extent // SEATS
    whole = blocks * per_p * extent + 2 * SUB + strips
    seat = ("pair", "core", "col")

    own, *out = pl.pallas_call(
        functools.partial(pack_kernel, cols),
        out_shape=[
            jax.ShapeDtypeStruct((whole + passed * strips, extent), p_tiles.dtype)
            for passed in (0, 1, 1, 1, 0)
        ],
        in_specs=[pl.BlockSpec(memory_space=pltpu.SMEM)] * 2
        + [pl.BlockSpec(memory_space=pltpu.VMEM)] * 2,
        scratch_shapes=[pltpu.VMEM((SEATS, strips // 2, extent), p_tiles.dtype)],
        name="pack",
    )(p_cols.T, q_cols, p_tiles, q_tiles)

    def along(values, step):
        hops = [(s, s ^ axes(s // cols % 2, cols)[step]) for s in range(SEATS)]
        return lax.ppermute(values, seat, hops)

    def across(values):
        return lax.ppermute(values, seat, [(s, s ^ cols) for s in range(SEATS)])

    def add(acc, packets, passed, coded=False):
        sizes = (blocks, per_p, per_q)
        return add_products(sizes, tile_count, cols, packets, passed, acc, coded)

    def opposite(values):
        return lax.ppermute(values, seat, [(s, s ^ (SEATS - 1 - cols)) for s in range(SEATS)])

    first = [along(out[step], step) for step in range(3)]
    beside = across(own)
    far = opposite(out[3])
    second = [along(rest_of(first[step], strips), (step + 1) % 3) for step in range(3)]
    acc = add(None, [own, beside] + first, [(0, 0), (0, 1), (1, 0), (1, 0), (1, 0)])
    first[2], far, second, acc = lax.optimization_barrier((first[2], far, second, acc))
    crossed = [across(each) for each in first]
    acc = add(acc, crossed[:2] + [far] + second, [(1, 1), (1, 1), (0, 0), (0, 0), (0, 0), (0, 0)])
    crossed = crossed[2:] + [across(each) for each in [far] + second]
    coded = add(acc, crossed, [(1, 1), (0, 1), (0, 1), (0, 1), (0, 1)], coded=True)
    every = ("plane",) + seat
    tiles = tile_count // cols
    landed = lax.all_to_all(coded, every, split_axis=0, concat_axis=0, tiled=True)
    return pl.pallas_call(
        finish_kernel,
        out_shape=jax.ShapeDtypeStruct((extent, tiles * extent), jnp.float32),
        compiler_params=pltpu.CompilerParams(vmem_limit_bytes=16 << 20),
        name="turn",
    )(landed.reshape((planes, SEATS) + landed.shape[1:]))


def solution(mesh):
    rows, cols = mesh.devices.shape
    pairs = SEATS // (2 * cols)
    shape = (rows // (2 * pairs), pairs, 2, cols)
    every = ("plane", "pair", "core", "col")
    inner = Mesh(mesh.devices.reshape(shape), every)
    placed = (
        P(every, None, None, None),
        P(every, None),
        P(every, None, None, None),
        P(every, None),
    )
    return jax.shard_map(
        body, mesh=inner, in_specs=placed, out_specs=P(every[:3], "col"), check_vma=False
    )
```

```python
import functools

import jax
import jax.numpy as jnp
from jax import lax
from jax.experimental import pallas as pl
from jax.experimental.pallas import tpu as pltpu
from jax.sharding import Mesh
from jax.sharding import PartitionSpec as P

SEATS = 16
SUB = 8
FLOOR = 100


def axes(core, cols):
    bits = [bit for bit in (1, 2, 4, 8) if bit != cols]
    return bits[core:] + bits[:core]


def pack_kernel(cols, p_ids, q_ids, p_ref, q_ref, own_ref, *rest):
    out_refs, strips = rest[:4], rest[4]
    blocks, per_q, extent, _ = q_ref.shape
    per_p = p_ids.shape[0]
    strip = extent // SEATS
    rows = per_q * strip
    lane = lax.broadcasted_iota(jnp.int32, (2 * SUB, extent), 1)
    ids = jnp.zeros((2 * SUB, extent), jnp.int32)
    for f in range(blocks):
        for k in range(per_p + per_q):
            value = p_ids[k, f] if k < per_p else q_ids[f, k - per_p]
            ids = jnp.where(lane == f * (per_p + per_q) + k, value, ids)
    ids = ids.astype(p_ref.dtype)
    for f in range(blocks):
        flipped = [q_ref[f, k].astype(jnp.float32).T for k in range(per_q)]
        for j in range(SEATS):
            pieces = [tile[j * strip:(j + 1) * strip] for tile in flipped]
            strips[j, f * rows:(f + 1) * rows] = jnp.concatenate(pieces, axis=0).astype(strips.dtype)
    here = lax.axis_index(("pair", "core", "col"))
    core = lax.axis_index("core")
    paths = [[()], [(0,), (0, 1)], [(1,), (1, 2)], [(2,), (2, 0)], [(0, 1, 2)]]
    for path, out_ref in zip(paths, (own_ref, *out_refs)):
        spots = []
        for steps in path:
            masks = [sum(axes(c, cols)[step] for step in steps) for c in range(2)]
            to = here ^ jnp.where(core == 0, masks[0], masks[1])
            spots += [to, to ^ cols]
        place = 0
        for to in spots[:-2]:
            out_ref[place:place + blocks * rows] = strips[to]
            place += blocks * rows
        for f in range(blocks):
            for k in range(per_p):
                out_ref[place:place + extent] = p_ref[f, k]
                place += extent
        out_ref[place:place + 2 * SUB] = ids
        place += 2 * SUB
        for to in (spots[-1], spots[-2]):
            out_ref[place:place + blocks * rows] = strips[to]
            place += blocks * rows


def rest_kernel(skip, in_ref, out_ref, sem):
    copy = pltpu.make_async_copy(in_ref.at[skip:], out_ref, sem)
    copy.start()
    copy.wait()


def rest_of(packet, skip):
    height, extent = packet.shape
    return pl.pallas_call(
        functools.partial(rest_kernel, skip),
        out_shape=jax.ShapeDtypeStruct((height - skip, extent), packet.dtype),
        in_specs=[pl.BlockSpec(memory_space=pl.ANY)],
        out_specs=pl.BlockSpec(memory_space=pl.ANY),
        scratch_shapes=[pltpu.SemaphoreType.DMA],
        compiler_params=pltpu.CompilerParams(vmem_limit_bytes=1 << 20),
        name="rest_of_packet",
    )(packet)


def product_kernel(sizes, tile_count, passed, first, coded, *refs):
    count = len(passed)
    packets, (out_ref, wide_ids, ids, id_sem, *sums) = refs[:count], refs[count + (not first):]
    acc_ref = sums[0] if coded else out_ref
    blocks, per_p, per_q = sizes
    strip, extent = acc_ref.shape[1:]
    rows = per_q * strip
    places = []
    for i, (before, swapped) in enumerate(passed):
        tiles = 2 * before * blocks * rows
        indices = tiles + blocks * per_p * extent
        mine = swapped * blocks * rows if before else indices + 2 * SUB + (1 - swapped) * blocks * rows
        places.append((tiles, mine))
        wide_ids[i:i + 1] = packets[i][indices:indices + 2 * SUB].astype(jnp.int32)[:1]
    id_copy = pltpu.make_async_copy(wide_ids, ids, id_sem)
    id_copy.start()
    if first:
        acc_ref[...] = jnp.zeros_like(acc_ref)
    else:
        acc_ref[...] = refs[count][...]
    id_copy.wait()
    for i, (tiles, mine) in enumerate(places):
        for f in range(blocks):
            left = packets[i][mine + f * rows:mine + (f + 1) * rows]
            base = tiles + f * per_p * extent
            right = [packets[i][base + k * extent:base + (k + 1) * extent] for k in range(per_p)]
            product = jnp.dot(
                left, jnp.concatenate(right, axis=1), preferred_element_type=jnp.float32
            )
            start = f * (per_p + per_q)
            spots = [
                ids[i, start + k] * tile_count + ids[i, start + per_p + l]
                for k in range(per_p)
                for l in range(per_q)
            ]
            before = [acc_ref[spot] for spot in spots]
            for n, spot in enumerate(spots):
                k, l = divmod(n, per_q)
                term = product[l * strip:(l + 1) * strip, k * extent:(k + 1) * extent]
                acc_ref[spot] = before[n] + term
    if coded:
        code(acc_ref, out_ref, out_ref.shape[1] * 2 - 2)


def code(acc_ref, out_ref, tiles):
    extra = 24 // tiles
    half = 1 << (15 + extra)
    for d in range(out_ref.shape[0]):
        values = [acc_ref[d * tiles + t] for t in range(tiles)]
        left = functools.reduce(jnp.maximum, [jnp.abs(value) for value in values]) * 2.0**FLOOR
        scale = jnp.full(left.shape, 2.0 ** (FLOOR - 1) * half, jnp.float32)
        last = jnp.zeros(left.shape, jnp.int32)
        for i in reversed(range(7)):
            big = left >= 2.0 ** (1 << i)
            down = jnp.where(big, 2.0 ** -(1 << i), 1.0)
            left, scale = left * down, scale * down
            last = jnp.where(big, last + (1 << i), last)
        low = []
        for t, value in enumerate(values):
            whole = jnp.floor(value * scale + 0.5).astype(jnp.int32)
            whole = jnp.minimum(whole, half - 1) + half
            low.append(whole & 0xFFFF)
            last = last | ((whole >> 16) << (8 + extra * t))
        for j in range(tiles // 2):
            out_ref[d, j] = low[2 * j] | (low[2 * j + 1] << 16)
        out_ref[d, tiles // 2] = last


def add_products(sizes, tile_count, cols, packets, passed, acc, coded=False):
    blocks, per_p, per_q = sizes
    extent = packets[0].shape[1]
    sums = jax.ShapeDtypeStruct((tile_count * tile_count, extent // SEATS, extent), jnp.float32)
    made = sums
    if coded:
        shape = (tile_count * cols, tile_count // cols // 2 + 1) + sums.shape[1:]
        made = jax.ShapeDtypeStruct(shape, jnp.int32)
    operands = [*packets] + ([] if acc is None else [acc])
    return pl.pallas_call(
        functools.partial(product_kernel, sizes, tile_count, passed, acc is None, coded),
        out_shape=made,
        in_specs=[pl.BlockSpec(memory_space=pltpu.VMEM)] * len(operands),
        out_specs=pl.BlockSpec(memory_space=pltpu.VMEM),
        scratch_shapes=[
            pltpu.VMEM((SEATS, extent), jnp.int32),
            pltpu.SMEM((SEATS, extent), jnp.int32),
            pltpu.SemaphoreType.DMA,
        ]
        + [pltpu.VMEM(sums.shape, sums.dtype)] * coded,
        input_output_aliases={} if acc is None or coded else {len(operands) - 1: 0},
        cost_estimate=pl.CostEstimate(
            flops=2 * len(packets) * blocks * per_p * per_q * extent**3 // SEATS,
            bytes_accessed=len(packets) * (1 << 20),
            transcendentals=0,
        ),
        compiler_params=pltpu.CompilerParams(vmem_limit_bytes=24 << 20),
        name="products",
    )(*operands)


def finish_kernel(x_ref, out_ref):
    planes, seats, words, strip, extent = x_ref.shape
    tiles = 2 * (words - 1)
    extra = 24 // tiles
    half = 1 << (15 + extra)
    wholes = [None] * tiles
    for z in range(planes):
        last = x_ref[z, :, words - 1]
        scale = jnp.full(last.shape, 2.0 ** (1 - FLOOR) / half, jnp.float32)
        for i in range(7):
            scale = scale * jnp.where((last >> i) & 1 == 1, 2.0 ** (1 << i), 1.0)
        for t in range(tiles):
            whole = (x_ref[z, :, t // 2] >> (16 * (t % 2))) & 0xFFFF
            whole = whole | (((last >> (8 + extra * t)) & ((1 << extra) - 1)) << 16)
            value = (whole - half).astype(jnp.float32) * scale
            wholes[t] = value if z == 0 else wholes[t] + value
    for t in range(tiles):
        out_ref[:, t * extent:(t + 1) * extent] = wholes[t].reshape(seats * strip, extent).T


def body(p_tiles, p_cols, q_tiles, q_cols):
    blocks, per_p, extent, _ = p_tiles.shape
    per_q = q_tiles.shape[1]
    planes, cols = lax.axis_size("plane"), lax.axis_size("col")
    tile_count = planes * SEATS // cols
    strips = 2 * blocks * per_q * extent // SEATS
    whole = blocks * per_p * extent + 2 * SUB + strips
    seat = ("pair", "core", "col")

    own, *out = pl.pallas_call(
        functools.partial(pack_kernel, cols),
        out_shape=[
            jax.ShapeDtypeStruct((whole + passed * strips, extent), p_tiles.dtype)
            for passed in (0, 1, 1, 1, 0)
        ],
        in_specs=[pl.BlockSpec(memory_space=pltpu.SMEM)] * 2
        + [pl.BlockSpec(memory_space=pltpu.VMEM)] * 2,
        scratch_shapes=[pltpu.VMEM((SEATS, strips // 2, extent), p_tiles.dtype)],
        name="pack",
    )(p_cols.T, q_cols, p_tiles, q_tiles)

    def along(values, step):
        hops = [(s, s ^ axes(s // cols % 2, cols)[step]) for s in range(SEATS)]
        return lax.ppermute(values, seat, hops)

    def across(values):
        return lax.ppermute(values, seat, [(s, s ^ cols) for s in range(SEATS)])

    def add(acc, packets, passed, coded=False):
        sizes = (blocks, per_p, per_q)
        return add_products(sizes, tile_count, cols, packets, passed, acc, coded)

    def opposite(values):
        return lax.ppermute(values, seat, [(s, s ^ (SEATS - 1 - cols)) for s in range(SEATS)])

    first = [along(out[step], step) for step in range(3)]
    beside = across(own)
    far = opposite(out[3])
    second = [along(rest_of(first[step], strips), (step + 1) % 3) for step in range(3)]
    crossed = [across(first[0])]
    acc = add(
        None, [own, beside] + first + crossed, [(0, 0), (0, 1), (1, 0), (1, 0), (1, 0), (1, 1)]
    )
    first[2], second, acc = lax.optimization_barrier((first[2], second, acc))
    acc = add(
        acc,
        [far, across(far), across(first[1])] + second,
        [(0, 0), (0, 1), (1, 1), (0, 0), (0, 0), (0, 0)],
    )
    crossed = [across(each) for each in [first[2]] + second]
    coded = add(acc, crossed, [(1, 1), (0, 1), (0, 1), (0, 1)], coded=True)
    every = ("plane",) + seat
    tiles = tile_count // cols
    landed = lax.all_to_all(coded, every, split_axis=0, concat_axis=0, tiled=True)
    return pl.pallas_call(
        finish_kernel,
        out_shape=jax.ShapeDtypeStruct((extent, tiles * extent), jnp.float32),
        compiler_params=pltpu.CompilerParams(vmem_limit_bytes=16 << 20),
        name="turn",
    )(landed.reshape((planes, SEATS) + landed.shape[1:]))


def solution(mesh):
    rows, cols = mesh.devices.shape
    pairs = SEATS // (2 * cols)
    shape = (rows // (2 * pairs), pairs, 2, cols)
    every = ("plane", "pair", "core", "col")
    inner = Mesh(mesh.devices.reshape(shape), every)
    placed = (
        P(every, None, None, None),
        P(every, None),
        P(every, None, None, None),
        P(every, None),
    )
    return jax.shard_map(
        body, mesh=inner, in_specs=placed, out_specs=P(every[:3], "col"), check_vma=False
    )
```

```python
import functools

import jax
import jax.numpy as jnp
from jax import lax
from jax.experimental import pallas as pl
from jax.experimental.pallas import tpu as pltpu
from jax.sharding import Mesh
from jax.sharding import PartitionSpec as P

SEATS = 16
SUB = 8
FLOOR = 100


def axes(core, cols):
    bits = [bit for bit in (1, 2, 4, 8) if bit != cols]
    return bits[core:] + bits[:core]


def pack_kernel(cols, p_ids, q_ids, p_ref, q_ref, own_ref, *rest):
    out_refs, strips = rest[:4], rest[4]
    blocks, per_q, extent, _ = q_ref.shape
    per_p = p_ids.shape[0]
    strip = extent // SEATS
    rows = per_q * strip
    lane = lax.broadcasted_iota(jnp.int32, (2 * SUB, extent), 1)
    ids = jnp.zeros((2 * SUB, extent), jnp.int32)
    for f in range(blocks):
        for k in range(per_p + per_q):
            value = p_ids[k, f] if k < per_p else q_ids[f, k - per_p]
            ids = jnp.where(lane == f * (per_p + per_q) + k, value, ids)
    ids = ids.astype(p_ref.dtype)
    for f in range(blocks):
        flipped = [q_ref[f, k].astype(jnp.float32).T for k in range(per_q)]
        for j in range(SEATS):
            pieces = [tile[j * strip:(j + 1) * strip] for tile in flipped]
            strips[j, f * rows:(f + 1) * rows] = jnp.concatenate(pieces, axis=0).astype(strips.dtype)
    here = lax.axis_index(("pair", "core", "col"))
    core = lax.axis_index("core")
    paths = [[()], [(0,), (0, 1)], [(1,), (1, 2)], [(2,), (2, 0)], [(0, 1, 2)]]
    for path, out_ref in zip(paths, (own_ref, *out_refs)):
        spots = []
        for steps in path:
            masks = [sum(axes(c, cols)[step] for step in steps) for c in range(2)]
            to = here ^ jnp.where(core == 0, masks[0], masks[1])
            spots += [to, to ^ cols]
        place = 0
        for to in spots[:-2]:
            out_ref[place:place + blocks * rows] = strips[to]
            place += blocks * rows
        for f in range(blocks):
            for k in range(per_p):
                out_ref[place:place + extent] = p_ref[f, k]
                place += extent
        out_ref[place:place + 2 * SUB] = ids
        place += 2 * SUB
        for to in (spots[-1], spots[-2]):
            out_ref[place:place + blocks * rows] = strips[to]
            place += blocks * rows


def rest_kernel(skip, in_ref, out_ref, sem):
    copy = pltpu.make_async_copy(in_ref.at[skip:], out_ref, sem)
    copy.start()
    copy.wait()


def rest_of(packet, skip):
    height, extent = packet.shape
    return pl.pallas_call(
        functools.partial(rest_kernel, skip),
        out_shape=jax.ShapeDtypeStruct((height - skip, extent), packet.dtype),
        in_specs=[pl.BlockSpec(memory_space=pl.ANY)],
        out_specs=pl.BlockSpec(memory_space=pl.ANY),
        scratch_shapes=[pltpu.SemaphoreType.DMA],
        compiler_params=pltpu.CompilerParams(vmem_limit_bytes=1 << 20),
        name="rest_of_packet",
    )(packet)


def product_kernel(sizes, tile_count, passed, first, coded, *refs):
    count = len(passed)
    packets, (out_ref, wide_ids, ids, id_sem, *sums) = refs[:count], refs[count + (not first):]
    acc_ref = sums[0] if coded else out_ref
    blocks, per_p, per_q = sizes
    strip, extent = acc_ref.shape[1:]
    rows = per_q * strip
    places = []
    for i, (before, swapped) in enumerate(passed):
        tiles = 2 * before * blocks * rows
        indices = tiles + blocks * per_p * extent
        mine = swapped * blocks * rows if before else indices + 2 * SUB + (1 - swapped) * blocks * rows
        places.append((tiles, mine))
        wide_ids[i:i + 1] = packets[i][indices:indices + 2 * SUB].astype(jnp.int32)[:1]
    id_copy = pltpu.make_async_copy(wide_ids, ids, id_sem)
    id_copy.start()
    if first:
        acc_ref[...] = jnp.zeros_like(acc_ref)
    else:
        acc_ref[...] = refs[count][...]

    def multiply(i, f):
        tiles, mine = places[i]
        left = packets[i][mine + f * rows:mine + (f + 1) * rows]
        base = tiles + f * per_p * extent
        right = [packets[i][base + k * extent:base + (k + 1) * extent] for k in range(per_p)]
        return jnp.dot(left, jnp.concatenate(right, axis=1), preferred_element_type=jnp.float32)

    early = [multiply(0, f) for f in range(blocks)]
    id_copy.wait()
    for i in range(count):
        for f in range(blocks):
            product = early[f] if i == 0 else multiply(i, f)
            start = f * (per_p + per_q)
            spots = [
                ids[i, start + k] * tile_count + ids[i, start + per_p + l]
                for k in range(per_p)
                for l in range(per_q)
            ]
            before = [acc_ref[spot] for spot in spots]
            for n, spot in enumerate(spots):
                k, l = divmod(n, per_q)
                term = product[l * strip:(l + 1) * strip, k * extent:(k + 1) * extent]
                acc_ref[spot] = before[n] + term
    if coded:
        code(acc_ref, out_ref, out_ref.shape[1] * 2 - 2)


def code(acc_ref, out_ref, tiles):
    extra = 24 // tiles
    half = 1 << (15 + extra)
    for d in range(out_ref.shape[0]):
        values = [acc_ref[d * tiles + t] for t in range(tiles)]
        left = functools.reduce(jnp.maximum, [jnp.abs(value) for value in values]) * 2.0**FLOOR
        scale = jnp.full(left.shape, 2.0 ** (FLOOR - 1) * half, jnp.float32)
        last = jnp.zeros(left.shape, jnp.int32)
        for i in reversed(range(7)):
            big = left >= 2.0 ** (1 << i)
            down = jnp.where(big, 2.0 ** -(1 << i), 1.0)
            left, scale = left * down, scale * down
            last = jnp.where(big, last + (1 << i), last)
        low = []
        for t, value in enumerate(values):
            whole = jnp.floor(value * scale + 0.5).astype(jnp.int32)
            whole = jnp.minimum(whole, half - 1) + half
            low.append(whole & 0xFFFF)
            last = last | ((whole >> 16) << (8 + extra * t))
        for j in range(tiles // 2):
            out_ref[d, j] = low[2 * j] | (low[2 * j + 1] << 16)
        out_ref[d, tiles // 2] = last


def add_products(sizes, tile_count, cols, packets, passed, acc, coded=False):
    blocks, per_p, per_q = sizes
    extent = packets[0].shape[1]
    sums = jax.ShapeDtypeStruct((tile_count * tile_count, extent // SEATS, extent), jnp.float32)
    made = sums
    if coded:
        shape = (tile_count * cols, tile_count // cols // 2 + 1) + sums.shape[1:]
        made = jax.ShapeDtypeStruct(shape, jnp.int32)
    operands = [*packets] + ([] if acc is None else [acc])
    return pl.pallas_call(
        functools.partial(product_kernel, sizes, tile_count, passed, acc is None, coded),
        out_shape=made,
        in_specs=[pl.BlockSpec(memory_space=pltpu.VMEM)] * len(operands),
        out_specs=pl.BlockSpec(memory_space=pltpu.VMEM),
        scratch_shapes=[
            pltpu.VMEM((SEATS, extent), jnp.int32),
            pltpu.SMEM((SEATS, extent), jnp.int32),
            pltpu.SemaphoreType.DMA,
        ]
        + [pltpu.VMEM(sums.shape, sums.dtype)] * coded,
        input_output_aliases={} if acc is None or coded else {len(operands) - 1: 0},
        cost_estimate=pl.CostEstimate(
            flops=2 * len(packets) * blocks * per_p * per_q * extent**3 // SEATS,
            bytes_accessed=len(packets) * (1 << 20),
            transcendentals=0,
        ),
        compiler_params=pltpu.CompilerParams(vmem_limit_bytes=24 << 20),
        name="products",
    )(*operands)


def finish_kernel(x_ref, out_ref):
    planes, seats, words, strip, extent = x_ref.shape
    tiles = 2 * (words - 1)
    extra = 24 // tiles
    half = 1 << (15 + extra)
    wholes = [None] * tiles
    for z in range(planes):
        last = x_ref[z, :, words - 1]
        scale = jnp.full(last.shape, 2.0 ** (1 - FLOOR) / half, jnp.float32)
        for i in range(7):
            scale = scale * jnp.where((last >> i) & 1 == 1, 2.0 ** (1 << i), 1.0)
        for t in range(tiles):
            whole = (x_ref[z, :, t // 2] >> (16 * (t % 2))) & 0xFFFF
            whole = whole | (((last >> (8 + extra * t)) & ((1 << extra) - 1)) << 16)
            value = (whole - half).astype(jnp.float32) * scale
            wholes[t] = value if z == 0 else wholes[t] + value
    for t in range(tiles):
        out_ref[:, t * extent:(t + 1) * extent] = wholes[t].reshape(seats * strip, extent).T


def body(p_tiles, p_cols, q_tiles, q_cols):
    blocks, per_p, extent, _ = p_tiles.shape
    per_q = q_tiles.shape[1]
    planes, cols = lax.axis_size("plane"), lax.axis_size("col")
    tile_count = planes * SEATS // cols
    strips = 2 * blocks * per_q * extent // SEATS
    whole = blocks * per_p * extent + 2 * SUB + strips
    seat = ("pair", "core", "col")

    own, *out = pl.pallas_call(
        functools.partial(pack_kernel, cols),
        out_shape=[
            jax.ShapeDtypeStruct((whole + passed * strips, extent), p_tiles.dtype)
            for passed in (0, 1, 1, 1, 0)
        ],
        in_specs=[pl.BlockSpec(memory_space=pltpu.SMEM)] * 2
        + [pl.BlockSpec(memory_space=pltpu.VMEM)] * 2,
        scratch_shapes=[pltpu.VMEM((SEATS, strips // 2, extent), p_tiles.dtype)],
        name="pack",
    )(p_cols.T, q_cols, p_tiles, q_tiles)

    def along(values, step):
        hops = [(s, s ^ axes(s // cols % 2, cols)[step]) for s in range(SEATS)]
        return lax.ppermute(values, seat, hops)

    def across(values):
        return lax.ppermute(values, seat, [(s, s ^ cols) for s in range(SEATS)])

    def add(acc, packets, passed, coded=False):
        sizes = (blocks, per_p, per_q)
        return add_products(sizes, tile_count, cols, packets, passed, acc, coded)

    def opposite(values):
        return lax.ppermute(values, seat, [(s, s ^ (SEATS - 1 - cols)) for s in range(SEATS)])

    first = [along(out[step], step) for step in range(3)]
    beside = across(own)
    far = opposite(out[3])
    second = [along(rest_of(first[step], strips), (step + 1) % 3) for step in range(3)]
    acc = add(None, [own, beside] + first, [(0, 0), (0, 1), (1, 0), (1, 0), (1, 0)])
    first[2], far, second, acc = lax.optimization_barrier((first[2], far, second, acc))
    crossed = [across(each) for each in first]
    acc = add(acc, crossed[:2] + [far] + second, [(1, 1), (1, 1), (0, 0), (0, 0), (0, 0), (0, 0)])
    crossed = crossed[2:] + [across(each) for each in [far] + second]
    coded = add(acc, crossed, [(1, 1), (0, 1), (0, 1), (0, 1), (0, 1)], coded=True)
    every = ("plane",) + seat
    tiles = tile_count // cols
    landed = lax.all_to_all(coded, every, split_axis=0, concat_axis=0, tiled=True)
    return pl.pallas_call(
        finish_kernel,
        out_shape=jax.ShapeDtypeStruct((extent, tiles * extent), jnp.float32),
        compiler_params=pltpu.CompilerParams(vmem_limit_bytes=16 << 20),
        name="turn",
    )(landed.reshape((planes, SEATS) + landed.shape[1:]))


def solution(mesh):
    rows, cols = mesh.devices.shape
    pairs = SEATS // (2 * cols)
    shape = (rows // (2 * pairs), pairs, 2, cols)
    every = ("plane", "pair", "core", "col")
    inner = Mesh(mesh.devices.reshape(shape), every)
    placed = (
        P(every, None, None, None),
        P(every, None),
        P(every, None, None, None),
        P(every, None),
    )
    return jax.shard_map(
        body, mesh=inner, in_specs=placed, out_specs=P(every[:3], "col"), check_vma=False
    )
```

```python
import functools

import jax
import jax.numpy as jnp
from jax import lax
from jax.experimental import pallas as pl
from jax.experimental.pallas import tpu as pltpu
from jax.sharding import Mesh
from jax.sharding import PartitionSpec as P

SEATS = 16
SUB = 8
FLOOR = 100


def axes(core, cols):
    bits = [bit for bit in (1, 2, 4, 8) if bit != cols]
    return bits[core:] + bits[:core]


def pack_kernel(cols, p_ids, q_ids, p_ref, q_ref, own_ref, *rest):
    out_refs, strips = rest[:4], rest[4]
    blocks, per_q, extent, _ = q_ref.shape
    per_p = p_ids.shape[0]
    strip = extent // SEATS
    rows = per_q * strip
    lane = lax.broadcasted_iota(jnp.int32, (2 * SUB, extent), 1)
    ids = jnp.zeros((2 * SUB, extent), jnp.int32)
    for f in range(blocks):
        for k in range(per_p + per_q):
            value = p_ids[k, f] if k < per_p else q_ids[f, k - per_p]
            ids = jnp.where(lane == f * (per_p + per_q) + k, value, ids)
    ids = ids.astype(p_ref.dtype)
    line = lax.broadcasted_iota(jnp.int32, (extent, extent), 0)
    unit = (line == lax.broadcasted_iota(jnp.int32, (extent, extent), 1)).astype(q_ref.dtype)
    for f in range(blocks):
        flipped = [
            lax.dot_general(unit, q_ref[f, k], (((1,), (1,)), ((), ())), preferred_element_type=jnp.float32)
            for k in range(per_q)
        ]
        for j in range(SEATS):
            pieces = [tile[j * strip:(j + 1) * strip] for tile in flipped]
            strips[j, f * rows:(f + 1) * rows] = jnp.concatenate(pieces, axis=0).astype(strips.dtype)
    here = lax.axis_index(("pair", "core", "col"))
    core = lax.axis_index("core")
    paths = [[()], [(0,), (0, 1)], [(1,), (1, 2)], [(2,), (2, 0)], [(0, 1, 2)]]
    for path, out_ref in zip(paths, (own_ref, *out_refs)):
        spots = []
        for steps in path:
            masks = [sum(axes(c, cols)[step] for step in steps) for c in range(2)]
            to = here ^ jnp.where(core == 0, masks[0], masks[1])
            spots += [to, to ^ cols]
        place = 0
        for to in spots[:-2]:
            out_ref[place:place + blocks * rows] = strips[to]
            place += blocks * rows
        for f in range(blocks):
            for k in range(per_p):
                out_ref[place:place + extent] = p_ref[f, k]
                place += extent
        out_ref[place:place + 2 * SUB] = ids
        place += 2 * SUB
        for to in (spots[-1], spots[-2]):
            out_ref[place:place + blocks * rows] = strips[to]
            place += blocks * rows


def rest_kernel(skip, in_ref, out_ref, sem):
    copy = pltpu.make_async_copy(in_ref.at[skip:], out_ref, sem)
    copy.start()
    copy.wait()


def rest_of(packet, skip):
    height, extent = packet.shape
    return pl.pallas_call(
        functools.partial(rest_kernel, skip),
        out_shape=jax.ShapeDtypeStruct((height - skip, extent), packet.dtype),
        in_specs=[pl.BlockSpec(memory_space=pl.ANY)],
        out_specs=pl.BlockSpec(memory_space=pl.ANY),
        scratch_shapes=[pltpu.SemaphoreType.DMA],
        compiler_params=pltpu.CompilerParams(vmem_limit_bytes=1 << 20),
        name="rest_of_packet",
    )(packet)


def product_kernel(sizes, tile_count, passed, first, coded, *refs):
    count = len(passed)
    packets, (out_ref, wide_ids, ids, id_sem, *sums) = refs[:count], refs[count + (not first):]
    acc_ref = sums[0] if coded else out_ref
    blocks, per_p, per_q = sizes
    strip, extent = acc_ref.shape[1:]
    rows = per_q * strip
    places = []
    for i, (before, swapped) in enumerate(passed):
        tiles = 2 * before * blocks * rows
        indices = tiles + blocks * per_p * extent
        mine = swapped * blocks * rows if before else indices + 2 * SUB + (1 - swapped) * blocks * rows
        places.append((tiles, mine))
        wide_ids[i:i + 1] = packets[i][indices:indices + 2 * SUB].astype(jnp.int32)[:1]
    id_copy = pltpu.make_async_copy(wide_ids, ids, id_sem)
    id_copy.start()
    if first:
        acc_ref[...] = jnp.zeros_like(acc_ref)
    else:
        acc_ref[...] = refs[count][...]
    id_copy.wait()
    for i, (tiles, mine) in enumerate(places):
        for f in range(blocks):
            left = packets[i][mine + f * rows:mine + (f + 1) * rows]
            base = tiles + f * per_p * extent
            right = [packets[i][base + k * extent:base + (k + 1) * extent] for k in range(per_p)]
            product = jnp.dot(
                left, jnp.concatenate(right, axis=1), preferred_element_type=jnp.float32
            )
            start = f * (per_p + per_q)
            spots = [
                ids[i, start + k] * tile_count + ids[i, start + per_p + l]
                for k in range(per_p)
                for l in range(per_q)
            ]
            before = [acc_ref[spot] for spot in spots]
            for n, spot in enumerate(spots):
                k, l = divmod(n, per_q)
                term = product[l * strip:(l + 1) * strip, k * extent:(k + 1) * extent]
                acc_ref[spot] = before[n] + term
    if coded:
        code(acc_ref, out_ref, out_ref.shape[1] * 2 - 2)


def code(acc_ref, out_ref, tiles):
    extra = 24 // tiles
    half = 1 << (15 + extra)
    for d in range(out_ref.shape[0]):
        values = [acc_ref[d * tiles + t] for t in range(tiles)]
        left = functools.reduce(jnp.maximum, [jnp.abs(value) for value in values]) * 2.0**FLOOR
        scale = jnp.full(left.shape, 2.0 ** (FLOOR - 1) * half, jnp.float32)
        last = jnp.zeros(left.shape, jnp.int32)
        for i in reversed(range(7)):
            big = left >= 2.0 ** (1 << i)
            down = jnp.where(big, 2.0 ** -(1 << i), 1.0)
            left, scale = left * down, scale * down
            last = jnp.where(big, last + (1 << i), last)
        low = []
        for t, value in enumerate(values):
            whole = jnp.floor(value * scale + 0.5).astype(jnp.int32)
            whole = jnp.minimum(whole, half - 1) + half
            low.append(whole & 0xFFFF)
            last = last | ((whole >> 16) << (8 + extra * t))
        for j in range(tiles // 2):
            out_ref[d, j] = low[2 * j] | (low[2 * j + 1] << 16)
        out_ref[d, tiles // 2] = last


def add_products(sizes, tile_count, cols, packets, passed, acc, coded=False):
    blocks, per_p, per_q = sizes
    extent = packets[0].shape[1]
    sums = jax.ShapeDtypeStruct((tile_count * tile_count, extent // SEATS, extent), jnp.float32)
    made = sums
    if coded:
        shape = (tile_count * cols, tile_count // cols // 2 + 1) + sums.shape[1:]
        made = jax.ShapeDtypeStruct(shape, jnp.int32)
    operands = [*packets] + ([] if acc is None else [acc])
    return pl.pallas_call(
        functools.partial(product_kernel, sizes, tile_count, passed, acc is None, coded),
        out_shape=made,
        in_specs=[pl.BlockSpec(memory_space=pltpu.VMEM)] * len(operands),
        out_specs=pl.BlockSpec(memory_space=pltpu.VMEM),
        scratch_shapes=[
            pltpu.VMEM((SEATS, extent), jnp.int32),
            pltpu.SMEM((SEATS, extent), jnp.int32),
            pltpu.SemaphoreType.DMA,
        ]
        + [pltpu.VMEM(sums.shape, sums.dtype)] * coded,
        input_output_aliases={} if acc is None or coded else {len(operands) - 1: 0},
        cost_estimate=pl.CostEstimate(
            flops=2 * len(packets) * blocks * per_p * per_q * extent**3 // SEATS,
            bytes_accessed=len(packets) * (1 << 20),
            transcendentals=0,
        ),
        compiler_params=pltpu.CompilerParams(vmem_limit_bytes=24 << 20),
        name="products",
    )(*operands)


def finish_kernel(x_ref, out_ref):
    planes, seats, words, strip, extent = x_ref.shape
    tiles = 2 * (words - 1)
    extra = 24 // tiles
    half = 1 << (15 + extra)
    wholes = [None] * tiles
    for z in range(planes):
        last = x_ref[z, :, words - 1]
        scale = jnp.full(last.shape, 2.0 ** (1 - FLOOR) / half, jnp.float32)
        for i in range(7):
            scale = scale * jnp.where((last >> i) & 1 == 1, 2.0 ** (1 << i), 1.0)
        for t in range(tiles):
            whole = (x_ref[z, :, t // 2] >> (16 * (t % 2))) & 0xFFFF
            whole = whole | (((last >> (8 + extra * t)) & ((1 << extra) - 1)) << 16)
            value = (whole - half).astype(jnp.float32) * scale
            wholes[t] = value if z == 0 else wholes[t] + value
    for t in range(tiles):
        out_ref[:, t * extent:(t + 1) * extent] = wholes[t].reshape(seats * strip, extent).T


def body(p_tiles, p_cols, q_tiles, q_cols):
    blocks, per_p, extent, _ = p_tiles.shape
    per_q = q_tiles.shape[1]
    planes, cols = lax.axis_size("plane"), lax.axis_size("col")
    tile_count = planes * SEATS // cols
    strips = 2 * blocks * per_q * extent // SEATS
    whole = blocks * per_p * extent + 2 * SUB + strips
    seat = ("pair", "core", "col")

    own, *out = pl.pallas_call(
        functools.partial(pack_kernel, cols),
        out_shape=[
            jax.ShapeDtypeStruct((whole + passed * strips, extent), p_tiles.dtype)
            for passed in (0, 1, 1, 1, 0)
        ],
        in_specs=[pl.BlockSpec(memory_space=pltpu.SMEM)] * 2
        + [pl.BlockSpec(memory_space=pltpu.VMEM)] * 2,
        scratch_shapes=[pltpu.VMEM((SEATS, strips // 2, extent), p_tiles.dtype)],
        name="pack",
    )(p_cols.T, q_cols, p_tiles, q_tiles)

    def along(values, step):
        hops = [(s, s ^ axes(s // cols % 2, cols)[step]) for s in range(SEATS)]
        return lax.ppermute(values, seat, hops)

    def across(values):
        return lax.ppermute(values, seat, [(s, s ^ cols) for s in range(SEATS)])

    def add(acc, packets, passed, coded=False):
        sizes = (blocks, per_p, per_q)
        return add_products(sizes, tile_count, cols, packets, passed, acc, coded)

    def opposite(values):
        return lax.ppermute(values, seat, [(s, s ^ (SEATS - 1 - cols)) for s in range(SEATS)])

    first = [along(out[step], step) for step in range(3)]
    beside = across(own)
    far = opposite(out[3])
    second = [along(rest_of(first[step], strips), (step + 1) % 3) for step in range(3)]
    acc = add(None, [own, beside] + first, [(0, 0), (0, 1), (1, 0), (1, 0), (1, 0)])
    first[2], far, second, acc = lax.optimization_barrier((first[2], far, second, acc))
    crossed = [across(each) for each in first]
    acc = add(acc, crossed[:2] + [far] + second, [(1, 1), (1, 1), (0, 0), (0, 0), (0, 0), (0, 0)])
    crossed = crossed[2:] + [across(each) for each in [far] + second]
    coded = add(acc, crossed, [(1, 1), (0, 1), (0, 1), (0, 1), (0, 1)], coded=True)
    every = ("plane",) + seat
    tiles = tile_count // cols
    landed = lax.all_to_all(coded, every, split_axis=0, concat_axis=0, tiled=True)
    return pl.pallas_call(
        finish_kernel,
        out_shape=jax.ShapeDtypeStruct((extent, tiles * extent), jnp.float32),
        compiler_params=pltpu.CompilerParams(vmem_limit_bytes=16 << 20),
        name="turn",
    )(landed.reshape((planes, SEATS) + landed.shape[1:]))


def solution(mesh):
    rows, cols = mesh.devices.shape
    pairs = SEATS // (2 * cols)
    shape = (rows // (2 * pairs), pairs, 2, cols)
    every = ("plane", "pair", "core", "col")
    inner = Mesh(mesh.devices.reshape(shape), every)
    placed = (
        P(every, None, None, None),
        P(every, None),
        P(every, None, None, None),
        P(every, None),
    )
    return jax.shard_map(
        body, mesh=inner, in_specs=placed, out_specs=P(every[:3], "col"), check_vma=False
    )
```

```python
import functools

import jax
import jax.numpy as jnp
from jax import lax
from jax.experimental import pallas as pl
from jax.experimental.pallas import tpu as pltpu
from jax.sharding import Mesh
from jax.sharding import PartitionSpec as P

SEATS = 16
SUB = 8
FLOOR = 100


def axes(core, cols):
    bits = [bit for bit in (1, 2, 4, 8) if bit != cols]
    return bits[core:] + bits[:core]


def pack_kernel(cols, p_ids, q_ids, p_ref, q_ref, *rest):
    out_refs, (strips, ids, sems) = rest[:-3], rest[-3:]
    blocks, per_q, extent, _ = q_ref.shape
    per_p = p_ids.shape[0]
    strip = extent // SEATS
    rows = per_q * strip
    height, tiles = blocks * rows, p_ref.shape[0]
    here = lax.axis_index(("pair", "core", "col"))
    core = lax.axis_index("core")
    paths = [[()], [(0,), (0, 1)], [(1,), (1, 2)], [(2,), (2, 0)], [(0, 1, 2)]]
    copies, later = [], []
    for path, out_ref in zip(paths, out_refs):
        spots = []
        for steps in path:
            masks = [sum(axes(c, cols)[step] for step in steps) for c in range(2)]
            to = here ^ jnp.where(core == 0, masks[0], masks[1])
            spots += [to, to ^ cols]
        place = 0
        for to in spots[:-2]:
            later.append((strips.at[to], out_ref.at[place:place + height]))
            place += height
        copies.append((p_ref, out_ref.at[place:place + tiles]))
        place += tiles
        later.append((ids, out_ref.at[place:place + 2 * SUB]))
        place += 2 * SUB
        for to in (spots[-1], spots[-2]):
            later.append((strips.at[to], out_ref.at[place:place + height]))
            place += height
    copies = [
        pltpu.make_async_copy(source, target, sems.at[n])
        for n, (source, target) in enumerate(copies + later)
    ]
    for copy in copies[:len(paths)]:
        copy.start()
    lane = lax.broadcasted_iota(jnp.int32, ids.shape, 1)
    words = jnp.zeros(ids.shape, jnp.int32)
    for f in range(blocks):
        for k in range(per_p + per_q):
            value = p_ids[k, f] if k < per_p else q_ids[f, k - per_p]
            words = jnp.where(lane == f * (per_p + per_q) + k, value, words)
    ids[...] = words.astype(ids.dtype)
    for f in range(blocks):
        flipped = [q_ref[f, k].astype(jnp.float32).T for k in range(per_q)]
        for j in range(SEATS):
            pieces = [tile[j * strip:(j + 1) * strip] for tile in flipped]
            strips[j, f * rows:(f + 1) * rows] = jnp.concatenate(pieces, axis=0).astype(strips.dtype)
    for copy in copies[len(paths):]:
        copy.start()
    for copy in copies:
        copy.wait()


def rest_kernel(skip, in_ref, out_ref, sem):
    copy = pltpu.make_async_copy(in_ref.at[skip:], out_ref, sem)
    copy.start()
    copy.wait()


def rest_of(packet, skip):
    height, extent = packet.shape
    return pl.pallas_call(
        functools.partial(rest_kernel, skip),
        out_shape=jax.ShapeDtypeStruct((height - skip, extent), packet.dtype),
        in_specs=[pl.BlockSpec(memory_space=pl.ANY)],
        out_specs=pl.BlockSpec(memory_space=pl.ANY),
        scratch_shapes=[pltpu.SemaphoreType.DMA],
        compiler_params=pltpu.CompilerParams(vmem_limit_bytes=1 << 20),
        name="rest_of_packet",
    )(packet)


def product_kernel(sizes, tile_count, passed, first, coded, *refs):
    count = len(passed)
    packets, (out_ref, wide_ids, ids, id_sem, *sums) = refs[:count], refs[count + (not first):]
    acc_ref = sums[0] if coded else out_ref
    blocks, per_p, per_q = sizes
    strip, extent = acc_ref.shape[1:]
    rows = per_q * strip
    places = []
    for i, (before, swapped) in enumerate(passed):
        tiles = 2 * before * blocks * rows
        indices = tiles + blocks * per_p * extent
        mine = swapped * blocks * rows if before else indices + 2 * SUB + (1 - swapped) * blocks * rows
        places.append((tiles, mine))
        wide_ids[i:i + 1] = packets[i][indices:indices + 2 * SUB].astype(jnp.int32)[:1]
    id_copy = pltpu.make_async_copy(wide_ids, ids, id_sem)
    id_copy.start()
    if first:
        acc_ref[...] = jnp.zeros_like(acc_ref)
    else:
        acc_ref[...] = refs[count][...]

    def multiply(i, f):
        tiles, mine = places[i]
        left = packets[i][mine + f * rows:mine + (f + 1) * rows]
        base = tiles + f * per_p * extent
        right = [packets[i][base + k * extent:base + (k + 1) * extent] for k in range(per_p)]
        return jnp.dot(left, jnp.concatenate(right, axis=1), preferred_element_type=jnp.float32)

    early = [multiply(0, f) for f in range(blocks)]
    id_copy.wait()
    for i in range(count):
        for f in range(blocks):
            product = early[f] if i == 0 else multiply(i, f)
            start = f * (per_p + per_q)
            spots = [
                ids[i, start + k] * tile_count + ids[i, start + per_p + l]
                for k in range(per_p)
                for l in range(per_q)
            ]
            before = [acc_ref[spot] for spot in spots]
            for n, spot in enumerate(spots):
                k, l = divmod(n, per_q)
                term = product[l * strip:(l + 1) * strip, k * extent:(k + 1) * extent]
                acc_ref[spot] = before[n] + term
    if coded:
        code(acc_ref, out_ref, out_ref.shape[1] * 2 - 2)


def code(acc_ref, out_ref, tiles):
    extra = 24 // tiles
    half = 1 << (15 + extra)
    for d in range(out_ref.shape[0]):
        values = [acc_ref[d * tiles + t] for t in range(tiles)]
        left = functools.reduce(jnp.maximum, [jnp.abs(value) for value in values]) * 2.0**FLOOR
        scale = jnp.full(left.shape, 2.0 ** (FLOOR - 1) * half, jnp.float32)
        last = jnp.zeros(left.shape, jnp.int32)
        for i in reversed(range(7)):
            big = left >= 2.0 ** (1 << i)
            down = jnp.where(big, 2.0 ** -(1 << i), 1.0)
            left, scale = left * down, scale * down
            last = jnp.where(big, last + (1 << i), last)
        low = []
        for t, value in enumerate(values):
            whole = jnp.floor(value * scale + 0.5).astype(jnp.int32)
            whole = jnp.minimum(whole, half - 1) + half
            low.append(whole & 0xFFFF)
            last = last | ((whole >> 16) << (8 + extra * t))
        for j in range(tiles // 2):
            out_ref[d, j] = low[2 * j] | (low[2 * j + 1] << 16)
        out_ref[d, tiles // 2] = last


def add_products(sizes, tile_count, cols, packets, passed, acc, coded=False):
    blocks, per_p, per_q = sizes
    extent = packets[0].shape[1]
    sums = jax.ShapeDtypeStruct((tile_count * tile_count, extent // SEATS, extent), jnp.float32)
    made = sums
    if coded:
        shape = (tile_count * cols, tile_count // cols // 2 + 1) + sums.shape[1:]
        made = jax.ShapeDtypeStruct(shape, jnp.int32)
    operands = [*packets] + ([] if acc is None else [acc])
    return pl.pallas_call(
        functools.partial(product_kernel, sizes, tile_count, passed, acc is None, coded),
        out_shape=made,
        in_specs=[pl.BlockSpec(memory_space=pltpu.VMEM)] * len(operands),
        out_specs=pl.BlockSpec(memory_space=pltpu.VMEM),
        scratch_shapes=[
            pltpu.VMEM((SEATS, extent), jnp.int32),
            pltpu.SMEM((SEATS, extent), jnp.int32),
            pltpu.SemaphoreType.DMA,
        ]
        + [pltpu.VMEM(sums.shape, sums.dtype)] * coded,
        input_output_aliases={} if acc is None or coded else {len(operands) - 1: 0},
        cost_estimate=pl.CostEstimate(
            flops=2 * len(packets) * blocks * per_p * per_q * extent**3 // SEATS,
            bytes_accessed=len(packets) * (1 << 20),
            transcendentals=0,
        ),
        compiler_params=pltpu.CompilerParams(vmem_limit_bytes=24 << 20),
        name="products",
    )(*operands)


def finish_kernel(x_ref, out_ref):
    planes, seats, words, strip, extent = x_ref.shape
    tiles = 2 * (words - 1)
    extra = 24 // tiles
    half = 1 << (15 + extra)
    wholes = [None] * tiles
    for z in range(planes):
        last = x_ref[z, :, words - 1]
        scale = jnp.full(last.shape, 2.0 ** (1 - FLOOR) / half, jnp.float32)
        for i in range(7):
            scale = scale * jnp.where((last >> i) & 1 == 1, 2.0 ** (1 << i), 1.0)
        for t in range(tiles):
            whole = (x_ref[z, :, t // 2] >> (16 * (t % 2))) & 0xFFFF
            whole = whole | (((last >> (8 + extra * t)) & ((1 << extra) - 1)) << 16)
            value = (whole - half).astype(jnp.float32) * scale
            wholes[t] = value if z == 0 else wholes[t] + value
    for t in range(tiles):
        out_ref[:, t * extent:(t + 1) * extent] = wholes[t].reshape(seats * strip, extent).T


def body(p_tiles, p_cols, q_tiles, q_cols):
    blocks, per_p, extent, _ = p_tiles.shape
    per_q = q_tiles.shape[1]
    planes, cols = lax.axis_size("plane"), lax.axis_size("col")
    tile_count = planes * SEATS // cols
    strips = 2 * blocks * per_q * extent // SEATS
    whole = blocks * per_p * extent + 2 * SUB + strips
    seat = ("pair", "core", "col")

    own, *out = pl.pallas_call(
        functools.partial(pack_kernel, cols),
        out_shape=[
            jax.ShapeDtypeStruct((whole + passed * strips, extent), p_tiles.dtype)
            for passed in (0, 1, 1, 1, 0)
        ],
        in_specs=[pl.BlockSpec(memory_space=pltpu.SMEM)] * 2
        + [pl.BlockSpec(memory_space=pltpu.VMEM)] * 2,
        out_specs=[pl.BlockSpec(memory_space=pl.ANY)] * 5,
        scratch_shapes=[
            pltpu.VMEM((SEATS, strips // 2, extent), p_tiles.dtype),
            pltpu.VMEM((2 * SUB, extent), p_tiles.dtype),
            pltpu.SemaphoreType.DMA((26,)),
        ],
        name="pack",
    )(p_cols.T, q_cols, p_tiles.reshape(-1, extent), q_tiles)

    def along(values, step):
        hops = [(s, s ^ axes(s // cols % 2, cols)[step]) for s in range(SEATS)]
        return lax.ppermute(values, seat, hops)

    def across(values):
        return lax.ppermute(values, seat, [(s, s ^ cols) for s in range(SEATS)])

    def add(acc, packets, passed, coded=False):
        sizes = (blocks, per_p, per_q)
        return add_products(sizes, tile_count, cols, packets, passed, acc, coded)

    def opposite(values):
        return lax.ppermute(values, seat, [(s, s ^ (SEATS - 1 - cols)) for s in range(SEATS)])

    first = [along(out[step], step) for step in range(3)]
    beside = across(own)
    far = opposite(out[3])
    second = [along(rest_of(first[step], strips), (step + 1) % 3) for step in range(3)]
    acc = add(None, [own, beside] + first, [(0, 0), (0, 1), (1, 0), (1, 0), (1, 0)])
    first[2], far, second, acc = lax.optimization_barrier((first[2], far, second, acc))
    crossed = [across(each) for each in first]
    acc = add(acc, crossed[:2] + [far] + second, [(1, 1), (1, 1), (0, 0), (0, 0), (0, 0), (0, 0)])
    crossed = crossed[2:] + [across(each) for each in [far] + second]
    coded = add(acc, crossed, [(1, 1), (0, 1), (0, 1), (0, 1), (0, 1)], coded=True)
    every = ("plane",) + seat
    tiles = tile_count // cols
    landed = lax.all_to_all(coded, every, split_axis=0, concat_axis=0, tiled=True)
    return pl.pallas_call(
        finish_kernel,
        out_shape=jax.ShapeDtypeStruct((extent, tiles * extent), jnp.float32),
        compiler_params=pltpu.CompilerParams(vmem_limit_bytes=16 << 20),
        name="turn",
    )(landed.reshape((planes, SEATS) + landed.shape[1:]))


def solution(mesh):
    rows, cols = mesh.devices.shape
    pairs = SEATS // (2 * cols)
    shape = (rows // (2 * pairs), pairs, 2, cols)
    every = ("plane", "pair", "core", "col")
    inner = Mesh(mesh.devices.reshape(shape), every)
    placed = (
        P(every, None, None, None),
        P(every, None),
        P(every, None, None, None),
        P(every, None),
    )
    return jax.shard_map(
        body, mesh=inner, in_specs=placed, out_specs=P(every[:3], "col"), check_vma=False
    )
```
